32 devices in a mesh: replica: 4 (over y, x), fsdp: 8 (over z, core).
Axes of the slice: x: 2, y: 2, z: 4, core: 2. Of those that a mesh axis runs over, the one named last changes fastest.
Arguments:
- tokens: bfloat16 [2, 32, 512, 1536], P(None, ('replica', 'fsdp')), may hold values from -6 to 6
- cotangent: bfloat16 [2, 32, 512, 1536], P(None, ('replica', 'fsdp')), may hold values from -6 to 6
- lengths: int32 [2, 32], P(None, ('replica', 'fsdp')), may hold values from 128 to 512, as said below
- routes: int32 [2, 32, 512, 2], P(None, ('replica', 'fsdp')), may hold values from 0 to 2, as said below
- slot_index: int32 [2, 32, 512, 2], P(None, ('replica', 'fsdp')), may hold values from 0 to 511, as said below
- norm_gains: float32 [2, 1536], P(None, 'fsdp'), may hold values from 0.5 to 1.5
- norm_first: float32 [2, 1536], P(None, 'fsdp'), may hold values from -0.0034179688 to 0.0034179688
- norm_second: float32 [2, 1536], P(None, 'fsdp'), may hold values from 1.3e-06 to 5.3e-06
- in_proj: float32 [1536, 2560], P('fsdp'), may hold values from -0.15625 to 0.15625
- in_first: float32 [1536, 2560], P('fsdp'), may hold values from -0.0034179688 to 0.0034179688
- in_second: float32 [1536, 2560], P('fsdp'), may hold values from 1.3e-06 to 5.3e-06
- out_proj: float32 [1536, 1536], P('fsdp'), may hold values from -1.25 to 1.25
- out_first: float32 [1536, 1536], P('fsdp'), may hold values from -0.0034179688 to 0.0034179688
- out_second: float32 [1536, 1536], P('fsdp'), may hold values from 1.3e-06 to 5.3e-06
- router: float32 [1536, 3], P('fsdp'), may hold values from -0.109375 to 0.109375
- router_first: float32 [1536, 3], P('fsdp'), may hold values from -0.0034179688 to 0.0034179688
- router_second: float32 [1536, 3], P('fsdp'), may hold values from 1.3e-06 to 5.3e-06
- up_proj: float32 [3, 1536, 2048], P(None, 'fsdp'), may hold values from -0.15625 to 0.15625
- up_first: float32 [3, 1536, 2048], P(None, 'fsdp'), may hold values from -0.0034179688 to 0.0034179688
- up_second: float32 [3, 1536, 2048], P(None, 'fsdp'), may hold values from 1.3e-06 to 5.3e-06
- down_proj: float32 [3, 1024, 1536], P(None, 'fsdp'), may hold values from -0.5 to 0.5
- down_first: float32 [3, 1024, 1536], P(None, 'fsdp'), may hold values from -0.0034179688 to 0.0034179688
- down_second: float32 [3, 1024, 1536], P(None, 'fsdp'), may hold values from 1.3e-06 to 5.3e-06
Outputs:
- block_out: bfloat16 [2, 32, 512, 1536], P(None, ('replica', 'fsdp'))
- input_grad: bfloat16 [2, 32, 512, 1536], P(None, ('replica', 'fsdp'))
- grad_rms: float32 [5], replicated
- down_rms: float32 [1], replicated
- norm_grad: float32 [2, 1536], P(None, 'fsdp')
- norm_update: float32 [2, 1536], P(None, 'fsdp')
- norm_first_new: float32 [2, 1536], P(None, 'fsdp')
- norm_second_new: float32 [2, 1536], P(None, 'fsdp')
- in_grad: float32 [1536, 2560], P('fsdp')
- in_update: float32 [1536, 2560], P('fsdp')
- in_first_new: float32 [1536, 2560], P('fsdp')
- in_second_new: float32 [1536, 2560], P('fsdp')
- out_grad: float32 [1536, 1536], P('fsdp')
- out_update: float32 [1536, 1536], P('fsdp')
- out_first_new: float32 [1536, 1536], P('fsdp')
- out_second_new: float32 [1536, 1536], P('fsdp')
- router_grad: float32 [1536, 3], P('fsdp')
- router_update: float32 [1536, 3], P('fsdp')
- router_first_new: float32 [1536, 3], P('fsdp')
- router_second_new: float32 [1536, 3], P('fsdp')
- up_grad: float32 [3, 1536, 2048], P(None, 'fsdp')
- up_update: float32 [3, 1536, 2048], P(None, 'fsdp')
- up_first_new: float32 [3, 1536, 2048], P(None, 'fsdp')
- up_second_new: float32 [3, 1536, 2048], P(None, 'fsdp')
- down_grad: float32 [3, 1024, 1536], P(None, 'fsdp')
- down_update: float32 [3, 1024, 1536], P(None, 'fsdp')
- down_first_new: float32 [3, 1024, 1536], P(None, 'fsdp')
- down_second_new: float32 [3, 1024, 1536], P(None, 'fsdp')
The draws below stay inside these ranges and needn't reach their ends.
Inputs may be any that keep to these rules, and one draw needn't show every extreme that they name: `lengths`: in every draw some sequence has exactly 512 valid tokens and some has exactly 128. `routes`: the two experts of a token differ. `slot_index`: for each sequence and expert, the tokens routed to it take distinct slots; its valid routed tokens take the lowest slots and its other routed tokens the slots after them; in every draw some expert takes all 512 tokens of some sequence.
All inputs are finite; a program needn't handle non-finite values.
Results may differ from the reference program's by a relative error of at most 0.015.
The reference program's roundings to bfloat16 on the way count: a program that leaves them out, or rounds other values in their place, can miss the bound.
Values may be sent and summed in bfloat16 or wider, within the bound.
No kernel may reach another device: no remote copies, remote signals or barrier semaphores. Data moves between devices by JAX's collectives and lax.ppermute only.
A program may use at most 384 MiB of HBM per device.

```python
import math
import jax
import jax.numpy as jnp
from jax import lax

D = 1536
QUERY_HEADS = 24
KEY_VALUE_HEADS = 8
HEAD_SIZE = 64
FE = 1024
E = 3
MB = 2
SEQ = 512
STEP = 10
CAP = 320
NSEQ = 32
QKV = 2560


def make_plan(key):
    seq_count = MB * NSEQ
    drawn = jax.random.randint(jax.random.fold_in(key, 101), (seq_count,), SEQ // 4, SEQ + 1)
    first_pick = jax.random.randint(jax.random.fold_in(key, 102), (), 0, seq_count)
    second_pick = (first_pick + 1 + jax.random.randint(jax.random.fold_in(key, 103), (), 0, seq_count - 1)) % seq_count
    drawn = drawn.at[first_pick].set(SEQ).at[second_pick].set(SEQ // 4)
    lengths = drawn.reshape(MB, NSEQ).astype(jnp.int32)
    grid_shape = (MB, NSEQ, SEQ)
    leading = jax.random.randint(jax.random.fold_in(key, 104), grid_shape, 0, E)
    forced_expert = jax.random.randint(jax.random.fold_in(key, 106), (), 0, E)
    sequence_ids = jnp.arange(seq_count).reshape(MB, NSEQ)[:, :, None]
    leading = jnp.where(sequence_ids == first_pick, forced_expert, leading)
    offset = jax.random.randint(jax.random.fold_in(key, 105), grid_shape, 1, E)
    trailing = (leading + offset) % E
    position = jnp.arange(SEQ)[None, None, :]
    is_valid = position < lengths[:, :, None]
    slot_lead = jnp.zeros(grid_shape, jnp.int32)
    slot_trail = jnp.zeros(grid_shape, jnp.int32)
    for expert in range(E):
        routed = (leading == expert) | (trailing == expert)
        priority = jnp.where(routed, jnp.where(is_valid, 0, 1), 2)
        jitter = jax.random.randint(jax.random.fold_in(key, 200 + expert), grid_shape, 0, 4096)
        ordering = (priority * 4096 + jitter) * SEQ + position
        ranks = jnp.argsort(jnp.argsort(ordering, axis=-1), axis=-1).astype(jnp.int32)
        slot_lead = jnp.where(leading == expert, ranks, slot_lead)
        slot_trail = jnp.where(trailing == expert, ranks, slot_trail)
    routes = jnp.stack([leading, trailing], axis=-1).astype(jnp.int32)
    slots = jnp.stack([slot_lead, slot_trail], axis=-1).astype(jnp.int32)
    return (lengths, routes, slots)


def draw_lengths(key, part):
    return make_plan(key)[0]


def draw_routes(key, part):
    return make_plan(key)[1]


def draw_slot_index(key, part):
    return make_plan(key)[2]


def level_of(own_key, dims, split, low, high):
    factor_of = 1.0
    for dim, shards_of in split:
        draws = jax.random.uniform(jax.random.fold_in(jax.random.fold_in(own_key, 6), dim), (shards_of,), jnp.float32, low / len(split), high / len(split))
        factor_of = factor_of * jnp.repeat(jnp.exp(draws), dims[dim] // shards_of).reshape((-1,) + (1,) * (len(dims) - 1 - dim))
    return factor_of


def noise(stream_key, extent, spread, bound, cuts=(), kind=jnp.bfloat16):
    values = spread * jax.random.normal(stream_key, extent, jnp.float32)
    if cuts:
        values = values * level_of(stream_key, extent, cuts, -0.22, 0.18)
    return jnp.clip(values, -bound, bound).astype(kind)


def setup_inputs(seed: int = 0) -> dict:
    key_list = jax.random.split(jax.random.key(seed), 24)
    tokens = noise(key_list[0], (MB, NSEQ, SEQ, D), 1.0, 6.0, ((1, 32),))
    cotangent = noise(key_list[1], (MB, NSEQ, SEQ, D), 1.0, 6.0, ((1, 32),))
    lengths = draw_lengths(jax.random.fold_in(key_list[23], 71), 0)
    routes = draw_routes(jax.random.fold_in(key_list[23], 71), 0)
    slot_index = draw_slot_index(jax.random.fold_in(key_list[23], 71), 0)
    norm_gains = jnp.clip(1.0 + 0.1 * jax.random.normal(key_list[5], (2, D), jnp.float32), 0.5, 1.5)
    norm_first = noise(key_list[6], (2, D), 0.0006, 0.0034179688, ((1, 8),), jnp.float32)
    norm_second = jnp.clip(jnp.exp(math.log(5.299999884300632e-06) - 1.40534253 * jax.random.uniform(key_list[7], (2, D), jnp.float32) ** level_of(key_list[7], (2, D), ((1, 8),), -0.2, 0.2)), 1.3000000080864993e-06, 5.299999884300632e-06)
    in_proj = noise(key_list[8], (D, QKV), D ** -0.5, 0.15625, ((0, 8),), jnp.float32)
    in_first = noise(key_list[9], (D, QKV), 0.0006, 0.0034179688, ((0, 8),), jnp.float32)
    in_second = jnp.clip(jnp.exp(math.log(5.299999884300632e-06) - 1.40534253 * jax.random.uniform(key_list[10], (D, QKV), jnp.float32) ** level_of(key_list[10], (D, QKV), ((0, 8),), -0.2, 0.2)), 1.3000000080864993e-06, 5.299999884300632e-06)
    out_proj = noise(key_list[11], (QUERY_HEADS * HEAD_SIZE, D), (QUERY_HEADS * HEAD_SIZE // 64) ** -0.5, 1.25, ((0, 8),), jnp.float32)
    out_first = noise(key_list[12], (QUERY_HEADS * HEAD_SIZE, D), 0.0006, 0.0034179688, ((0, 8),), jnp.float32)
    out_second = jnp.clip(jnp.exp(math.log(5.299999884300632e-06) - 1.40534253 * jax.random.uniform(key_list[13], (QUERY_HEADS * HEAD_SIZE, D), jnp.float32) ** level_of(key_list[13], (QUERY_HEADS * HEAD_SIZE, D), ((0, 8),), -0.2, 0.2)), 1.3000000080864993e-06, 5.299999884300632e-06)
    router = noise(key_list[14], (D, E), (2 * D) ** -0.5, 0.109375, ((0, 8),), jnp.float32)
    router_first = noise(key_list[15], (D, E), 0.0006, 0.0034179688, ((0, 8),), jnp.float32)
    router_second = jnp.clip(jnp.exp(math.log(5.299999884300632e-06) - 1.40534253 * jax.random.uniform(key_list[16], (D, E), jnp.float32) ** level_of(key_list[16], (D, E), ((0, 8),), -0.2, 0.2)), 1.3000000080864993e-06, 5.299999884300632e-06)
    up_proj = noise(key_list[17], (E, D, 2 * FE), D ** -0.5, 0.15625, ((1, 8),), jnp.float32)
    up_first = noise(key_list[18], (E, D, 2 * FE), 0.0006, 0.0034179688, ((1, 8),), jnp.float32)
    up_second = jnp.clip(jnp.exp(math.log(5.299999884300632e-06) - 1.40534253 * jax.random.uniform(key_list[19], (E, D, 2 * FE), jnp.float32) ** level_of(key_list[19], (E, D, 2 * FE), ((1, 8),), -0.2, 0.2)), 1.3000000080864993e-06, 5.299999884300632e-06)
    down_proj = noise(key_list[20], (E, FE, D), (FE // 8) ** -0.5, 0.5, ((1, 8),), jnp.float32)
    down_first = noise(key_list[21], (E, FE, D), 0.0006, 0.0034179688, ((1, 8),), jnp.float32)
    down_second = jnp.clip(jnp.exp(math.log(5.299999884300632e-06) - 1.40534253 * jax.random.uniform(key_list[22], (E, FE, D), jnp.float32) ** level_of(key_list[22], (E, FE, D), ((1, 8),), -0.2, 0.2)), 1.3000000080864993e-06, 5.299999884300632e-06)
    return dict(tokens=tokens, cotangent=cotangent, lengths=lengths, routes=routes, slot_index=slot_index, norm_gains=norm_gains, norm_first=norm_first, norm_second=norm_second, in_proj=in_proj, in_first=in_first, in_second=in_second, out_proj=out_proj, out_first=out_first, out_second=out_second, router=router, router_first=router_first, router_second=router_second, up_proj=up_proj, up_first=up_first, up_second=up_second, down_proj=down_proj, down_first=down_first, down_second=down_second)


@jax.custom_vjp
def low(v):
    return lax.optimization_barrier(v.astype(jnp.bfloat16)).astype(jnp.float32)

@jax.custom_vjp
def low_back(v):
    return v

def low_keep(v):
    return (low(v), None)

def low_pass(kept, grad):
    return (grad,)

def back_keep(v):
    return (v, None)

def back_low(kept, grad):
    return (low(grad),)
low.defvjp(low_keep, low_pass)
low_back.defvjp(back_keep, back_low)
precise = lax.Precision.HIGHEST
epsilon = 1e-06
beta_first = 0.9
beta_second = 0.95
learn_rate = 0.02
weight_decay = 0.1
adam_floor = 1e-08
clip_level = 0.005

def product(left_side, right_side):
    return jnp.dot(left_side, right_side, precision=precise)

def norm_scale(values):
    return lax.rsqrt(lax.optimization_barrier(jnp.mean(values * values, axis=-1, keepdims=True)) + epsilon)

def softmax_rows(scores):
    highest = lax.optimization_barrier(jnp.max(scores, axis=-1, keepdims=True))
    raised = jnp.exp(scores - highest)
    return raised / lax.optimization_barrier(jnp.sum(raised, axis=-1, keepdims=True))

def forward(rows_in, weights, length, route, slot):
    gains = low(weights[0])
    w_in = low(weights[1])
    w_out = low(weights[2])
    w_router = low(weights[3])
    w_up = low(weights[4])
    w_down = low(weights[5])
    sequence_length = rows_in.shape[0]
    position = jnp.arange(sequence_length)
    live_mask = (position < length).astype(jnp.float32)
    normed_one = low(rows_in * norm_scale(rows_in) * gains[0])
    projected_rows = low(low_back(product(normed_one, w_in)))
    query_width = QUERY_HEADS * HEAD_SIZE
    key_value_width = KEY_VALUE_HEADS * HEAD_SIZE
    query_rows = projected_rows[:, :query_width].reshape(sequence_length, KEY_VALUE_HEADS, QUERY_HEADS // KEY_VALUE_HEADS, HEAD_SIZE)
    key_rows_full = projected_rows[:, query_width:query_width + key_value_width].reshape(sequence_length, KEY_VALUE_HEADS, HEAD_SIZE)
    value_rows_full = projected_rows[:, query_width + key_value_width:].reshape(sequence_length, KEY_VALUE_HEADS, HEAD_SIZE)
    scores = low_back(jnp.einsum('qhgd,khd->hgqk', query_rows, key_rows_full, precision=precise) * HEAD_SIZE ** (-0.5))
    allowed = (position[None, :] <= position[:, None]) & (position[None, :] < length)
    scores = jnp.where(allowed, scores, -1000000000.0)
    probs = low(softmax_rows(scores))
    mixed = jnp.einsum('hgqk,khd->qhgd', probs, value_rows_full, precision=precise).reshape(sequence_length, query_width)
    mixed = low(low_back(mixed))
    residual = rows_in + low_back(product(mixed, w_out))
    normed_two = low(residual * norm_scale(residual) * gains[1])
    router_prob = softmax_rows(product(normed_two, w_router))
    onehot = (route[:, :, None] == jnp.arange(E)[None, None, :]).astype(jnp.float32)
    gate_weights = lax.optimization_barrier(jnp.sum(onehot * router_prob[:, None, :], axis=-1))
    keep_mask = ((position[:, None] < length) & (slot < CAP)).astype(jnp.float32)
    target = jnp.where(keep_mask > 0, route * CAP + slot, E * CAP).astype(jnp.int32)
    spread_rows = jnp.broadcast_to(normed_two[:, None, :], (sequence_length, 2, D)) * keep_mask[:, :, None]
    buffer = jnp.zeros((E * CAP + 1, D), jnp.float32).at[target.reshape(-1)].add(spread_rows.reshape(-1, D))
    expert_in = buffer[:E * CAP].reshape(E, CAP, D)
    gate_up = low_back(jnp.einsum('ecd,edf->ecf', expert_in, w_up, precision=precise))
    hidden = low(jax.nn.silu(gate_up[:, :, :FE]) * gate_up[:, :, FE:])
    expert_out = low_back(jnp.einsum('ecf,efd->ecd', hidden, w_down, precision=precise))
    padded = jnp.concatenate([expert_out.reshape(E * CAP, D), jnp.zeros((1, D), jnp.float32)], axis=0)
    mixture = lax.optimization_barrier(jnp.sum((gate_weights * keep_mask)[:, :, None] * padded[target], axis=1))
    return live_mask[:, None] * (residual + mixture)

def adam_step(master, first, second, gradient, rms, decayed):
    clipped = gradient * jnp.minimum(1.0, clip_level / rms)
    first_new = beta_first * first + (1.0 - beta_first) * clipped
    second_new = beta_second * second + (1.0 - beta_second) * clipped * clipped
    first_hat = first_new / (1.0 - beta_first ** STEP)
    second_hat = second_new / (1.0 - beta_second ** STEP)
    change = first_hat / (jnp.sqrt(second_hat) + adam_floor) + decayed * weight_decay * master
    update = -learn_rate * change
    return (gradient, update, first_new, second_new)

def reference(tokens, cotangent, lengths, routes, slot_index, norm_gains, norm_first, norm_second, in_proj, in_first, in_second, out_proj, out_first, out_second, router, router_first, router_second, up_proj, up_first, up_second, down_proj, down_first, down_second):
    masters = (norm_gains, in_proj, out_proj, router, up_proj, down_proj)
    seq_count = MB * NSEQ
    items = (tokens.reshape(seq_count, SEQ, D), cotangent.reshape(seq_count, SEQ, D), lengths.reshape(seq_count).astype(jnp.int32), routes.reshape(seq_count, SEQ, 2).astype(jnp.int32), slot_index.reshape(seq_count, SEQ, 2).astype(jnp.int32))

    def one_sequence(running, item):
        rows_in, cot_rows, length, route, slot = item

        def run(rows_float, weights):
            return forward(rows_float, weights, length, route, slot)
        result, pull = jax.vjp(run, rows_in.astype(jnp.float32), masters)
        rows_grad, weight_grads = pull(cot_rows.astype(jnp.float32))
        running = tuple((earlier + later for earlier, later in zip(running, weight_grads)))
        return (running, (result.astype(jnp.bfloat16), rows_grad.astype(jnp.bfloat16)))
    initial = tuple((jnp.zeros_like(master) for master in masters))
    totals, (results, row_grads) = lax.scan(one_sequence, initial, items)
    grad_scale = 1.0 / (MB * NSEQ)
    grads = tuple((total * grad_scale for total in totals))
    rms = jnp.stack([jnp.sqrt(jnp.mean(grad * grad) + epsilon) for grad in grads])
    norm_res = adam_step(norm_gains, norm_first, norm_second, grads[0], rms[0], 0.0)
    in_res = adam_step(in_proj, in_first, in_second, grads[1], rms[1], 1.0)
    out_res = adam_step(out_proj, out_first, out_second, grads[2], rms[2], 1.0)
    router_res = adam_step(router, router_first, router_second, grads[3], rms[3], 1.0)
    up_res = adam_step(up_proj, up_first, up_second, grads[4], rms[4], 1.0)
    down_res = adam_step(down_proj, down_first, down_second, grads[5], rms[5], 1.0)
    return (results.reshape(MB, NSEQ, SEQ, D), row_grads.reshape(MB, NSEQ, SEQ, D), rms[:5], rms[5:6], norm_res[0], norm_res[1], norm_res[2], norm_res[3], in_res[0], in_res[1], in_res[2], in_res[3], out_res[0], out_res[1], out_res[2], out_res[3], router_res[0], router_res[1], router_res[2], router_res[3], up_res[0], up_res[1], up_res[2], up_res[3], down_res[0], down_res[1], down_res[2], down_res[3])
```

```python
import functools

import jax
import jax.numpy as jnp
from jax import lax
from jax.experimental import pallas as pl
from jax.experimental.pallas import tpu as pltpu
from jax.sharding import PartitionSpec as P

QUERY_HEADS = 24
KEY_VALUE_HEADS = 8
HEAD_SIZE = 64
FE = 1024
E = 3
STEP = 10
CAP = 320
BLK = 512

epsilon = 1e-06
beta_first = 0.9
beta_second = 0.95
learn_rate = 0.02
weight_decay = 0.1
adam_floor = 1e-08
clip_level = 0.005

bf16 = jnp.bfloat16
f32 = jnp.float32

LAST = (((1,), (1,)), ((), ()))
FIRST = (((0,), (0,)), ((), ()))


def dot(a, b):
    return jnp.dot(a, b, preferred_element_type=f32)


def dot_last(a, b):
    return lax.dot_general(a, b, LAST, preferred_element_type=f32)


def dot_first(a, b):
    return lax.dot_general(a, b, FIRST, preferred_element_type=f32)


def params(mib=56):
    return pltpu.CompilerParams(vmem_limit_bytes=mib * 1024 * 1024)


def cost(flops, nbytes):
    return pl.CostEstimate(flops=int(flops), bytes_accessed=int(nbytes), transcendentals=0)


def whole(shape, space=None):
    zeros = (0,) * len(shape)
    return pl.BlockSpec(shape, lambda *_: zeros, pipeline_mode=pl.Buffered(1))


def round_up(n, m):
    return -(-n // m) * m


def shift_core_pairs(x, k):
    size = lax.axis_size("fsdp")
    return lax.ppermute(x, "fsdp", [(i, (i + 2 * k) % size) for i in range(size)])


def swap_core(x):
    size = lax.axis_size("fsdp")
    return lax.ppermute(x, "fsdp", [(i, i ^ 1) for i in range(size)])


def swap_replica(x, bit):
    size = lax.axis_size("replica")
    return lax.ppermute(x, "replica", [(i, i ^ bit) for i in range(size)])


def bit_order(first):
    bits = []
    while (1 << len(bits)) < lax.axis_size("replica"):
        bits.append(1 << len(bits))
    return bits[first % len(bits) :] + bits[: first % len(bits)]


def assemble_kernel(masks, places, idx_ref, *refs):
    n_in = 6
    ins, out, sems = refs[:n_in], refs[n_in], refs[n_in + 1]
    own, low, high, own_c, low_c, high_c = ins
    held = refs[n_in + 2]
    part, z, c = idx_ref[0], idx_ref[1], idx_ref[2]
    half = len(masks) // 2
    rows = low.shape[2]
    n_z = places + 1
    copies = []
    for group, core in (((own, low, high), c), ((own_c, low_c, high_c), 1 - c)):
        copies.append((group[0], held.at[2 * z + core]))
        for j, mask in enumerate(masks):
            source = group[1] if j < half else group[2]
            at = pl.multiple_of((part ^ mask) * rows, 16)
            for k in range(1, n_z):
                zk = lax.rem(z + n_z - k, n_z)
                copies.append((source.at[j % half, k - 1], held.at[2 * zk + core, pl.ds(at, rows)]))
    started = []
    for i, (source, target) in enumerate(copies):
        copy = pltpu.make_async_copy(source, target, sems.at[i])
        copy.start()
        started.append(copy)
    for copy in started:
        copy.wait()
    copy = pltpu.make_async_copy(held, out, sems.at[len(copies)])
    copy.start()
    copy.wait()


def gather_packed(shard, first):
    n_rep, n_f = lax.axis_size("replica"), lax.axis_size("fsdp")
    n_z = n_f // 2
    rows = shard.shape[0] // n_rep
    part, place = lax.axis_index("replica"), lax.axis_index("fsdp")
    own_c = swap_core(shard)
    mine = lax.dynamic_slice_in_dim(shard, part * rows, rows, axis=0)
    stack = jnp.stack([shift_core_pairs(mine, k) for k in range(1, n_z)])[None]
    masks = [0]
    order = bit_order(first)
    for i, bit in enumerate(order):
        received = swap_replica(stack, bit)
        masks = masks + [m ^ bit for m in masks]
        if i < len(order) - 1:
            stack = jnp.concatenate([stack, received])
    low, high = stack, received
    low_c, high_c = swap_core(low), swap_core(high)
    idx = jnp.stack([part, place // 2, place % 2]).astype(jnp.int32)
    anyspec = pl.BlockSpec(memory_space=pl.ANY)
    n_copies = 2 * (1 + n_rep * (n_z - 1))
    return pl.pallas_call(
        functools.partial(assemble_kernel, tuple(masks), n_z - 1),
        out_shape=jax.ShapeDtypeStruct((n_f,) + shard.shape, bf16),
        grid_spec=pltpu.PrefetchScalarGridSpec(
            num_scalar_prefetch=1,
            grid=(1,),
            in_specs=[anyspec] * 6,
            out_specs=anyspec,
            scratch_shapes=[
                pltpu.SemaphoreType.DMA((n_copies + 1,)),
                pltpu.VMEM((n_f,) + shard.shape, bf16),
            ],
        ),
        compiler_params=params(),
        cost_estimate=cost(0, 4 * n_f * shard.size),
        name="assemble",
    )(idx, shard, low, high, own_c, low_c, high_c)


def reduce_packed(keep, send, first):
    n_rep, n_z = lax.axis_size("replica"), lax.axis_size("fsdp") // 2
    part, place = lax.axis_index("replica"), lax.axis_index("fsdp")
    z = place // 2
    rows = keep.shape[1] // n_rep
    order = bit_order(first)
    n_bits = len(order)
    shape = (n_z,) + (2,) * n_bits + (rows, BLK)
    bits = [1 << b for b in range(n_bits)]
    live = list(reversed(bits))
    terms = [keep.reshape(shape), swap_core(send).reshape(shape)]

    def part_sum(index, axis):
        return functools.reduce(
            jnp.add, [lax.dynamic_index_in_dim(t, index, axis, keepdims=False).astype(f32) for t in terms]
        )

    for bit in order:
        axis = 1 + live.index(bit)
        live.remove(bit)
        own = (part // bit) % 2
        got = swap_replica(part_sum(1 - own, axis).astype(bf16), bit)
        terms = [lax.dynamic_index_in_dim(t, own, axis, keepdims=False) for t in terms] + [got]
    gots = [shift_core_pairs(part_sum((z + k) % n_z, 0).astype(bf16), k) for k in range(1, n_z)]
    summed = part_sum(z, 0)
    for got in gots:
        summed = summed + got.astype(f32)
    stack = summed.astype(bf16)
    done = []
    for bit in order:
        got = swap_replica(stack, bit)
        own = (part // bit) % 2
        pair = jnp.stack([stack, got])
        stack = jnp.where(own == 1, pair[::-1], pair)
    names = list(reversed(order))
    stack = jnp.transpose(stack, tuple(names.index(b) for b in reversed(bits)) + (n_bits, n_bits + 1))
    return stack.reshape(n_rep * rows, BLK)


def sum_small(x):
    size = lax.axis_size("fsdp")
    bit = 1
    while bit < size:
        x = x + lax.ppermute(x, "fsdp", [(i, i ^ bit) for i in range(size)])
        bit *= 2
    return x


def sum_all(x):
    x = sum_small(x)
    bit = 1
    while bit < lax.axis_size("replica"):
        x = x + swap_replica(x, bit)
        bit *= 2
    return x


def pack_kernel(counts, *refs):
    out = refs[-1]
    at = 0
    for ref, n in zip(refs, counts):
        value = ref[0] if len(ref.shape) == 3 else ref[...]
        for j in range(n):
            out[at : at + value.shape[0], :] = value[:, j * BLK : (j + 1) * BLK].astype(bf16)
            at += value.shape[0]
    if len(refs) - 1 > len(counts):
        extra = refs[len(counts)][...]
        out[at : at + extra.shape[0], :] = extra
        at += extra.shape[0]
    if at < out.shape[0]:
        out[at:, :] = jnp.zeros((out.shape[0] - at, BLK), bf16)


def pack_call(parts, unit, extra=None):
    specs, counts, total = [], [], 0
    for w, e in parts:
        if e is None:
            specs.append(pl.BlockSpec(w.shape, lambda i: (0, 0)))
        else:
            specs.append(pl.BlockSpec((1,) + w.shape[1:], lambda i, e=e: (e, 0, 0)))
        counts.append(w.shape[-1] // BLK)
        total += counts[-1] * w.shape[-2]
    args = [w for w, _ in parts]
    if extra is not None:
        args.append(extra)
        specs.append(pl.BlockSpec(extra.shape, lambda i: (0, 0)))
        total += extra.shape[0]
    total = round_up(total, unit)
    return pl.pallas_call(
        functools.partial(pack_kernel, tuple(counts)),
        grid=(1,),
        in_specs=specs,
        out_specs=pl.BlockSpec((total, BLK), lambda i: (0, 0)),
        out_shape=jax.ShapeDtypeStruct((total, BLK), bf16),
        compiler_params=params(),
        cost_estimate=cost(0, 6 * total * BLK),
        name="pack",
    )(*args)


def pad_rows(x, rows):
    return jnp.pad(x, ((0, rows - x.shape[0]), (0, 0)))


def qkv_kernel(x_ref, gain_ref, w_ref, qkv_ref, n1_ref):
    tokens, width = x_ref.shape

    @pl.when(pl.program_id(0) == 0)
    def _():
        def body(i, _):
            rows = pl.ds(pl.multiple_of(i * 128, 128), 128)
            xf = x_ref[rows, :].astype(f32)
            scale = lax.rsqrt(jnp.mean(xf * xf, axis=-1, keepdims=True) + epsilon)
            n1_ref[rows, :] = (xf * scale * gain_ref[...]).astype(bf16)
            return 0

        lax.fori_loop(0, tokens // 128, body, 0)

    w = w_ref[...].reshape(width, BLK)

    def body(i, _):
        rows = pl.ds(pl.multiple_of(i * 256, 256), 256)
        qkv_ref[rows, :] = dot(n1_ref[rows, :], w).astype(bf16)
        return 0

    lax.fori_loop(0, tokens // 256, body, 0)


def qkv_call(x, gain, w_in, rows, n):
    tokens, width = x.shape
    n_f = w_in.shape[0]
    return pl.pallas_call(
        qkv_kernel,
        grid=(n,),
        in_specs=[
            whole((tokens, width)),
            whole((1, width)),
            pl.BlockSpec((n_f, rows, BLK), lambda j: (0, j, 0)),
        ],
        out_specs=[
            pl.BlockSpec((tokens, BLK), lambda j: (0, j)),
            pl.BlockSpec((tokens, width), lambda j: (0, 0)),
        ],
        out_shape=[
            jax.ShapeDtypeStruct((tokens, n * BLK), bf16),
            jax.ShapeDtypeStruct((tokens, width), bf16),
        ],
        compiler_params=params(),
        cost_estimate=cost(2 * tokens * width * n * BLK, 2 * width * n * BLK + 4 * tokens * width),
        name="qkv",
    )(x, gain, w_in)


HALF = 256


def attention_kernel(len_ref, q_ref, k_ref, v_ref, p_ref, mix_ref):
    seq = q_ref.shape[0]
    length = len_ref[pl.program_id(0)]
    key = lax.broadcasted_iota(jnp.int32, (seq, seq), 0)
    query = lax.broadcasted_iota(jnp.int32, (seq, seq), 1)
    bias = jnp.where((key <= query) & (key < length), 0.0, -1000000000.0).astype(f32)
    group = QUERY_HEADS // KEY_VALUE_HEADS
    for h in range(2 * group):
        g = h // group
        lanes = slice(h * HEAD_SIZE, (h + 1) * HEAD_SIZE)
        kv = slice(g * HEAD_SIZE, (g + 1) * HEAD_SIZE)
        q = q_ref[:, lanes] * jnp.asarray(HEAD_SIZE ** (-0.5), bf16)
        for start in range(0, seq, HALF):
            stop = start + HALF
            s = dot_last(k_ref[:stop, kv], q[start:stop]) + bias[:stop, start:stop]
            raised = jnp.exp(s - jnp.max(s, axis=0, keepdims=True))
            probs = (raised * (1.0 / jnp.sum(raised, axis=0, keepdims=True))).astype(bf16)
            p_ref[0, h, :stop, start:stop] = probs
            if stop < seq:
                p_ref[0, h, stop:, start:stop] = jnp.zeros((seq - stop, HALF), bf16)
            mixed = dot_first(v_ref[:stop, kv], probs)
            mix_ref[start:stop, lanes] = mixed.T.astype(bf16)


def attention_call(lengths, qkv, n_seq):
    tokens = qkv.shape[0]
    seq = tokens // n_seq
    pairs = KEY_VALUE_HEADS // 2
    heads = QUERY_HEADS // pairs
    qw = heads * HEAD_SIZE
    kw = 2 * HEAD_SIZE
    k_at = QUERY_HEADS * HEAD_SIZE // kw
    v_at = k_at + pairs
    return pl.pallas_call(
        attention_kernel,
        grid_spec=pltpu.PrefetchScalarGridSpec(
            num_scalar_prefetch=1,
            grid=(n_seq, pairs),
            in_specs=[
                pl.BlockSpec((seq, qw), lambda s, j, _: (s, j)),
                pl.BlockSpec((seq, kw), lambda s, j, _: (s, k_at + j)),
                pl.BlockSpec((seq, kw), lambda s, j, _: (s, v_at + j)),
            ],
            out_specs=[
                pl.BlockSpec((1, heads, seq, seq), lambda s, j, _: (s, j, 0, 0)),
                pl.BlockSpec((seq, qw), lambda s, j, _: (s, j)),
            ],
        ),
        out_shape=[
            jax.ShapeDtypeStruct((n_seq, QUERY_HEADS, seq, seq), bf16),
            jax.ShapeDtypeStruct((tokens, QUERY_HEADS * HEAD_SIZE), bf16),
        ],
        compiler_params=params(),
        cost_estimate=cost(16 * n_seq * QUERY_HEADS * seq * seq * HEAD_SIZE, 2 * n_seq * QUERY_HEADS * seq * seq),
        name="attention",
    )(lengths, qkv, qkv, qkv)


def attention_back_kernel(q_ref, k_ref, v_ref, p_ref, mix_ref, dmix_ref, dq_ref, dk_ref, dv_ref):
    seq = q_ref.shape[0]
    group = QUERY_HEADS // KEY_VALUE_HEADS
    scale = HEAD_SIZE ** (-0.5)
    ones = jnp.ones((8, HEAD_SIZE), bf16)
    for g in range(2):
        kv = slice(g * HEAD_SIZE, (g + 1) * HEAD_SIZE)
        k, v = k_ref[:, kv], v_ref[:, kv]
        n_half = seq // HALF
        dk = [jnp.zeros((HALF, HEAD_SIZE), f32) for _ in range(n_half)]
        dv = [jnp.zeros((HALF, HEAD_SIZE), f32) for _ in range(n_half)]
        for i in range(group):
            h = g * group + i
            lanes = slice(h * HEAD_SIZE, (h + 1) * HEAD_SIZE)
            for start in range(0, seq, HALF):
                stop = start + HALF
                dmix = dmix_ref[start:stop, lanes]
                q = q_ref[start:stop, lanes]
                both = dmix.astype(f32) * mix_ref[start:stop, lanes].astype(f32)
                high = both.astype(bf16)
                low = (both - high.astype(f32)).astype(bf16)
                delta = (dot_last(ones, high) + dot_last(ones, low))[:1]
                probs = p_ref[0, h, :stop, start:stop]
                dp = dot_last(v[:stop], dmix)
                ds = (probs.astype(f32) * (dp - delta)).astype(bf16)
                dq = dot_first(k[:stop], ds)
                dq_ref[start:stop, lanes] = (dq.T * scale).astype(bf16)
                dk_part = dot(ds, q)
                dv_part = dot(probs, dmix)
                for m in range(stop // HALF):
                    rows = slice(m * HALF, (m + 1) * HALF)
                    dk[m] += dk_part[rows]
                    dv[m] += dv_part[rows]
        for m in range(n_half):
            rows = slice(m * HALF, (m + 1) * HALF)
            dk_ref[rows, kv] = (dk[m] * scale).astype(bf16)
            dv_ref[rows, kv] = dv[m].astype(bf16)


def attention_back_call(qkv, probs, mixed, dmixed, n_seq):
    tokens = qkv.shape[0]
    seq = tokens // n_seq
    pairs = KEY_VALUE_HEADS // 2
    heads = QUERY_HEADS // pairs
    qw = heads * HEAD_SIZE
    kw = 2 * HEAD_SIZE
    k_at = QUERY_HEADS * HEAD_SIZE // kw
    v_at = k_at + pairs
    qspec = pl.BlockSpec((seq, qw), lambda s, j: (s, j))
    kspec = pl.BlockSpec((seq, kw), lambda s, j: (s, j))
    return pl.pallas_call(
        attention_back_kernel,
        grid=(n_seq, pairs),
        in_specs=[
            qspec,
            pl.BlockSpec((seq, kw), lambda s, j: (s, k_at + j)),
            pl.BlockSpec((seq, kw), lambda s, j: (s, v_at + j)),
            pl.BlockSpec((1, heads, seq, seq), lambda s, j: (s, j, 0, 0)),
            qspec,
            qspec,
        ],
        out_specs=[qspec, kspec, kspec],
        out_shape=[
            jax.ShapeDtypeStruct((tokens, QUERY_HEADS * HEAD_SIZE), bf16),
            jax.ShapeDtypeStruct((tokens, KEY_VALUE_HEADS * HEAD_SIZE), bf16),
            jax.ShapeDtypeStruct((tokens, KEY_VALUE_HEADS * HEAD_SIZE), bf16),
        ],
        compiler_params=params(),
        cost_estimate=cost(32 * n_seq * QUERY_HEADS * seq * seq * HEAD_SIZE, 2 * n_seq * QUERY_HEADS * seq * seq),
        name="attention_back",
    )(qkv, qkv, qkv, probs, mixed, dmixed)


TILE = 256


def resid_kernel(rows, n, mix_ref, w_ref, x_ref, gain_ref, router_ref, resid_ref, n2_ref, prob_ref):
    width = x_ref.shape[1]
    mixed = mix_ref[...]
    squares = jnp.zeros((TILE, 1), f32)
    for j in range(n):
        cols = slice(j * BLK, (j + 1) * BLK)
        w = w_ref[:, j * rows : (j + 1) * rows, :].reshape(-1, BLK)
        part = x_ref[:, cols].astype(f32) + dot(mixed, w)
        resid_ref[:, cols] = part
        squares += jnp.sum(part * part, axis=-1, keepdims=True)
    scale = lax.rsqrt(squares * (1.0 / width) + epsilon)
    n2 = (resid_ref[...] * scale * gain_ref[...]).astype(bf16)
    n2_ref[...] = n2
    logits = dot_last(router_ref[...], n2)
    logits = jnp.where(lax.broadcasted_iota(jnp.int32, logits.shape, 0) < E, logits, -1e30)
    raised = jnp.exp(logits - jnp.max(logits, axis=0, keepdims=True))
    prob_ref[...] = raised / jnp.sum(raised, axis=0, keepdims=True)


def resid_call(mixed, w_out, x, gain, router, rows, n):
    tokens, width = x.shape
    tile = pl.BlockSpec((TILE, width), lambda i: (i, 0))
    return pl.pallas_call(
        functools.partial(resid_kernel, rows, n),
        grid=(tokens // TILE,),
        in_specs=[
            tile,
            whole((w_out.shape[0], n * rows, BLK)),
            tile,
            whole((1, width)),
            whole((8, width)),
        ],
        out_specs=[tile, tile, pl.BlockSpec((8, TILE), lambda i: (0, i))],
        out_shape=[
            jax.ShapeDtypeStruct((tokens, width), f32),
            jax.ShapeDtypeStruct((tokens, width), bf16),
            jax.ShapeDtypeStruct((8, tokens), f32),
        ],
        compiler_params=params(),
        cost_estimate=cost(2 * tokens * width * width, 2 * width * width + 12 * tokens * width),
        name="resid",
    )(mixed, w_out, x, gain, router)


def dispatch_kernel(slot_ref, prob_ref, n2_ref, cot_ref, buf_ref, dys_ref, gate_ref):
    e = pl.program_id(1)
    slots = slot_ref[0, pl.ds(e, 1), :]
    hit = lax.broadcasted_iota(jnp.int32, (CAP, slots.shape[1]), 0) == slots
    gate = jnp.sum(jnp.where(hit, prob_ref[pl.ds(e, 1), :], 0.0), axis=-1, keepdims=True)
    gate_ref[0, 0] = jnp.broadcast_to(gate, (CAP, 128))
    hit = jnp.where(hit, 1.0, 0.0).astype(bf16)
    buf_ref[0, 0] = dot(hit, n2_ref[...]).astype(bf16)
    dys_ref[0, 0] = dot(hit, cot_ref[...]).astype(bf16)


def dispatch_call(slots, prob, n2, cot, n_seq):
    tokens, width = n2.shape
    seq = tokens // n_seq
    out = pl.BlockSpec((1, 1, CAP, width), lambda s, e: (e, s, 0, 0))
    return pl.pallas_call(
        dispatch_kernel,
        grid=(n_seq, E),
        in_specs=[
            pl.BlockSpec((1, 8, seq), lambda s, e: (s, 0, 0)),
            pl.BlockSpec((8, seq), lambda s, e: (0, s)),
            pl.BlockSpec((seq, width), lambda s, e: (s, 0)),
            pl.BlockSpec((seq, width), lambda s, e: (s, 0)),
        ],
        out_specs=[out, out, pl.BlockSpec((1, 1, CAP, 128), lambda s, e: (e, s, 0, 0))],
        out_shape=[
            jax.ShapeDtypeStruct((E, n_seq, CAP, width), bf16),
            jax.ShapeDtypeStruct((E, n_seq, CAP, width), bf16),
            jax.ShapeDtypeStruct((E, n_seq, CAP, 128), f32),
        ],
        compiler_params=params(),
        cost_estimate=cost(4 * E * CAP * tokens * width, 20 * tokens * width),
        name="dispatch",
    )(slots, prob, n2, cot)


def split_cores(block, c, rows):
    parts = block.reshape(-1, 2, rows, block.shape[-1])
    even, odd = parts[:, 0], parts[:, 1]
    return (
        jnp.where(c == 0, even, odd).astype(bf16),
        jnp.where(c == 0, odd, even).astype(bf16),
    )


def expert_kernel(
    e,
    up_rows,
    down_rows,
    idx_ref,
    buf_ref,
    dys_ref,
    gate_ref,
    slot_ref,
    up_a_ref,
    up_b_ref,
    down_ref,
    yg_ref,
    dbuf_ref,
    dgate_ref,
    keep_ref,
    send_ref,
    y_acc,
    d_acc,
    dyexp_ref,
    hid_ref,
    da_ref,
    db_ref,
    dg_acc,
    up_held,
    down_held,
    sems,
):
    h = pl.program_id(0)
    last = pl.num_programs(0) - 1
    c = idx_ref[0]
    n_seq = buf_ref.shape[1]
    width = buf_ref.shape[3]
    n_d = width // BLK
    up_a = up_a_ref[...].reshape(width, BLK)
    up_b = up_b_ref[...].reshape(width, BLK)
    downs = [down_ref[:, j * down_rows : (j + 1) * down_rows, :].reshape(BLK, BLK) for j in range(n_d)]
    for s in range(n_seq):
        rows = slice(s * CAP, (s + 1) * CAP)
        gate = gate_ref[0, s, :, :1]

        @pl.when(h == 0)
        def _():
            dyexp_ref[rows, :] = (gate * dys_ref[0, s].astype(f32)).astype(bf16)

        x = buf_ref[0, s]
        a = dot(x, up_a)
        b = dot(x, up_b)
        sigma = jax.nn.sigmoid(a)
        silu = a * sigma
        hid = (silu * b).astype(bf16)
        hid_ref[rows, :] = hid
        du = dot_last(dys_ref[0, s, :, :BLK], downs[0])
        for j in range(1, n_d):
            du += dot_last(dys_ref[0, s, :, j * BLK : (j + 1) * BLK], downs[j])
        dg = jnp.sum(du * hid.astype(f32), axis=-1, keepdims=True)
        dh = gate * du
        da = (dh * b * sigma * (1.0 + a * (1.0 - sigma))).astype(bf16)
        db = (dh * silu).astype(bf16)
        da_ref[rows, :] = da
        db_ref[rows, :] = db

        @pl.when(h == 0)
        def _():
            dg_acc[rows, :] = jnp.broadcast_to(dg, (CAP, 128))
            for j in range(n_d):
                y_acc[rows, j * BLK : (j + 1) * BLK] = dot(hid, downs[j])
            d_acc[rows, :] = dot_last(da, up_a) + dot_last(db, up_b)

        @pl.when(h > 0)
        def _():
            dg_acc[rows, :] += jnp.broadcast_to(dg, (CAP, 128))
            for j in range(n_d):
                y_acc[rows, j * BLK : (j + 1) * BLK] += dot(hid, downs[j])
            d_acc[rows, :] += dot_last(da, up_a) + dot_last(db, up_b)

        @pl.when(h == last)
        def _():
            yg_ref[s] = (gate * y_acc[rows, :]).astype(bf16)
            dbuf_ref[s] = d_acc[rows, :].astype(bf16)
            slots = slot_ref[s, e : e + 1, :]
            hit = lax.broadcasted_iota(jnp.int32, (CAP, slots.shape[1]), 0) == slots
            row = jnp.sum(jnp.where(hit, dg_acc[rows, :1], 0.0), axis=0, keepdims=True)
            dgate_ref[s] = jnp.broadcast_to(row, (8, slots.shape[1]))

    step = 384
    per = step // (2 * up_rows)

    for m in range(width // step):
        x = jnp.concatenate([buf_ref[0, s, :, m * step : (m + 1) * step] for s in range(n_seq)], axis=0)
        xt = x.T
        for i, d_ref in enumerate((da_ref, db_ref)):
            keep, send = split_cores(dot(xt, d_ref[...]), c, up_rows)
            up_held[h, 0, i, m * per : (m + 1) * per] = keep
            up_held[h, 1, i, m * per : (m + 1) * per] = send
    hid_t = hid_ref[...].T
    for j in range(n_d):
        keep, send = split_cores(dot(hid_t, dyexp_ref[:, j * BLK : (j + 1) * BLK]), c, down_rows)
        down_held[h, 0, :, j * down_rows : (j + 1) * down_rows, :] = keep
        down_held[h, 1, :, j * down_rows : (j + 1) * down_rows, :] = send
    n_h = FE // BLK
    n_zh = keep_ref.shape[0] // n_h

    def copies(step):
        found = []
        for side, ref in enumerate((keep_ref, send_ref)):
            for i in range(2):
                place = pl.ds((i * n_h + step) * up_rows, up_rows)
                found.append((up_held.at[step, side, i], ref.at[:, place, :]))
            place = pl.ds(2 * n_h * up_rows, n_d * down_rows)
            found.append((down_held.at[step, side], ref.at[step * n_zh : (step + 1) * n_zh, place, :]))
        return [pltpu.make_async_copy(a, b, sems.at[step, i]) for i, (a, b) in enumerate(found)]

    for step in range(n_h):

        @pl.when(h == step)
        def _():
            for copy in copies(step):
                copy.start()

    @pl.when(h == last)
    def _():
        for step in range(n_h):
            for copy in copies(step):
                copy.wait()


def expert_call(e, at, core, buf, dys, gates, slots, w, up_rows, down_rows, unit):
    _, n_seq, _, width = buf.shape
    n_f = w.shape[0]
    n_z = n_f // 2
    n_h = FE // BLK
    n_d = width // BLK
    seq = slots.shape[2]
    data = pl.BlockSpec((1, n_seq, CAP, width), lambda h, _: (e, 0, 0, 0), pipeline_mode=pl.Buffered(1))
    out = pl.BlockSpec((n_seq, CAP, width), lambda h, _: (0, 0, 0))
    anyspec = pl.BlockSpec(memory_space=pl.ANY)
    total = round_up(2 * n_h * up_rows + n_d * down_rows, unit)
    grad_shape = jax.ShapeDtypeStruct((n_z, total, BLK), bf16)
    rows = n_seq * CAP
    yg, dbuf, dgate, keep, send = pl.pallas_call(
        functools.partial(expert_kernel, e, up_rows, down_rows),
        grid_spec=pltpu.PrefetchScalarGridSpec(
            num_scalar_prefetch=1,
            grid=(n_h,),
            in_specs=[
                data,
                data,
                pl.BlockSpec((1, n_seq, CAP, 128), lambda h, _: (e, 0, 0, 0)),
                pl.BlockSpec((n_seq, 8, seq), lambda h, _: (0, 0, 0)),
                pl.BlockSpec((n_f, up_rows, BLK), lambda h, _: (0, at // up_rows + h, 0)),
                pl.BlockSpec((n_f, up_rows, BLK), lambda h, _: (0, at // up_rows + n_h + h, 0)),
                pl.BlockSpec(
                    (n_f // n_h, n_d * down_rows, BLK),
                    lambda h, _: (h, (at + 2 * n_h * up_rows) // (n_d * down_rows), 0),
                ),
            ],
            out_specs=[
                out,
                out,
                pl.BlockSpec((n_seq, 8, seq), lambda h, _: (0, 0, 0)),
                anyspec,
                anyspec,
            ],
            scratch_shapes=[
                pltpu.VMEM((rows, width), f32),
                pltpu.VMEM((rows, width), f32),
                pltpu.VMEM((rows, width), bf16),
                pltpu.VMEM((rows, BLK), bf16),
                pltpu.VMEM((rows, BLK), bf16),
                pltpu.VMEM((rows, BLK), bf16),
                pltpu.VMEM((rows, 128), f32),
                pltpu.VMEM((n_h, 2, 2, n_z, up_rows, BLK), bf16),
                pltpu.VMEM((n_h, 2, n_z // n_h, n_d * down_rows, BLK), bf16),
                pltpu.SemaphoreType.DMA((n_h, 6)),
            ],
        ),
        out_shape=[
            jax.ShapeDtypeStruct((n_seq, CAP, width), bf16),
            jax.ShapeDtypeStruct((n_seq, CAP, width), bf16),
            jax.ShapeDtypeStruct((n_seq, 8, seq), f32),
            grad_shape,
            grad_shape,
        ],
        compiler_params=params(60),
        cost_estimate=cost(18 * rows * width * FE, 40 * width * FE),
        name="expert",
    )(core, buf, dys, gates, slots, w, w, w)
    return yg, dbuf, dgate[:, 0], keep, send


def spread(col_ref, e):
    slots = col_ref[:, e : e + 1]
    hit = lax.broadcasted_iota(jnp.int32, (col_ref.shape[0], CAP), 1) == slots
    return jnp.where(hit, 1.0, 0.0).astype(bf16)


def combine_kernel(col_ref, resid_ref, y0_ref, y1_ref, y2_ref, out_ref):
    total = resid_ref[...]
    for e, y_ref in enumerate((y0_ref, y1_ref, y2_ref)):
        total += dot(spread(col_ref, e), y_ref[0])
    out_ref[...] = jnp.where(col_ref[:, E : E + 1] > 0, total, 0.0).astype(bf16)


def combine_call(cols, resid, ys, n_seq):
    tokens, width = resid.shape
    per = tokens // n_seq // TILE
    tile = pl.BlockSpec((TILE, width), lambda i: (i, 0))
    return pl.pallas_call(
        combine_kernel,
        grid=(tokens // TILE,),
        in_specs=[pl.BlockSpec((TILE, 8), lambda i: (i, 0)), tile]
        + [pl.BlockSpec((1, CAP, width), lambda i: (i // per, 0, 0))] * E,
        out_specs=tile,
        out_shape=jax.ShapeDtypeStruct((tokens, width), bf16),
        compiler_params=params(),
        cost_estimate=cost(2 * E * CAP * tokens * width, 12 * tokens * width),
        name="combine",
    )(cols, resid, *ys)


def hi_lo(x):
    high = x.astype(bf16)
    return high, (x - high.astype(f32)).astype(bf16)


def middle_kernel(
    rows,
    n,
    col_ref,
    d0_ref,
    d1_ref,
    d2_ref,
    prob_ref,
    dprob_ref,
    router_ref,
    n2_ref,
    resid_ref,
    cot_ref,
    gain_ref,
    w_ref,
    dresid_ref,
    dattn_ref,
    dmix_ref,
    small_ref,
):
    width = resid_ref.shape[1]

    @pl.when(pl.program_id(0) == 0)
    def _():
        small_ref[...] = jnp.zeros_like(small_ref)

    prob, dprob = prob_ref[...], dprob_ref[...]
    dlogit = prob * (dprob - jnp.sum(dprob * prob, axis=0, keepdims=True))
    high, low = hi_lo(dlogit)
    dn2 = dot_first(high, router_ref[...]) + dot_first(low, router_ref[...])
    for e, d_ref in enumerate((d0_ref, d1_ref, d2_ref)):
        dn2 += dot(spread(col_ref, e), d_ref[0])
    n2 = n2_ref[...]
    small_ref[:8, :] += dot(high, n2) + dot(low, n2)
    resid = resid_ref[...]
    scale = lax.rsqrt(jnp.mean(resid * resid, axis=-1, keepdims=True) + epsilon)
    small_ref[8:, :] += jnp.broadcast_to(jnp.sum(dn2 * resid * scale, axis=0, keepdims=True), (8, width))
    weighted = dn2 * gain_ref[...]
    along = jnp.mean(weighted * resid, axis=-1, keepdims=True)
    dy = jnp.where(col_ref[:, E : E + 1] > 0, cot_ref[...].astype(f32), 0.0)
    dresid = dy + scale * weighted - resid * (scale * scale * scale * along)
    dresid_ref[...] = dresid
    dattn = dresid.astype(bf16)
    dattn_ref[...] = dattn
    dmix = dot_last(dattn[:, :BLK], w_ref[:, :rows, :].reshape(-1, BLK))
    for j in range(1, n):
        w = w_ref[:, j * rows : (j + 1) * rows, :].reshape(-1, BLK)
        dmix += dot_last(dattn[:, j * BLK : (j + 1) * BLK], w)
    dmix_ref[...] = dmix.astype(bf16)


def middle_call(cols, ds, prob, dprob, router, n2, resid, cot, gain, w_out, rows, n, n_seq):
    tokens, width = resid.shape
    per = tokens // n_seq // TILE
    tile = pl.BlockSpec((TILE, width), lambda i: (i, 0))
    row8 = pl.BlockSpec((8, TILE), lambda i: (0, i))
    return pl.pallas_call(
        functools.partial(middle_kernel, rows, n),
        grid=(tokens // TILE,),
        in_specs=[pl.BlockSpec((TILE, 8), lambda i: (i, 0))]
        + [pl.BlockSpec((1, CAP, width), lambda i: (i // per, 0, 0))] * E
        + [
            row8,
            row8,
            whole((8, width)),
            tile,
            tile,
            tile,
            whole((1, width)),
            whole((w_out.shape[0], n * rows, BLK)),
        ],
        out_specs=[tile, tile, tile, pl.BlockSpec((16, width), lambda i: (0, 0))],
        out_shape=[
            jax.ShapeDtypeStruct((tokens, width), f32),
            jax.ShapeDtypeStruct((tokens, width), bf16),
            jax.ShapeDtypeStruct((tokens, width), bf16),
            jax.ShapeDtypeStruct((16, width), f32),
        ],
        compiler_params=params(),
        cost_estimate=cost(2 * tokens * width * (width + E * CAP), 20 * tokens * width),
        name="middle",
    )(cols, *ds, prob, dprob, router, n2, resid, cot, gain, w_out)


def weight_grad_kernel(rows, idx_ref, left_ref, right_ref, keep_ref, send_ref, turned_ref):
    c = idx_ref[0]
    width = left_ref.shape[1]
    step = 384
    per = step // (2 * rows)

    @pl.when(pl.program_id(0) == 0)
    def _():
        for m in range(width // step):
            turned_ref[m * step : (m + 1) * step, :] = left_ref[:, m * step : (m + 1) * step].T

    right = right_ref[...]
    for m in range(width // step):
        keep, send = split_cores(dot(turned_ref[m * step : (m + 1) * step, :], right), c, rows)
        keep_ref[m * per : (m + 1) * per] = keep
        send_ref[m * per : (m + 1) * per] = send


def weight_grad_call(core, left, right, rows, n_z, name):
    tokens, width = left.shape
    n = right.shape[1] // BLK
    out = pl.BlockSpec((n_z, rows, BLK), lambda j, _: (0, j, 0))
    shape = jax.ShapeDtypeStruct((n_z, n * rows, BLK), bf16)
    return pl.pallas_call(
        functools.partial(weight_grad_kernel, rows),
        grid_spec=pltpu.PrefetchScalarGridSpec(
            num_scalar_prefetch=1,
            grid=(n,),
            in_specs=[
                pl.BlockSpec((tokens, width), lambda j, _: (0, 0), pipeline_mode=pl.Buffered(1)),
                pl.BlockSpec((tokens, BLK), lambda j, _: (0, j)),
            ],
            out_specs=[out, out],
            scratch_shapes=[pltpu.VMEM((width, tokens), bf16)],
        ),
        out_shape=[shape, shape],
        compiler_params=params(),
        cost_estimate=cost(2 * tokens * width * n * BLK, 2 * width * n * BLK + 4 * tokens * width),
        name=name,
    )(core, left, right)


def input_grad_kernel(rows, n, d_ref, w_ref, x_ref, dresid_ref, gain_ref, out_ref, small_ref):
    width = x_ref.shape[1]

    @pl.when(pl.program_id(0) == 0)
    def _():
        small_ref[...] = jnp.zeros_like(small_ref)

    dn1 = dot_last(d_ref[:, :BLK], w_ref[:, :rows, :].reshape(-1, BLK))
    for j in range(1, n):
        w = w_ref[:, j * rows : (j + 1) * rows, :].reshape(-1, BLK)
        dn1 += dot_last(d_ref[:, j * BLK : (j + 1) * BLK], w)
    x = x_ref[...].astype(f32)
    scale = lax.rsqrt(jnp.mean(x * x, axis=-1, keepdims=True) + epsilon)
    small_ref[...] += jnp.broadcast_to(jnp.sum(dn1 * x * scale, axis=0, keepdims=True), (8, width))
    weighted = dn1 * gain_ref[...]
    along = jnp.mean(weighted * x, axis=-1, keepdims=True)
    out = dresid_ref[...] + scale * weighted - x * (scale * scale * scale * along)
    out_ref[...] = out.astype(bf16)


def input_grad_call(dqkv, w_in, x, dresid, gain, rows, n):
    tokens, width = x.shape
    tile = pl.BlockSpec((TILE, width), lambda i: (i, 0))
    return pl.pallas_call(
        functools.partial(input_grad_kernel, rows, n),
        grid=(tokens // TILE,),
        in_specs=[
            pl.BlockSpec((TILE, n * BLK), lambda i: (i, 0)),
            whole((w_in.shape[0], n * rows, BLK)),
            tile,
            tile,
            whole((1, width)),
        ],
        out_specs=[tile, pl.BlockSpec((8, width), lambda i: (0, 0))],
        out_shape=[
            jax.ShapeDtypeStruct((tokens, width), bf16),
            jax.ShapeDtypeStruct((8, width), f32),
        ],
        compiler_params=params(),
        cost_estimate=cost(2 * tokens * width * n * BLK, 2 * width * n * BLK + 12 * tokens * width),
        name="input_grad",
    )(dqkv, w_in, x, dresid, gain)


def adam_step(master, first, second, gradient, clip, decayed):
    clipped = gradient * clip
    first_new = beta_first * first + (1.0 - beta_first) * clipped
    second_new = beta_second * second + (1.0 - beta_second) * clipped * clipped
    first_hat = first_new * (1.0 / (1.0 - beta_first**STEP))
    second_hat = second_new * (1.0 / (1.0 - beta_second**STEP))
    change = first_hat / (jnp.sqrt(second_hat) + adam_floor) + decayed * weight_decay * master
    update = -learn_rate * change
    return (gradient, update, first_new, second_new)


def adam_kernel(scale, clip_ref, g_ref, master_ref, first_ref, second_ref, *outs):
    gradient = g_ref[...].astype(f32) * scale
    results = adam_step(master_ref[...], first_ref[...], second_ref[...], gradient, clip_ref[0], 1.0)
    for out, result in zip(outs, results):
        out[...] = result


def adam_call(clip, packed, at, master, first, second, scale, name):
    rows, cols = master.shape
    natural = pl.BlockSpec((rows, BLK), lambda j, _: (0, j))
    shape = jax.ShapeDtypeStruct(master.shape, f32)
    return pl.pallas_call(
        functools.partial(adam_kernel, scale),
        grid_spec=pltpu.PrefetchScalarGridSpec(
            num_scalar_prefetch=1,
            grid=(cols // BLK,),
            in_specs=[pl.BlockSpec((rows, BLK), lambda j, _: (at // rows + j, 0)), natural, natural, natural],
            out_specs=[natural] * 4,
        ),
        out_shape=[shape] * 4,
        compiler_params=params(),
        cost_estimate=cost(20 * master.size, 30 * master.size),
        name=name,
    )(clip, packed, master, first, second)


def adam_experts_kernel(scale, clip_ref, g0_ref, g1_ref, g2_ref, master_ref, first_ref, second_ref, *outs):
    for e, g_ref in enumerate((g0_ref, g1_ref, g2_ref)):

        @pl.when(pl.program_id(0) == e)
        def _():
            gradient = g_ref[...].astype(f32) * scale
            results = adam_step(master_ref[0], first_ref[0], second_ref[0], gradient, clip_ref[0], 1.0)
            for out, result in zip(outs, results):
                out[0] = result


def adam_experts_call(clip, packed, at, master, first, second, scale, name):
    _, rows, cols = master.shape
    n = cols // BLK
    natural = pl.BlockSpec((1, rows, BLK), lambda e, j, _: (e, 0, j))
    shape = jax.ShapeDtypeStruct(master.shape, f32)

    def g_spec(own):
        return pl.BlockSpec(
            (rows, BLK), lambda e, j, _: (at // rows + jnp.where(e < own, 0, jnp.where(e > own, n - 1, j)), 0)
        )

    return pl.pallas_call(
        functools.partial(adam_experts_kernel, scale),
        grid_spec=pltpu.PrefetchScalarGridSpec(
            num_scalar_prefetch=1,
            grid=(E, n),
            in_specs=[g_spec(e) for e in range(E)] + [natural] * 3,
            out_specs=[natural] * 4,
        ),
        out_shape=[shape] * 4,
        compiler_params=params(),
        cost_estimate=cost(20 * master.size, 30 * master.size),
        name=name,
    )(clip, *packed, master, first, second)


def per_device(
    tokens,
    cotangent,
    lengths,
    routes,
    slot_index,
    norm_gains,
    norm_first,
    norm_second,
    in_proj,
    in_first,
    in_second,
    out_proj,
    out_first,
    out_second,
    router,
    router_first,
    router_second,
    up_proj,
    up_first,
    up_second,
    down_proj,
    down_first,
    down_second,
):
    n_rep, n_f = lax.axis_size("replica"), lax.axis_size("fsdp")
    n_z = n_f // 2
    n_mb, n_local, seq, width = tokens.shape
    n_seq = n_mb * n_local
    total_tokens = n_seq * seq
    unit = 16 * n_rep
    rows = in_proj.shape[0]
    down_rows = down_proj.shape[1]
    n_in, n_out, n_up, n_down = (w.shape[-1] // BLK for w in (in_proj, out_proj, up_proj, down_proj))
    core = (lax.axis_index("fsdp") % 2).astype(jnp.int32)[None]

    smalls = jnp.concatenate([norm_gains.astype(bf16), router.astype(bf16).T], axis=0)
    n_small = round_up(smalls.size, BLK) // BLK
    smalls = jnp.pad(smalls.reshape(-1), (0, 16 * BLK - smalls.size)).reshape(16, BLK)
    in_shard = pack_call([(in_proj, None)], unit, smalls)
    out_shard = pack_call([(out_proj, None)], unit)
    early_shard = pack_call([(up_proj, 0), (down_proj, 0)], unit)
    late_shard = pack_call([(w, e) for e in range(1, E) for w in (up_proj, down_proj)], unit)
    e_rows = n_up * rows + n_down * down_rows

    w_in = gather_packed(in_shard, 0)
    w_out = gather_packed(out_shard, 1)
    w_early = gather_packed(early_shard, 0)
    w_late = gather_packed(late_shard, 1)

    small_all = w_in[:, n_in * rows : n_in * rows + n_small, :].reshape(n_f, n_small * BLK)[:, : 5 * rows]
    small_all = small_all.reshape(n_f, 5, rows).transpose(1, 0, 2).reshape(5, width)
    gain_one = small_all[0:1].astype(f32)
    gain_two = small_all[1:2].astype(f32)
    router8 = pad_rows(small_all[2:5], 8)

    length = lengths.reshape(n_seq).astype(jnp.int32)
    route = routes.reshape(n_seq, seq, 2)
    slot = slot_index.reshape(n_seq, seq, 2)
    live = jnp.arange(seq)[None, :] < length[:, None]
    kept = live[:, :, None] & (slot < CAP)
    slot_of = [
        jnp.max(jnp.where(kept & (route == e), slot, -1), axis=-1) for e in range(E)
    ]
    slot_rows = jnp.stack(slot_of + [live.astype(jnp.int32)] + [jnp.full_like(slot_of[0], -1)] * 4, axis=1)
    slot_cols = slot_rows.transpose(0, 2, 1).reshape(total_tokens, 8)

    x = tokens.reshape(total_tokens, width)
    cot = cotangent.reshape(total_tokens, width)

    qkv, n1 = qkv_call(x, gain_one, w_in, rows, n_in)
    probs, mixed = attention_call(length, qkv, n_seq)
    resid, n2, prob = resid_call(mixed, w_out, x, gain_two, router8, rows, n_out)
    buf, dys, gates = dispatch_call(slot_rows, prob, n2, cot, n_seq)

    ys, dbufs, dgates, sums = [], [], [], []
    for e in range(E):
        w, at = (w_early, 0) if e == 0 else (w_late, (e - 1) * e_rows)
        y, dbuf, dgate, keep, send = expert_call(
            e, at, core, buf, dys, gates, slot_rows, w, rows, down_rows, unit
        )
        ys.append(y)
        dbufs.append(dbuf)
        dgates.append(dgate.reshape(1, total_tokens))
        sums.append(reduce_packed(keep, send, e))
    dprob = pad_rows(jnp.concatenate(dgates, axis=0), 8)
    block_out = combine_call(slot_cols, resid, ys, n_seq)

    dresid, dattn, dmixed, small_two = middle_call(
        slot_cols, dbufs, prob, dprob, router8, n2, resid, cot, gain_two, w_out, rows, n_out, n_seq
    )

    def reduce_one(keep, send, first):
        n = keep.shape[1]
        extra = round_up(n, unit) - n
        if extra:
            keep = jnp.pad(keep, ((0, 0), (0, extra), (0, 0)))
            send = jnp.pad(send, ((0, 0), (0, extra), (0, 0)))
        return reduce_packed(keep, send, first)

    out_sum = reduce_one(*weight_grad_call(core, mixed, dattn, rows, n_z, "out_grad"), 1)
    dq, dk, dv = attention_back_call(qkv, probs, mixed, dmixed, n_seq)
    dqkv = jnp.concatenate([dq, dk, dv], axis=1)
    in_sum = reduce_one(*weight_grad_call(core, n1, dqkv, rows, n_z, "in_grad"), 0)
    input_grad, small_one = input_grad_call(dqkv, w_in, x, dresid, gain_one, rows, n_in)

    grad_scale = 1.0 / (n_seq * n_rep * n_f)
    small_sum = sum_all(jnp.concatenate([small_one[:1], small_two[8:9], small_two[:E]], axis=0)) * grad_scale
    at = lax.axis_index("fsdp") * rows
    small_mine = lax.dynamic_slice_in_dim(small_sum, at, rows, axis=1)
    def square(packed):
        values = packed.astype(f32) * grad_scale
        return jnp.sum(values * values)

    at_down = n_up * rows
    late = sum_small(jnp.stack([square(in_sum[: n_in * rows])]))
    early = sum_small(
        jnp.stack(
            [
                square(out_sum[: n_out * rows]),
                sum(square(s[:at_down]) for s in sums),
                sum(square(s[at_down:e_rows]) for s in sums),
            ]
        )
    )
    totals = (
        jnp.sum(small_sum[:2] * small_sum[:2]),
        late[0],
        early[0],
        jnp.sum(small_sum[2:] * small_sum[2:]),
        early[1],
        early[2],
    )
    weights = (norm_gains, in_proj, out_proj, router, up_proj, down_proj)
    counts = (2 * width,) + tuple(w.size * n_f for w in weights[1:])
    rms = [jnp.sqrt(t / float(n) + epsilon) for t, n in zip(totals, counts)]
    clips = [jnp.minimum(1.0, clip_level / r)[None] for r in rms]
    norm_res = adam_step(norm_gains, norm_first, norm_second, small_mine[:2], clips[0], 0.0)
    in_res = adam_call(clips[1], in_sum, 0, in_proj, in_first, in_second, grad_scale, "in_adam")
    out_res = adam_call(clips[2], out_sum, 0, out_proj, out_first, out_second, grad_scale, "out_adam")
    router_res = adam_step(router, router_first, router_second, small_mine[2:].T, clips[3], 1.0)
    up_res = adam_experts_call(clips[4], sums, 0, up_proj, up_first, up_second, grad_scale, "up_adam")
    down_res = adam_experts_call(
        clips[5], sums, at_down, down_proj, down_first, down_second, grad_scale, "down_adam"
    )
    return (
        block_out.reshape(tokens.shape),
        input_grad.reshape(tokens.shape),
        jnp.stack(rms[:5]),
        jnp.stack(rms[5:]),
        *norm_res,
        *in_res,
        *out_res,
        *router_res,
        *up_res,
        *down_res,
    )


def solution(mesh):
    data = P(None, ("replica", "fsdp"), None, None)
    gains = P(None, "fsdp")
    flat = P("fsdp", None)
    experts = P(None, "fsdp", None)
    return jax.shard_map(
        per_device,
        mesh=mesh,
        in_specs=(data, data, P(None, ("replica", "fsdp")), data, data)
        + (gains,) * 3
        + (flat,) * 9
        + (experts,) * 6,
        out_specs=(data, data, P(), P()) + (gains,) * 4 + (flat,) * 12 + (experts,) * 8,
        check_vma=False,
    )
```

```python
import functools

import jax
import jax.numpy as jnp
from jax import lax
from jax.experimental import pallas as pl
from jax.experimental.pallas import tpu as pltpu
from jax.sharding import PartitionSpec as P

QUERY_HEADS = 24
KEY_VALUE_HEADS = 8
HEAD_SIZE = 64
FE = 1024
E = 3
STEP = 10
CAP = 320
BLK = 512

epsilon = 1e-06
beta_first = 0.9
beta_second = 0.95
learn_rate = 0.02
weight_decay = 0.1
adam_floor = 1e-08
clip_level = 0.005

bf16 = jnp.bfloat16
f32 = jnp.float32

LAST = (((1,), (1,)), ((), ()))
FIRST = (((0,), (0,)), ((), ()))


def dot(a, b):
    return jnp.dot(a, b, preferred_element_type=f32)


def dot_last(a, b):
    return lax.dot_general(a, b, LAST, preferred_element_type=f32)


def dot_first(a, b):
    return lax.dot_general(a, b, FIRST, preferred_element_type=f32)


def params(mib=56):
    return pltpu.CompilerParams(vmem_limit_bytes=mib * 1024 * 1024)


def cost(flops, nbytes):
    return pl.CostEstimate(flops=int(flops) // 1000000000, bytes_accessed=int(nbytes) // 1000000, transcendentals=0)


def whole(shape, space=None):
    zeros = (0,) * len(shape)
    return pl.BlockSpec(shape, lambda *_: zeros, pipeline_mode=pl.Buffered(1))


def hold(values, after):
    if not after:
        return values
    return lax.optimization_barrier((values, list(after)))[0]


def kernel_call(
    kernel, args, *, grid, in_specs, out_specs, out_shape, name, cost_estimate, prefetch=0, scratch=(), after=(), mib=56, aliases=None
):
    args = list(args)
    args[0] = hold(args[0], after)
    return pl.pallas_call(
        kernel,
        grid_spec=pltpu.PrefetchScalarGridSpec(
            num_scalar_prefetch=prefetch,
            grid=grid,
            in_specs=list(in_specs),
            out_specs=out_specs,
            scratch_shapes=list(scratch),
        ),
        out_shape=out_shape,
        compiler_params=params(mib),
        cost_estimate=cost_estimate,
        input_output_aliases=aliases or {},
        name=name,
    )(*args)


def round_up(n, m):
    return -(-n // m) * m


def shift_core_pairs(x, k):
    size = lax.axis_size("fsdp")
    return lax.ppermute(x, "fsdp", [(i, (i + 2 * k) % size) for i in range(size)])


def core_groups():
    size = lax.axis_size("fsdp")
    return [list(range(c, size, 2)) for c in range(2)]


def swap_core(x):
    size = lax.axis_size("fsdp")
    return lax.ppermute(x, "fsdp", [(i, i ^ 1) for i in range(size)])


def swap_replica(x, bit):
    size = lax.axis_size("replica")
    return lax.ppermute(x, "replica", [(i, i ^ bit) for i in range(size)])


def bit_order(first):
    bits = []
    while (1 << len(bits)) < lax.axis_size("replica"):
        bits.append(1 << len(bits))
    return bits[first % len(bits) :] + bits[: first % len(bits)]


def stack_kernel(cuts, n_z, z_ref, *refs):
    pieces, outs = refs[: -len(cuts)], refs[-len(cuts) :]
    for (at, size), out in zip(cuts, outs):
        for k in range(1, n_z):
            if len(pieces) > 1:
                out[0, k - 1] = pieces[k - 1][at : at + size, :]
            else:
                out[0, k - 1] = pieces[0][lax.rem(z_ref[0] + n_z - k, n_z), at : at + size, :]


def assemble_kernel(masks, n_z, cuts, rows, idx_ref, *refs):
    n_in = 2 * (1 + 2 * len(cuts))
    out, sems, held = refs[n_in:]
    part, z, c = idx_ref[0], idx_ref[1], idx_ref[2]
    half = len(masks[0]) // 2
    blocks, count = [], 0
    for ins, core in ((refs[: n_in // 2], c), (refs[n_in // 2 : n_in], 1 - c)):
        for k in range(n_z):
            at_block = 2 * lax.rem(z + n_z - k, n_z) + core
            found = []
            if k == 0:
                found.append((ins[0], held.at[at_block]))
            else:
                for i, (offset, size) in enumerate(cuts):
                    for j, mask in enumerate(masks[i]):
                        at = pl.multiple_of((part ^ mask) * rows + offset, 16)
                        found.append(
                            (ins[1 + 2 * i + j // half].at[j % half, k - 1], held.at[at_block, pl.ds(at, size)])
                        )
            copies = [pltpu.make_async_copy(a, b, sems.at[count + i]) for i, (a, b) in enumerate(found)]
            count += len(copies)
            for copy in copies:
                copy.start()
            blocks.append((at_block, copies))
    written = []
    for i, (at_block, copies) in enumerate(blocks):
        for copy in copies:
            copy.wait()
        copy = pltpu.make_async_copy(held.at[at_block], out.at[at_block], sems.at[count + i])
        copy.start()
        written.append(copy)
    for copy in written:
        copy.wait()


class Gather:
    def __init__(self, shard):
        self.shard = shard
        self.n_z = lax.axis_size("fsdp") // 2
        self.rows = shard.shape[0] // lax.axis_size("replica")
        half = round_up(self.rows // 2, 16)
        self.cuts = ((0, half), (half, self.rows - half))
        self.orders = [bit_order(i) for i in range(len(self.cuts))]
        self.masks = [[0] for _ in self.cuts]

    def start(self, mine, direct):
        if direct:
            self.pieces = [shift_core_pairs(mine, k) for k in range(1, self.n_z)]
        else:
            self.pieces = [lax.all_gather(mine, "fsdp", axis_index_groups=core_groups())]

    def stack(self, after=()):
        in_specs = [pl.BlockSpec(p.shape, (lambda i, _: (0, 0, 0)) if p.ndim == 3 else (lambda i, _: (0, 0))) for p in self.pieces]
        shapes = [(1, self.n_z - 1, size, BLK) for _, size in self.cuts]
        self.stacks = kernel_call(
            functools.partial(stack_kernel, self.cuts, self.n_z),
            [(lax.axis_index("fsdp") // 2).astype(jnp.int32)[None], *self.pieces],
            prefetch=1,
            grid=(1,),
            in_specs=in_specs,
            out_specs=[pl.BlockSpec(shape, lambda i, _: (0, 0, 0, 0)) for shape in shapes],
            out_shape=[jax.ShapeDtypeStruct(shape, bf16) for shape in shapes],
            name="stack",
            cost_estimate=cost(0, 4 * self.rows * BLK * (self.n_z - 1)),
            after=after,
        )
        self.swap(0)

    def swap(self, step):
        self.received = [swap_replica(x, order[step]) for x, order in zip(self.stacks, self.orders)]
        self.masks = [m + [v ^ order[step] for v in m] for m, order in zip(self.masks, self.orders)]

    def double(self, after=()):
        for step in range(1, len(self.orders[0])):
            arrived = hold(self.received, after)
            self.stacks = [jnp.concatenate(pair) for pair in zip(self.stacks, arrived)]
            self.swap(step)

    def swap_early(self):
        self.own_c = swap_core(self.shard)
        self.low_c = [swap_core(x) for x in self.stacks]

    def settle(self, after):
        self.received, self.own_c, self.low_c = hold((self.received, self.own_c, self.low_c), after)

    def assemble(self, after=()):
        place = lax.axis_index("fsdp")
        idx = jnp.stack([lax.axis_index("replica"), place // 2, place % 2]).astype(jnp.int32)
        ins = [self.shard]
        other = [self.own_c]
        high_c = [swap_core(x) for x in self.received]
        for pair in zip(self.stacks, self.received):
            ins += pair
        for pair in zip(self.low_c, high_c):
            other += pair
        n_f = lax.axis_size("fsdp")
        n_copies = 2 * (1 + len(self.cuts) * len(self.masks[0]) * (self.n_z - 1))
        anyspec = pl.BlockSpec(memory_space=pl.ANY)
        return kernel_call(
            functools.partial(assemble_kernel, self.masks, self.n_z, self.cuts, self.rows),
            [idx, *ins, *other],
            prefetch=1,
            grid=(1,),
            in_specs=[anyspec] * (2 * len(ins)),
            out_specs=anyspec,
            out_shape=jax.ShapeDtypeStruct((n_f,) + self.shard.shape, bf16),
            scratch=[
                pltpu.SemaphoreType.DMA((n_copies + n_f,)),
                pltpu.VMEM((n_f,) + self.shard.shape, bf16),
            ],
            name="assemble",
            cost_estimate=cost(0, 4 * n_f * self.shard.size),
            after=after,
        )


class Reduce:
    def __init__(self, keep, received, first=0):
        n_rep, self.n_z = lax.axis_size("replica"), lax.axis_size("fsdp") // 2
        self.part, self.z = lax.axis_index("replica"), lax.axis_index("fsdp") // 2
        self.rows = keep.shape[1] // n_rep
        n_bits = len(bit_order(0))
        self.bits = [1 << b for b in range(n_bits)]
        self.order = bit_order(first)
        shape = (self.n_z,) + (2,) * n_bits + (self.rows, BLK)
        half = round_up(self.rows // 2, 16)
        self.cuts = ((0, half), (half, self.rows - half))
        self.orders = [bit_order(i) for i in range(len(self.cuts))]
        self.live = [list(reversed(self.bits)) for _ in self.cuts]
        self.terms = [[keep.reshape(shape)] for _ in self.cuts]
        self.newest = [received.reshape(shape)]
        halves = [functools.partial(self.halve, i) for i in range(n_bits)]
        gathers = [functools.partial(self.gather, i, bit) for i, bit in enumerate(self.order)]
        self.todo = [halves[:1], halves[1:], [self.along], gathers[:1], gathers[1:]]

    def step(self, after=()):
        self.newest = hold(self.newest, after)
        for action in self.todo.pop(0):
            sent = action()
        return sent

    def part_sum(self, terms):
        return functools.reduce(jnp.add, [t.astype(f32) for t in terms])

    def halve(self, i):
        news, marks = [], []
        for p, (at, size) in enumerate(self.cuts):
            self.terms[p] = self.terms[p] + [self.newest[p % len(self.newest)]]
            bit = self.orders[p][i]
            axis = 1 + self.live[p].index(bit)
            self.live[p].remove(bit)
            own = (self.part // bit) % 2

            def take(t, index):
                starts, sizes = [0] * t.ndim, list(t.shape)
                starts[axis], sizes[axis] = index, 1
                if i == 0:
                    starts[-2], sizes[-2] = at, size
                out = lax.dynamic_slice(t, starts, sizes)
                return out.reshape(out.shape[:axis] + out.shape[axis + 1 :])

            away = self.part_sum([take(t, 1 - own) for t in self.terms[p]]).astype(bf16)
            self.terms[p] = [take(t, own) for t in self.terms[p]]
            news.append(swap_replica(away, bit))
            marks.append(away)
        self.newest = news
        return marks

    def at_place(self, z):
        parts = [
            self.part_sum([lax.dynamic_index_in_dim(t, z, 0, keepdims=False) for t in terms]) for terms in self.terms
        ]
        return jnp.concatenate(parts)

    def along(self):
        self.terms = [terms + [new] for terms, new in zip(self.terms, self.newest)]
        aways = [self.at_place((self.z + k) % self.n_z).astype(bf16) for k in range(1, self.n_z)]
        self.newest = [shift_core_pairs(away, k) for k, away in enumerate(aways, 1)]
        return aways

    def gather(self, i, bit):
        if i == 0:
            summed = self.at_place(self.z)
            for got in self.newest:
                summed = summed + got.astype(f32)
            self.have = summed.astype(bf16)
        else:
            self.have = self.joined()
        self.newest, self.bit = [swap_replica(self.have, bit)], bit
        return [self.have]

    def joined(self):
        pair = jnp.stack([self.have, self.newest[0]])
        return jnp.where((self.part // self.bit) % 2 == 1, pair[::-1], pair)

    def result(self, after=()):
        self.newest = hold(self.newest, after)
        stack = self.joined()
        names = list(reversed(self.order))
        n_bits = len(names)
        stack = jnp.transpose(stack, tuple(names.index(b) for b in reversed(self.bits)) + (n_bits, n_bits + 1))
        return stack.reshape(-1, BLK)


def pair_sum(keep, got):
    return (keep.astype(f32) + got.astype(f32)).astype(bf16)


def sum_small(x):
    size = lax.axis_size("fsdp")
    bit = 1
    while bit < size:
        x = x + lax.ppermute(x, "fsdp", [(i, i ^ bit) for i in range(size)])
        bit *= 2
    return x


def pack_kernel(counts, has_extra, has_before, prefix_ref, *refs):
    n = len(counts) + has_extra + has_before
    out = refs[n]
    at = 0
    for ref, count in zip(refs, counts):
        value = ref[0] if len(ref.shape) == 3 else ref[...]
        for j in range(count):
            out[at : at + value.shape[0], :] = value[:, j * BLK : (j + 1) * BLK].astype(bf16)
            at += value.shape[0]
    if has_extra:
        extra = refs[len(counts)][...]
        out[at : at + extra.shape[0], :] = extra
        at += extra.shape[0]
    if at < out.shape[0]:
        out[at:, :] = jnp.zeros((out.shape[0] - at, BLK), bf16)
    mine = refs[n + 1]
    rows = mine.shape[0]
    mine[...] = out[pl.ds(pl.multiple_of(prefix_ref[0] * rows, 16), rows), :]
    if has_before:
        refs[n + 2][...] = refs[n - 1][...]


def pack_call(parts, unit, extra=None, before=None, after=()):
    specs, counts, total = [], [], 0
    for w, e in parts:
        if e is None:
            specs.append(pl.BlockSpec(w.shape, lambda i, _: (0, 0)))
        else:
            specs.append(pl.BlockSpec((1,) + w.shape[1:], lambda i, _, e=e: (e, 0, 0)))
        counts.append(w.shape[-1] // BLK)
        total += counts[-1] * w.shape[-2]
    part = lax.axis_index("replica").astype(jnp.int32)[None]
    args = [part] + [w for w, _ in parts]
    if extra is not None:
        args.append(extra)
        specs.append(pl.BlockSpec(extra.shape, lambda i, _: (0, 0)))
        total += extra.shape[0]
    total = round_up(total, unit)
    n_rep = lax.axis_size("replica")
    shapes = [(total, BLK), (total // n_rep, BLK)]
    if before is not None:
        shapes.append((before.shape[0] // n_rep, BLK))
        args.append(before)
        specs.append(pl.BlockSpec(shapes[-1], lambda i, part: (part[0], 0)))
    return kernel_call(
        functools.partial(pack_kernel, tuple(counts), extra is not None, before is not None),
        args,
        prefetch=1,
        grid=(1,),
        in_specs=specs,
        out_specs=[pl.BlockSpec(shape, lambda i, _: (0, 0)) for shape in shapes],
        out_shape=[jax.ShapeDtypeStruct(shape, bf16) for shape in shapes],
        cost_estimate=cost(0, 6 * total * BLK),
        name="pack",
        after=after,
    )


def pad_rows(x, rows):
    return jnp.pad(x, ((0, rows - x.shape[0]), (0, 0)))


def qkv_kernel(x_ref, gain_ref, w_ref, qkv_ref, n1_ref):
    tokens, width = x_ref.shape

    @pl.when(pl.program_id(0) == 0)
    def _():
        def body(i, _):
            rows = pl.ds(pl.multiple_of(i * 128, 128), 128)
            xf = x_ref[rows, :].astype(f32)
            scale = lax.rsqrt(jnp.mean(xf * xf, axis=-1, keepdims=True) + epsilon)
            n1_ref[rows, :] = (xf * scale * gain_ref[...]).astype(bf16)
            return 0

        lax.fori_loop(0, tokens // 128, body, 0)

    w = w_ref[...].reshape(width, BLK)

    def body(i, _):
        rows = pl.ds(pl.multiple_of(i * 256, 256), 256)
        qkv_ref[rows, :] = dot(n1_ref[rows, :], w).astype(bf16)
        return 0

    lax.fori_loop(0, tokens // 256, body, 0)


def qkv_call(x, gain, w_in, rows, n, after=()):
    tokens, width = x.shape
    n_f = w_in.shape[0]
    return kernel_call(
        qkv_kernel,
        [x, gain, w_in],
        grid=(n,),
        in_specs=[
            whole((tokens, width)),
            whole((1, width)),
            pl.BlockSpec((n_f, rows, BLK), lambda j: (0, j, 0)),
        ],
        out_specs=[
            pl.BlockSpec((tokens, BLK), lambda j: (0, j)),
            pl.BlockSpec((tokens, width), lambda j: (0, 0)),
        ],
        out_shape=[
            jax.ShapeDtypeStruct((tokens, n * BLK), bf16),
            jax.ShapeDtypeStruct((tokens, width), bf16),
        ],
        cost_estimate=cost(2 * tokens * width * n * BLK, 2 * width * n * BLK + 4 * tokens * width),
        name="qkv",
        after=after,
    )


HALF = 256


def attention_kernel(len_ref, q_ref, k_ref, v_ref, p_ref, mix_ref):
    seq = q_ref.shape[0]
    length = len_ref[pl.program_id(0)]
    key = lax.broadcasted_iota(jnp.int32, (seq, seq), 0)
    query = lax.broadcasted_iota(jnp.int32, (seq, seq), 1)
    bias = jnp.where((key <= query) & (key < length), 0.0, -1000000000.0).astype(f32)
    group = QUERY_HEADS // KEY_VALUE_HEADS
    for h in range(2 * group):
        g = h // group
        lanes = slice(h * HEAD_SIZE, (h + 1) * HEAD_SIZE)
        kv = slice(g * HEAD_SIZE, (g + 1) * HEAD_SIZE)
        q = q_ref[:, lanes] * jnp.asarray(HEAD_SIZE ** (-0.5), bf16)
        for start in range(0, seq, HALF):
            stop = start + HALF
            s = dot_last(k_ref[:stop, kv], q[start:stop]) + bias[:stop, start:stop]
            raised = jnp.exp(s - jnp.max(s, axis=0, keepdims=True))
            probs = (raised * (1.0 / jnp.sum(raised, axis=0, keepdims=True))).astype(bf16)
            p_ref[0, h, :stop, start:stop] = probs
            if stop < seq:
                p_ref[0, h, stop:, start:stop] = jnp.zeros((seq - stop, HALF), bf16)
            mixed = dot_first(v_ref[:stop, kv], probs)
            mix_ref[start:stop, lanes] = mixed.T.astype(bf16)


def attention_call(lengths, qkv, n_seq, after=()):
    tokens = qkv.shape[0]
    seq = tokens // n_seq
    pairs = KEY_VALUE_HEADS // 2
    heads = QUERY_HEADS // pairs
    qw = heads * HEAD_SIZE
    kw = 2 * HEAD_SIZE
    k_at = QUERY_HEADS * HEAD_SIZE // kw
    v_at = k_at + pairs
    return kernel_call(
        attention_kernel,
        [lengths, qkv, qkv, qkv],
            prefetch=1,
            grid=(n_seq, pairs),
            in_specs=[
                pl.BlockSpec((seq, qw), lambda s, j, _: (s, j)),
                pl.BlockSpec((seq, kw), lambda s, j, _: (s, k_at + j)),
                pl.BlockSpec((seq, kw), lambda s, j, _: (s, v_at + j)),
            ],
            out_specs=[
                pl.BlockSpec((1, heads, seq, seq), lambda s, j, _: (s, j, 0, 0)),
                pl.BlockSpec((seq, qw), lambda s, j, _: (s, j)),
            ],
        out_shape=[
            jax.ShapeDtypeStruct((n_seq, QUERY_HEADS, seq, seq), bf16),
            jax.ShapeDtypeStruct((tokens, QUERY_HEADS * HEAD_SIZE), bf16),
        ],
        cost_estimate=cost(16 * n_seq * QUERY_HEADS * seq * seq * HEAD_SIZE, 2 * n_seq * QUERY_HEADS * seq * seq),
        name="attention",
        after=after,
    )


def attention_back_kernel(q_ref, k_ref, v_ref, p_ref, mix_ref, dmix_ref, dq_ref, dk_ref, dv_ref):
    seq = q_ref.shape[0]
    group = QUERY_HEADS // KEY_VALUE_HEADS
    scale = HEAD_SIZE ** (-0.5)
    ones = jnp.ones((8, HEAD_SIZE), bf16)
    for g in range(2):
        kv = slice(g * HEAD_SIZE, (g + 1) * HEAD_SIZE)
        k, v = k_ref[:, kv], v_ref[:, kv]
        n_half = seq // HALF
        dk = [jnp.zeros((HALF, HEAD_SIZE), f32) for _ in range(n_half)]
        dv = [jnp.zeros((HALF, HEAD_SIZE), f32) for _ in range(n_half)]
        for i in range(group):
            h = g * group + i
            lanes = slice(h * HEAD_SIZE, (h + 1) * HEAD_SIZE)
            for start in range(0, seq, HALF):
                stop = start + HALF
                dmix = dmix_ref[start:stop, lanes]
                q = q_ref[start:stop, lanes]
                both = dmix.astype(f32) * mix_ref[start:stop, lanes].astype(f32)
                high = both.astype(bf16)
                low = (both - high.astype(f32)).astype(bf16)
                delta = (dot_last(ones, high) + dot_last(ones, low))[:1]
                probs = p_ref[0, h, :stop, start:stop]
                dp = dot_last(v[:stop], dmix)
                ds = (probs.astype(f32) * (dp - delta)).astype(bf16)
                dq = dot_first(k[:stop], ds)
                dq_ref[start:stop, lanes] = (dq.T * scale).astype(bf16)
                dk_part = dot(ds, q)
                dv_part = dot(probs, dmix)
                for m in range(stop // HALF):
                    rows = slice(m * HALF, (m + 1) * HALF)
                    dk[m] += dk_part[rows]
                    dv[m] += dv_part[rows]
        for m in range(n_half):
            rows = slice(m * HALF, (m + 1) * HALF)
            dk_ref[rows, kv] = (dk[m] * scale).astype(bf16)
            dv_ref[rows, kv] = dv[m].astype(bf16)


def attention_back_call(qkv, probs, mixed, dmixed, n_seq, after=()):
    tokens = qkv.shape[0]
    seq = tokens // n_seq
    pairs = KEY_VALUE_HEADS // 2
    heads = QUERY_HEADS // pairs
    qw = heads * HEAD_SIZE
    kw = 2 * HEAD_SIZE
    k_at = QUERY_HEADS * HEAD_SIZE // kw
    v_at = k_at + pairs
    qspec = pl.BlockSpec((seq, qw), lambda s, j: (s, j))
    kspec = pl.BlockSpec((seq, kw), lambda s, j: (s, j))
    return kernel_call(
        attention_back_kernel,
        [qkv, qkv, qkv, probs, mixed, dmixed],
        grid=(n_seq, pairs),
        in_specs=[
            qspec,
            pl.BlockSpec((seq, kw), lambda s, j: (s, k_at + j)),
            pl.BlockSpec((seq, kw), lambda s, j: (s, v_at + j)),
            pl.BlockSpec((1, heads, seq, seq), lambda s, j: (s, j, 0, 0)),
            qspec,
            qspec,
        ],
        out_specs=[qspec, kspec, kspec],
        out_shape=[
            jax.ShapeDtypeStruct((tokens, QUERY_HEADS * HEAD_SIZE), bf16),
            jax.ShapeDtypeStruct((tokens, KEY_VALUE_HEADS * HEAD_SIZE), bf16),
            jax.ShapeDtypeStruct((tokens, KEY_VALUE_HEADS * HEAD_SIZE), bf16),
        ],
        cost_estimate=cost(32 * n_seq * QUERY_HEADS * seq * seq * HEAD_SIZE, 2 * n_seq * QUERY_HEADS * seq * seq),
        name="attention_back",
        after=after,
    )


TILE = 256


def resid_kernel(rows, n, mix_ref, w_ref, x_ref, gain_ref, router_ref, resid_ref, n2_ref, prob_ref):
    width = x_ref.shape[1]
    mixed = mix_ref[...]
    squares = jnp.zeros((TILE, 1), f32)
    for j in range(n):
        cols = slice(j * BLK, (j + 1) * BLK)
        w = w_ref[:, j * rows : (j + 1) * rows, :].reshape(-1, BLK)
        part = x_ref[:, cols].astype(f32) + dot(mixed, w)
        resid_ref[:, cols] = part
        squares += jnp.sum(part * part, axis=-1, keepdims=True)
    scale = lax.rsqrt(squares * (1.0 / width) + epsilon)
    n2 = (resid_ref[...] * scale * gain_ref[...]).astype(bf16)
    n2_ref[...] = n2
    logits = dot_last(router_ref[...], n2)
    logits = jnp.where(lax.broadcasted_iota(jnp.int32, logits.shape, 0) < E, logits, -1e30)
    raised = jnp.exp(logits - jnp.max(logits, axis=0, keepdims=True))
    prob_ref[...] = raised / jnp.sum(raised, axis=0, keepdims=True)


def resid_call(mixed, w_out, at, x, gain, router, rows, n, after=()):
    tokens, width = x.shape
    tile = pl.BlockSpec((TILE, width), lambda i: (i, 0))
    return kernel_call(
        functools.partial(resid_kernel, rows, n),
        [mixed, w_out, x, gain, router],
        grid=(tokens // TILE,),
        in_specs=[
            tile,
            pl.BlockSpec((w_out.shape[0], n * rows, BLK), lambda i: (0, at, 0), pipeline_mode=pl.Buffered(1)),
            tile,
            whole((1, width)),
            whole((8, width)),
        ],
        out_specs=[tile, tile, pl.BlockSpec((8, TILE), lambda i: (0, i))],
        out_shape=[
            jax.ShapeDtypeStruct((tokens, width), f32),
            jax.ShapeDtypeStruct((tokens, width), bf16),
            jax.ShapeDtypeStruct((8, tokens), f32),
        ],
        cost_estimate=cost(2 * tokens * width * width, 2 * width * width + 12 * tokens * width),
        name="resid",
        after=after,
    )


def dispatch_kernel(slot_ref, prob_ref, n2_ref, cot_ref, buf_ref, dys_ref, gate_ref):
    e = pl.program_id(1)
    slots = slot_ref[0, pl.ds(e, 1), :]
    hit = lax.broadcasted_iota(jnp.int32, (CAP, slots.shape[1]), 0) == slots
    gate = jnp.sum(jnp.where(hit, prob_ref[pl.ds(e, 1), :], 0.0), axis=-1, keepdims=True)
    gate_ref[0, 0] = jnp.broadcast_to(gate, (CAP, 128))
    hit = jnp.where(hit, 1.0, 0.0).astype(bf16)
    buf_ref[0, 0] = dot(hit, n2_ref[...]).astype(bf16)
    dys_ref[0, 0] = dot(hit, cot_ref[...]).astype(bf16)


def dispatch_call(slots, prob, n2, cot, n_seq, after=()):
    tokens, width = n2.shape
    seq = tokens // n_seq
    out = pl.BlockSpec((1, 1, CAP, width), lambda s, e: (e, s, 0, 0))
    return kernel_call(
        dispatch_kernel,
        [slots, prob, n2, cot],
        grid=(n_seq, E),
        in_specs=[
            pl.BlockSpec((1, 8, seq), lambda s, e: (s, 0, 0)),
            pl.BlockSpec((8, seq), lambda s, e: (0, s)),
            pl.BlockSpec((seq, width), lambda s, e: (s, 0)),
            pl.BlockSpec((seq, width), lambda s, e: (s, 0)),
        ],
        out_specs=[out, out, pl.BlockSpec((1, 1, CAP, 128), lambda s, e: (e, s, 0, 0))],
        out_shape=[
            jax.ShapeDtypeStruct((E, n_seq, CAP, width), bf16),
            jax.ShapeDtypeStruct((E, n_seq, CAP, width), bf16),
            jax.ShapeDtypeStruct((E, n_seq, CAP, 128), f32),
        ],
        cost_estimate=cost(4 * E * CAP * tokens * width, 20 * tokens * width),
        name="dispatch",
        after=after,
    )


def split_cores(block, c, rows):
    parts = block.reshape(-1, 2, rows, block.shape[-1])
    even, odd = parts[:, 0], parts[:, 1]
    return (
        jnp.where(c == 0, even, odd).astype(bf16),
        jnp.where(c == 0, odd, even).astype(bf16),
    )


def expert_kernel(
    e,
    up_rows,
    down_rows,
    idx_ref,
    buf_ref,
    dys_ref,
    gate_ref,
    slot_ref,
    up_a_ref,
    up_b_ref,
    down_ref,
    yg_ref,
    dbuf_ref,
    dgate_ref,
    keep_ref,
    send_ref,
    y_acc,
    d_acc,
    dyexp_ref,
    hid_ref,
    da_ref,
    db_ref,
    dg_acc,
    up_held,
    down_held,
    sems,
):
    h = pl.program_id(0)
    last = pl.num_programs(0) - 1
    c = idx_ref[0]
    n_seq = buf_ref.shape[1]
    width = buf_ref.shape[3]
    n_d = width // BLK
    up_a = up_a_ref[...].reshape(width, BLK)
    up_b = up_b_ref[...].reshape(width, BLK)
    downs = [down_ref[:, j * down_rows : (j + 1) * down_rows, :].reshape(BLK, BLK) for j in range(n_d)]
    for s in range(n_seq):
        rows = slice(s * CAP, (s + 1) * CAP)
        gate = gate_ref[0, s, :, :1]

        @pl.when(h == 0)
        def _():
            dyexp_ref[rows, :] = (gate * dys_ref[0, s].astype(f32)).astype(bf16)

        x = buf_ref[0, s]
        a = dot(x, up_a)
        b = dot(x, up_b)
        sigma = jax.nn.sigmoid(a)
        silu = a * sigma
        hid = (silu * b).astype(bf16)
        hid_ref[rows, :] = hid
        du = dot_last(dys_ref[0, s, :, :BLK], downs[0])
        for j in range(1, n_d):
            du += dot_last(dys_ref[0, s, :, j * BLK : (j + 1) * BLK], downs[j])
        dg = jnp.sum(du * hid.astype(f32), axis=-1, keepdims=True)
        dh = gate * du
        da = (dh * b * sigma * (1.0 + a * (1.0 - sigma))).astype(bf16)
        db = (dh * silu).astype(bf16)
        da_ref[rows, :] = da
        db_ref[rows, :] = db

        @pl.when(h == 0)
        def _():
            dg_acc[rows, :] = jnp.broadcast_to(dg, (CAP, 128))
            for j in range(n_d):
                y_acc[rows, j * BLK : (j + 1) * BLK] = dot(hid, downs[j])
            d_acc[rows, :] = dot_last(da, up_a) + dot_last(db, up_b)

        @pl.when(h > 0)
        def _():
            dg_acc[rows, :] += jnp.broadcast_to(dg, (CAP, 128))
            for j in range(n_d):
                y_acc[rows, j * BLK : (j + 1) * BLK] += dot(hid, downs[j])
            d_acc[rows, :] += dot_last(da, up_a) + dot_last(db, up_b)

        @pl.when(h == last)
        def _():
            yg_ref[s] = (gate * y_acc[rows, :]).astype(bf16)
            dbuf_ref[s] = d_acc[rows, :].astype(bf16)
            slots = slot_ref[s, e : e + 1, :]
            hit = lax.broadcasted_iota(jnp.int32, (CAP, slots.shape[1]), 0) == slots
            row = jnp.sum(jnp.where(hit, dg_acc[rows, :1], 0.0), axis=0, keepdims=True)
            dgate_ref[s] = jnp.broadcast_to(row, (8, slots.shape[1]))

    step = 384
    per = step // (2 * up_rows)

    for m in range(width // step):
        x = jnp.concatenate([buf_ref[0, s, :, m * step : (m + 1) * step] for s in range(n_seq)], axis=0)
        xt = x.T
        for i, d_ref in enumerate((da_ref, db_ref)):
            keep, send = split_cores(dot(xt, d_ref[...]), c, up_rows)
            up_held[h, 0, i, m * per : (m + 1) * per] = keep
            up_held[h, 1, i, m * per : (m + 1) * per] = send
    hid_t = hid_ref[...].T
    for j in range(n_d):
        keep, send = split_cores(dot(hid_t, dyexp_ref[:, j * BLK : (j + 1) * BLK]), c, down_rows)
        down_held[h, 0, :, j * down_rows : (j + 1) * down_rows, :] = keep
        down_held[h, 1, :, j * down_rows : (j + 1) * down_rows, :] = send
    n_h = FE // BLK
    n_zh = keep_ref.shape[0] // n_h

    def copies(step):
        found = []
        for side, ref in enumerate((keep_ref, send_ref)):
            for i in range(2):
                place = pl.ds((i * n_h + step) * up_rows, up_rows)
                found.append((up_held.at[step, side, i], ref.at[:, place, :]))
            place = pl.ds(2 * n_h * up_rows, n_d * down_rows)
            found.append((down_held.at[step, side], ref.at[step * n_zh : (step + 1) * n_zh, place, :]))
        return [pltpu.make_async_copy(a, b, sems.at[step, i]) for i, (a, b) in enumerate(found)]

    for step in range(n_h):

        @pl.when(h == step)
        def _():
            for copy in copies(step):
                copy.start()

    @pl.when(h == last)
    def _():
        for step in range(n_h):
            for copy in copies(step):
                copy.wait()


def expert_call(e, at, core, buf, dys, gates, slots, w, up_rows, down_rows, unit, after=()):
    _, n_seq, _, width = buf.shape
    n_f = w.shape[0]
    n_z = n_f // 2
    n_h = FE // BLK
    n_d = width // BLK
    seq = slots.shape[2]
    data = pl.BlockSpec((1, n_seq, CAP, width), lambda h, _: (e, 0, 0, 0), pipeline_mode=pl.Buffered(1))
    out = pl.BlockSpec((n_seq, CAP, width), lambda h, _: (0, 0, 0))
    anyspec = pl.BlockSpec(memory_space=pl.ANY)
    total = round_up(2 * n_h * up_rows + n_d * down_rows, unit)
    grad_shape = jax.ShapeDtypeStruct((n_z, total, BLK), bf16)
    rows = n_seq * CAP
    yg, dbuf, dgate, keep, send = kernel_call(
        functools.partial(expert_kernel, e, up_rows, down_rows),
        [core, buf, dys, gates, slots, w, w, w],
            prefetch=1,
            grid=(n_h,),
            in_specs=[
                data,
                data,
                pl.BlockSpec((1, n_seq, CAP, 128), lambda h, _: (e, 0, 0, 0)),
                pl.BlockSpec((n_seq, 8, seq), lambda h, _: (0, 0, 0)),
                pl.BlockSpec((n_f, up_rows, BLK), lambda h, _: (0, at // up_rows + h, 0)),
                pl.BlockSpec((n_f, up_rows, BLK), lambda h, _: (0, at // up_rows + n_h + h, 0)),
                pl.BlockSpec(
                    (n_f // n_h, n_d * down_rows, BLK),
                    lambda h, _: (h, (at + 2 * n_h * up_rows) // (n_d * down_rows), 0),
                ),
            ],
            out_specs=[
                out,
                out,
                pl.BlockSpec((n_seq, 8, seq), lambda h, _: (0, 0, 0)),
                anyspec,
                anyspec,
            ],
            scratch=[
                pltpu.VMEM((rows, width), f32),
                pltpu.VMEM((rows, width), f32),
                pltpu.VMEM((rows, width), bf16),
                pltpu.VMEM((rows, BLK), bf16),
                pltpu.VMEM((rows, BLK), bf16),
                pltpu.VMEM((rows, BLK), bf16),
                pltpu.VMEM((rows, 128), f32),
                pltpu.VMEM((n_h, 2, 2, n_z, up_rows, BLK), bf16),
                pltpu.VMEM((n_h, 2, n_z // n_h, n_d * down_rows, BLK), bf16),
                pltpu.SemaphoreType.DMA((n_h, 6)),
            ],
        out_shape=[
            jax.ShapeDtypeStruct((n_seq, CAP, width), bf16),
            jax.ShapeDtypeStruct((n_seq, CAP, width), bf16),
            jax.ShapeDtypeStruct((n_seq, 8, seq), f32),
            grad_shape,
            grad_shape,
        ],
        mib=60,
        cost_estimate=cost(18 * rows * width * FE, 40 * width * FE),
        name="expert",
        after=after,
    )
    return yg, dbuf, dgate, keep, send


def spread(col_ref, e):
    slots = col_ref[:, e : e + 1]
    hit = lax.broadcasted_iota(jnp.int32, (col_ref.shape[0], CAP), 1) == slots
    return jnp.where(hit, 1.0, 0.0).astype(bf16)


def combine_kernel(col_ref, resid_ref, y0_ref, y1_ref, y2_ref, out_ref):
    total = resid_ref[...]
    for e, y_ref in enumerate((y0_ref, y1_ref, y2_ref)):
        total += dot(spread(col_ref, e), y_ref[0])
    out_ref[...] = jnp.where(col_ref[:, E : E + 1] > 0, total, 0.0).astype(bf16)


def combine_call(cols, resid, ys, n_seq, after=()):
    tokens, width = resid.shape
    per = tokens // n_seq // TILE
    tile = pl.BlockSpec((TILE, width), lambda i: (i, 0))
    return kernel_call(
        combine_kernel,
        [cols, resid, *ys],
        grid=(tokens // TILE,),
        in_specs=[pl.BlockSpec((TILE, 8), lambda i: (i, 0)), tile]
        + [pl.BlockSpec((1, CAP, width), lambda i: (i // per, 0, 0))] * E,
        out_specs=tile,
        out_shape=jax.ShapeDtypeStruct((tokens, width), bf16),
        cost_estimate=cost(2 * E * CAP * tokens * width, 12 * tokens * width),
        name="combine",
        after=after,
    )


def hi_lo(x):
    high = x.astype(bf16)
    return high, (x - high.astype(f32)).astype(bf16)


def middle_kernel(
    rows,
    n,
    col_ref,
    d0_ref,
    d1_ref,
    d2_ref,
    g0_ref,
    g1_ref,
    g2_ref,
    prob_ref,
    router_ref,
    n2_ref,
    resid_ref,
    cot_ref,
    gain_ref,
    w_ref,
    dresid_ref,
    dattn_ref,
    dmix_ref,
    small_ref,
):

    @pl.when(pl.program_id(0) == 0)
    def _():
        small_ref[...] = jnp.zeros_like(small_ref)

    prob = prob_ref[...]
    expert = lax.broadcasted_iota(jnp.int32, prob.shape, 0)
    dprob = jnp.zeros_like(prob)
    for e, g_ref in enumerate((g0_ref, g1_ref, g2_ref)):
        dprob = jnp.where(expert == e, g_ref[0], dprob)
    dlogit = prob * (dprob - jnp.sum(dprob * prob, axis=0, keepdims=True))
    high, low = hi_lo(dlogit)
    dn2 = dot_first(high, router_ref[...]) + dot_first(low, router_ref[...])
    for e, d_ref in enumerate((d0_ref, d1_ref, d2_ref)):
        dn2 += dot(spread(col_ref, e), d_ref[0])
    n2 = n2_ref[...]
    small_ref[...] += dot(high, n2) + dot(low, n2)
    resid = resid_ref[...]
    scale = lax.rsqrt(jnp.mean(resid * resid, axis=-1, keepdims=True) + epsilon)
    weighted = dn2 * gain_ref[...]
    along = jnp.mean(weighted * resid, axis=-1, keepdims=True)
    dy = jnp.where(col_ref[:, E : E + 1] > 0, cot_ref[...].astype(f32), 0.0)
    dresid = dy + scale * weighted - resid * (scale * scale * scale * along)
    dresid_ref[...] = dresid
    dattn = dresid.astype(bf16)
    dattn_ref[...] = dattn
    dmix = dot_last(dattn[:, :BLK], w_ref[:, :rows, :].reshape(-1, BLK))
    for j in range(1, n):
        w = w_ref[:, j * rows : (j + 1) * rows, :].reshape(-1, BLK)
        dmix += dot_last(dattn[:, j * BLK : (j + 1) * BLK], w)
    dmix_ref[...] = dmix.astype(bf16)


def middle_call(cols, ds, dgates, prob, router, n2, resid, cot, gain, w_out, at, rows, n, n_seq, after=()):
    tokens, width = resid.shape
    per = tokens // n_seq // TILE
    tile = pl.BlockSpec((TILE, width), lambda i: (i, 0))
    row8 = pl.BlockSpec((8, TILE), lambda i: (0, i))
    return kernel_call(
        functools.partial(middle_kernel, rows, n),
        [cols, *ds, *dgates, prob, router, n2, resid, cot, gain, w_out],
        grid=(tokens // TILE,),
        in_specs=[pl.BlockSpec((TILE, 8), lambda i: (i, 0))]
        + [pl.BlockSpec((1, CAP, width), lambda i: (i // per, 0, 0))] * E
        + [pl.BlockSpec((1, 8, TILE), lambda i: (i // per, 0, i % per))] * E
        + [
            row8,
            whole((8, width)),
            tile,
            tile,
            tile,
            whole((1, width)),
            pl.BlockSpec((w_out.shape[0], n * rows, BLK), lambda i: (0, at, 0), pipeline_mode=pl.Buffered(1)),
        ],
        out_specs=[tile, tile, tile, pl.BlockSpec((8, width), lambda i: (0, 0))],
        out_shape=[
            jax.ShapeDtypeStruct((tokens, width), f32),
            jax.ShapeDtypeStruct((tokens, width), bf16),
            jax.ShapeDtypeStruct((tokens, width), bf16),
            jax.ShapeDtypeStruct((8, width), f32),
        ],
        cost_estimate=cost(2 * tokens * width * (width + E * CAP), 20 * tokens * width),
        name="middle",
        after=after,
    )


def weight_grad_kernel(rows, n_old, idx_ref, left_ref, right_ref, *refs):
    keep_ref, send_ref, turned_ref = refs[n_old:]
    c = idx_ref[0]
    width = left_ref.shape[1]
    step = 384
    per = step // (2 * rows)

    @pl.when(pl.program_id(0) == 0)
    def _():
        for m in range(width // step):
            turned_ref[m * step : (m + 1) * step, :] = left_ref[:, m * step : (m + 1) * step].T

    right = right_ref[...]
    for m in range(width // step):
        keep, send = split_cores(dot(turned_ref[m * step : (m + 1) * step, :], right), c, rows)
        keep_ref[m * per : (m + 1) * per] = keep
        send_ref[m * per : (m + 1) * per] = send


def weight_grad_call(core, left, right, rows, n_z, total, at, name, old=(), after=()):
    tokens, width = left.shape
    n = right.shape[1] // BLK
    out = pl.BlockSpec((n_z, rows, BLK), lambda j, _: (0, at + j, 0))
    shape = jax.ShapeDtypeStruct((n_z, total, BLK), bf16)
    return kernel_call(
        functools.partial(weight_grad_kernel, rows, len(old)),
        [core, left, right, *old],
        prefetch=1,
        grid=(n,),
        in_specs=[
            pl.BlockSpec((tokens, width), lambda j, _: (0, 0), pipeline_mode=pl.Buffered(1)),
            pl.BlockSpec((tokens, BLK), lambda j, _: (0, j)),
        ]
        + [pl.BlockSpec(memory_space=pl.ANY)] * len(old),
        out_specs=[out, out],
        scratch=[pltpu.VMEM((width, tokens), bf16)],
        out_shape=[shape, shape],
        cost_estimate=cost(2 * tokens * width * n * BLK, 2 * width * n * BLK + 4 * tokens * width),
        aliases={3 + i: i for i in range(len(old))},
        name=name,
        after=after,
    )


def input_grad_kernel(rows, n, d_ref, w_ref, x_ref, dresid_ref, gain_ref, out_ref):
    dn1 = dot_last(d_ref[:, :BLK], w_ref[:, :rows, :].reshape(-1, BLK))
    for j in range(1, n):
        w = w_ref[:, j * rows : (j + 1) * rows, :].reshape(-1, BLK)
        dn1 += dot_last(d_ref[:, j * BLK : (j + 1) * BLK], w)
    x = x_ref[...].astype(f32)
    scale = lax.rsqrt(jnp.mean(x * x, axis=-1, keepdims=True) + epsilon)
    weighted = dn1 * gain_ref[...]
    along = jnp.mean(weighted * x, axis=-1, keepdims=True)
    out = dresid_ref[...] + scale * weighted - x * (scale * scale * scale * along)
    out_ref[...] = out.astype(bf16)


def input_grad_call(dqkv, w_in, x, dresid, gain, rows, n, after=()):
    tokens, width = x.shape
    tile = pl.BlockSpec((TILE, width), lambda i: (i, 0))
    return kernel_call(
        functools.partial(input_grad_kernel, rows, n),
        [dqkv, w_in, x, dresid, gain],
        grid=(tokens // TILE,),
        in_specs=[
            pl.BlockSpec((TILE, n * BLK), lambda i: (i, 0)),
            whole((w_in.shape[0], n * rows, BLK)),
            tile,
            tile,
            whole((1, width)),
        ],
        out_specs=tile,
        out_shape=jax.ShapeDtypeStruct((tokens, width), bf16),
        cost_estimate=cost(2 * tokens * width * n * BLK, 2 * width * n * BLK + 12 * tokens * width),
        name="input_grad",
        after=after,
    )


def adam_step(master, first, second, gradient, clip, decayed):
    clipped = gradient * clip
    first_new = beta_first * first + (1.0 - beta_first) * clipped
    second_new = beta_second * second + (1.0 - beta_second) * clipped * clipped
    first_hat = first_new * (1.0 / (1.0 - beta_first**STEP))
    second_hat = second_new * (1.0 / (1.0 - beta_second**STEP))
    change = first_hat / (jnp.sqrt(second_hat) + adam_floor) + decayed * weight_decay * master
    update = -learn_rate * change
    return (gradient, update, first_new, second_new)


def adam_kernel(scale, which, clip_ref, g_ref, master_ref, first_ref, second_ref, *outs):
    gradient = g_ref[...].astype(f32) * scale
    results = adam_step(master_ref[...], first_ref[...], second_ref[...], gradient, clip_ref[0, which], 1.0)
    for out, result in zip(outs, results):
        out[...] = result


def adam_call(clip, which, packed, at, master, first, second, scale, name, after=()):
    rows, cols = master.shape
    natural = pl.BlockSpec((rows, BLK), lambda j, _: (0, j))
    shape = jax.ShapeDtypeStruct(master.shape, f32)
    return kernel_call(
        functools.partial(adam_kernel, scale, which),
        [clip, packed, master, first, second],
            prefetch=1,
            grid=(cols // BLK,),
            in_specs=[pl.BlockSpec((rows, BLK), lambda j, _: (at // rows + j, 0)), natural, natural, natural],
            out_specs=[natural] * 4,
        out_shape=[shape] * 4,
        cost_estimate=cost(20 * master.size, 30 * master.size),
        name=name,
        after=after,
    )


def adam_experts_kernel(scale, which, clip_ref, g0_ref, g1_ref, g2_ref, master_ref, first_ref, second_ref, *outs):
    for e, g_ref in enumerate((g0_ref, g1_ref, g2_ref)):

        @pl.when(pl.program_id(0) == e)
        def _():
            gradient = g_ref[...].astype(f32) * scale
            results = adam_step(master_ref[0], first_ref[0], second_ref[0], gradient, clip_ref[0, which], 1.0)
            for out, result in zip(outs, results):
                out[0] = result


def adam_experts_call(clip, which, packed, at, master, first, second, scale, name, after=()):
    _, rows, cols = master.shape
    n = cols // BLK
    natural = pl.BlockSpec((1, rows, BLK), lambda e, j, _: (e, 0, j))
    shape = jax.ShapeDtypeStruct(master.shape, f32)

    def g_spec(own):
        return pl.BlockSpec(
            (rows, BLK), lambda e, j, _: (at // rows + jnp.where(e < own, 0, jnp.where(e > own, n - 1, j)), 0)
        )

    return kernel_call(
        functools.partial(adam_experts_kernel, scale, which),
        [clip, *packed, master, first, second],
            prefetch=1,
            grid=(E, n),
            in_specs=[g_spec(e) for e in range(E)] + [natural] * 3,
            out_specs=[natural] * 4,
        out_shape=[shape] * 4,
        cost_estimate=cost(20 * master.size, 30 * master.size),
        name=name,
        after=after,
    )


def per_device(
    tokens,
    cotangent,
    lengths,
    routes,
    slot_index,
    norm_gains,
    norm_first,
    norm_second,
    in_proj,
    in_first,
    in_second,
    out_proj,
    out_first,
    out_second,
    router,
    router_first,
    router_second,
    up_proj,
    up_first,
    up_second,
    down_proj,
    down_first,
    down_second,
):
    n_rep, n_f = lax.axis_size("replica"), lax.axis_size("fsdp")
    n_z = n_f // 2
    n_mb, n_local, seq, width = tokens.shape
    n_seq = n_mb * n_local
    total_tokens = n_seq * seq
    unit = 16 * n_rep
    rows = in_proj.shape[0]
    down_rows = down_proj.shape[1]
    n_in, n_out, n_up, n_down = (w.shape[-1] // BLK for w in (in_proj, out_proj, up_proj, down_proj))
    core = (lax.axis_index("fsdp") % 2).astype(jnp.int32)[None]

    smalls = jnp.concatenate([norm_gains.astype(bf16), router.astype(bf16).T], axis=0)
    n_small = round_up(smalls.size, BLK) // BLK
    smalls = jnp.pad(smalls.reshape(-1), (0, 16 * BLK - smalls.size)).reshape(16, BLK)
    e_rows = n_up * rows + n_down * down_rows
    in_shard, in_mine = pack_call([(in_proj, None)], unit, smalls)
    mid_shard, _ = pack_call([(up_proj, 0), (down_proj, 0), (out_proj, None)], unit, after=[in_shard])
    late_shard, late_mine, mid_mine = pack_call(
        [(w, e) for e in range(1, E) for w in (up_proj, down_proj)], unit, before=mid_shard
    )
    g_in, g_mid, g_late = Gather(in_shard), Gather(mid_shard), Gather(late_shard)
    g_in.start(in_mine, True)
    g_in.own_c = swap_core(in_shard)
    g_in.stack(after=[late_shard, g_in.own_c])
    g_mid.start(hold(mid_mine, g_in.stacks), False)
    g_in.double(after=[late_shard])
    g_in.low_c = [swap_core(x) for x in hold(g_in.stacks, g_in.received)]
    w_in = g_in.assemble()
    g_late.start(hold(late_mine, g_mid.pieces), False)

    small_all = w_in[:, n_in * rows : n_in * rows + n_small, :].reshape(n_f, n_small * BLK)[:, : 5 * rows]
    small_all = small_all.reshape(n_f, 5, rows).transpose(1, 0, 2).reshape(5, width)
    gain_one = small_all[0:1].astype(f32)
    gain_two = small_all[1:2].astype(f32)
    router8 = pad_rows(small_all[2:5], 8)

    length = lengths.reshape(n_seq).astype(jnp.int32)
    route = routes.reshape(n_seq, seq, 2)
    slot = slot_index.reshape(n_seq, seq, 2)
    live = jnp.arange(seq)[None, :] < length[:, None]
    kept = live[:, :, None] & (slot < CAP)
    slot_of = [
        jnp.max(jnp.where(kept & (route == e), slot, -1), axis=-1) for e in range(E)
    ]
    slot_rows = jnp.stack(slot_of + [live.astype(jnp.int32)] + [jnp.full_like(slot_of[0], -1)] * 4, axis=1)
    slot_cols = slot_rows.transpose(0, 2, 1).reshape(total_tokens, 8)

    x = tokens.reshape(total_tokens, width)
    cot = cotangent.reshape(total_tokens, width)

    qkv, n1 = qkv_call(x, gain_one, w_in, rows, n_in)
    g_mid.stack(after=[qkv])
    g_mid.double(after=[qkv])
    g_mid.swap_early()
    probs, mixed = attention_call(length, qkv, n_seq, after=g_mid.stacks)
    g_mid.settle([mixed])
    g_late.stack(after=[mixed, *g_mid.received])
    w_mid = g_mid.assemble(after=g_late.stacks)
    w_at = e_rows // (n_out * rows)
    resid, n2, prob = resid_call(mixed, w_mid, w_at, x, gain_two, router8, rows, n_out)
    g_late.double(after=[resid])
    g_late.swap_early()
    buf, dys, gates = dispatch_call(slot_rows, prob, n2, cot, n_seq, after=g_late.stacks)

    def expert(e, w, at, after):
        return expert_call(e, at, core, buf, dys, gates, slot_rows, w, rows, down_rows, unit, after)

    y0, dbuf0, dgate0, keep0, send0 = expert(0, w_mid, 0, ())
    g_late.settle([y0])
    got0 = swap_core(hold(send0, g_late.received))
    w_late = g_late.assemble(after=[y0])
    total0 = pair_sum(keep0, hold(got0, [w_late]))
    part0 = lax.psum_scatter(total0, "fsdp", axis_index_groups=core_groups())
    y1, dbuf1, dgate1, keep1, send1 = expert(1, w_late, 0, [total0])
    got1 = swap_core(send1)
    y2, dbuf2, dgate2, keep2, send2 = expert(2, w_late, e_rows, [y1])
    sum1 = Reduce(keep1, got1, 0)
    sent = sum1.step([y2])
    got2 = swap_core(hold(send2, sent))

    dresid, dattn, dmixed, router_part = middle_call(
        slot_cols,
        (dbuf0, dbuf1, dbuf2),
        (dgate0, dgate1, dgate2),
        prob,
        router8,
        n2,
        resid,
        cot,
        gain_two,
        w_mid,
        w_at,
        rows,
        n_out,
        n_seq,
        after=sent,
    )
    io_rows = round_up((n_in + n_out) * rows + 16, unit)
    keep, send = weight_grad_call(core, mixed, dattn, rows, n_z, io_rows, n_in, "out_grad")
    router_part = router_part[:E].astype(bf16).reshape(E, n_z, 2, rows).transpose(2, 1, 0, 3)
    router_part = jnp.pad(router_part, ((0, 0), (0, 0), (0, 16 - E), (0, BLK - rows)))
    at = (0, (n_in + n_out) * rows, 0)
    keep = lax.dynamic_update_slice(keep, lax.dynamic_index_in_dim(router_part, core[0], keepdims=False), at)
    send = lax.dynamic_update_slice(send, lax.dynamic_index_in_dim(router_part, 1 - core[0], keepdims=False), at)
    sum2 = Reduce(keep2, got2, 1)
    sent = sum1.step([send]) + sum2.step([send])
    dq, dk, dv = attention_back_call(qkv, probs, mixed, dmixed, n_seq, sent + [part0])
    sent = sum1.step([dq]) + sum2.step([dq])
    dqkv = jnp.concatenate([dq, dk, dv], axis=1)
    keep, send = weight_grad_call(core, n1, dqkv, rows, n_z, io_rows, 0, "in_grad", (keep, send), sent)
    sum2.newest = hold(sum2.newest, [send])
    got = swap_core(hold(send, sum2.newest))
    sum0 = lax.psum(part0, "replica")
    input_grad = input_grad_call(dqkv, w_in, x, dresid, gain_one, rows, n_in, [send])
    got = hold(got, [input_grad])
    sum1.newest = hold(sum1.newest, [input_grad])
    io_sum = Reduce(keep, got, 0)
    sent = io_sum.step(sum1.newest) + sum2.step(sum1.newest)
    block_out = combine_call(slot_cols, resid, (y0, y1, y2), n_seq, sent)
    sum2.newest = hold(sum2.newest, [block_out])
    sent = sum1.step(sum2.newest) + sum2.step()
    sent = io_sum.step(sent)
    sent = sum1.step(sent) + sum2.step(sent)
    sent = io_sum.step(sent)
    sums = [hold(sum0, sent), sum1.result(sent), sum2.result(sent)]

    grad_scale = 1.0 / (n_seq * n_rep * n_f)
    weights = (norm_gains, in_proj, out_proj, router, up_proj, down_proj)
    counts = (2 * width,) + tuple(w.size * n_f for w in weights[1:])

    def square(packed):
        values = packed.astype(f32) * grad_scale
        return jnp.sum(values * values)

    def along_rows(shard, packed, n):
        both = shard[: n * rows].astype(f32) * packed[: n * rows].astype(f32)
        return jnp.sum(both.reshape(n, rows, BLK), axis=(0, 2)) * grad_scale

    def rms_of(squares, which):
        lane = lax.broadcasted_iota(jnp.int32, (8, 128), 1)
        values = sum(jnp.where(lane == i, value, 0.0) for i, value in enumerate(squares))
        sizes = sum(jnp.where(lane == i, 1.0 / counts[w], 0.0) for i, w in enumerate(which))
        rms = jnp.sqrt(sum_small(values) * sizes + epsilon)
        return rms, jnp.minimum(1.0, clip_level / rms)

    at_down = n_up * rows
    early_rms, early_clip = rms_of([sum(square(s[:at_down]) for s in sums), sum(square(s[at_down:e_rows]) for s in sums)], (4, 5))
    sent = io_sum.step([early_clip])
    down_res = adam_experts_call(
        hold(early_clip, sent), 1, sums, at_down, down_proj, down_first, down_second, grad_scale, "down_adam"
    )
    sent = io_sum.step([down_res[1]])
    up_res = adam_experts_call(
        hold(early_clip, sent), 0, sums, 0, up_proj, up_first, up_second, grad_scale, "up_adam"
    )
    gains_low = norm_gains.astype(bf16).astype(f32)
    shards = (mid_shard, late_shard, late_shard[e_rows:])
    gain_two_grad = sum(along_rows(shard, packed, n_up) for shard, packed in zip(shards, sums))

    total = io_sum.result([up_res[1], gain_two_grad])
    in_sum, out_sum = total[: n_in * rows], total[n_in * rows : (n_in + n_out) * rows]
    at = (n_in + n_out) * rows
    router_grad = total[at : at + E, :rows].astype(f32) * grad_scale
    gain_one_grad = along_rows(in_shard, in_sum, n_in) / gains_low[0]
    gain_two_grad = gain_two_grad + jnp.sum(router.astype(bf16).astype(f32).T * router_grad, axis=0)
    gain_two_grad = gain_two_grad / gains_low[1]
    gain_grad = jnp.stack([gain_one_grad, gain_two_grad])
    late = [jnp.sum(gain_grad * gain_grad), square(in_sum), square(out_sum), jnp.sum(router_grad * router_grad)]
    late_rms, late_clip = rms_of(late, (0, 1, 2, 3))
    in_res = adam_call(late_clip, 1, total, 0, in_proj, in_first, in_second, grad_scale, "in_adam")
    out_res = adam_call(late_clip, 2, total, n_in * rows, out_proj, out_first, out_second, grad_scale, "out_adam")
    norm_res = adam_step(norm_gains, norm_first, norm_second, gain_grad, late_clip[0, 0], 0.0)
    router_res = adam_step(router, router_first, router_second, router_grad.T, late_clip[0, 3], 1.0)
    rms = jnp.concatenate([late_rms[0, :4], early_rms[0, :2]])
    return (
        block_out.reshape(tokens.shape),
        input_grad.reshape(tokens.shape),
        rms[:5],
        rms[5:],
        *norm_res,
        *in_res,
        *out_res,
        *router_res,
        *up_res,
        *down_res,
    )


def solution(mesh):
    data = P(None, ("replica", "fsdp"), None, None)
    gains = P(None, "fsdp")
    flat = P("fsdp", None)
    experts = P(None, "fsdp", None)
    return jax.shard_map(
        per_device,
        mesh=mesh,
        in_specs=(data, data, P(None, ("replica", "fsdp")), data, data)
        + (gains,) * 3
        + (flat,) * 9
        + (experts,) * 6,
        out_specs=(data, data, P(), P()) + (gains,) * 4 + (flat,) * 12 + (experts,) * 8,
        check_vma=False,
    )
```

```python
import functools

import jax
import jax.numpy as jnp
from jax import lax
from jax.experimental import pallas as pl
from jax.experimental.pallas import tpu as pltpu
from jax.sharding import PartitionSpec as P

QUERY_HEADS = 24
KEY_VALUE_HEADS = 8
HEAD_SIZE = 64
FE = 1024
E = 3
STEP = 10
CAP = 320
BLK = 512

epsilon = 1e-06
beta_first = 0.9
beta_second = 0.95
learn_rate = 0.02
weight_decay = 0.1
adam_floor = 1e-08
clip_level = 0.005

bf16 = jnp.bfloat16
f32 = jnp.float32

LAST = (((1,), (1,)), ((), ()))
FIRST = (((0,), (0,)), ((), ()))


def dot(a, b):
    return jnp.dot(a, b, preferred_element_type=f32)


def dot_last(a, b):
    return lax.dot_general(a, b, LAST, preferred_element_type=f32)


def dot_first(a, b):
    return lax.dot_general(a, b, FIRST, preferred_element_type=f32)


def params(mib=56):
    return pltpu.CompilerParams(vmem_limit_bytes=mib * 1024 * 1024)


def cost(flops, nbytes):
    return pl.CostEstimate(flops=int(flops) // 1000000000, bytes_accessed=int(nbytes) // 1000000, transcendentals=0)


def whole(shape, space=None):
    zeros = (0,) * len(shape)
    return pl.BlockSpec(shape, lambda *_: zeros, pipeline_mode=pl.Buffered(1))


def hold(values, after):
    if not after:
        return values
    return lax.optimization_barrier((values, list(after)))[0]


def kernel_call(
    kernel, args, *, grid, in_specs, out_specs, out_shape, name, cost_estimate, prefetch=0, scratch=(), after=(), mib=56, aliases=None
):
    args = list(args)
    args[0] = hold(args[0], after)
    return pl.pallas_call(
        kernel,
        grid_spec=pltpu.PrefetchScalarGridSpec(
            num_scalar_prefetch=prefetch,
            grid=grid,
            in_specs=list(in_specs),
            out_specs=out_specs,
            scratch_shapes=list(scratch),
        ),
        out_shape=out_shape,
        compiler_params=params(mib),
        cost_estimate=cost_estimate,
        input_output_aliases=aliases or {},
        name=name,
    )(*args)


def round_up(n, m):
    return -(-n // m) * m


def shift_core_pairs(x, k):
    size = lax.axis_size("fsdp")
    return lax.ppermute(x, "fsdp", [(i, (i + 2 * k) % size) for i in range(size)])


def core_groups():
    size = lax.axis_size("fsdp")
    return [list(range(c, size, 2)) for c in range(2)]


def swap_core(x):
    size = lax.axis_size("fsdp")
    return lax.ppermute(x, "fsdp", [(i, i ^ 1) for i in range(size)])


def swap_replica(x, bit):
    size = lax.axis_size("replica")
    return lax.ppermute(x, "replica", [(i, i ^ bit) for i in range(size)])


def bit_order(first):
    bits = []
    while (1 << len(bits)) < lax.axis_size("replica"):
        bits.append(1 << len(bits))
    return bits[first % len(bits) :] + bits[: first % len(bits)]


def stack_kernel(cuts, n_z, z_ref, *refs):
    pieces, outs = refs[: -len(cuts)], refs[-len(cuts) :]
    for (at, size), out in zip(cuts, outs):
        for k in range(1, n_z):
            if len(pieces) > 1:
                out[0, k - 1] = pieces[k - 1][at : at + size, :]
            else:
                out[0, k - 1] = pieces[0][lax.rem(z_ref[0] + n_z - k, n_z), at : at + size, :]


def assemble_kernel(masks, n_z, cuts, rows, idx_ref, *refs):
    n_in = 2 * (1 + 2 * len(cuts))
    out, sems, held = refs[n_in:]
    part, z, c = idx_ref[0], idx_ref[1], idx_ref[2]
    half = len(masks[0]) // 2
    blocks, count = [], 0
    for ins, core in ((refs[: n_in // 2], c), (refs[n_in // 2 : n_in], 1 - c)):
        for k in range(n_z):
            at_block = 2 * lax.rem(z + n_z - k, n_z) + core
            found = []
            if k == 0:
                found.append((ins[0], held.at[at_block]))
            else:
                for i, (offset, size) in enumerate(cuts):
                    for j, mask in enumerate(masks[i]):
                        at = pl.multiple_of((part ^ mask) * rows + offset, 16)
                        found.append(
                            (ins[1 + 2 * i + j // half].at[j % half, k - 1], held.at[at_block, pl.ds(at, size)])
                        )
            copies = [pltpu.make_async_copy(a, b, sems.at[count + i]) for i, (a, b) in enumerate(found)]
            count += len(copies)
            for copy in copies:
                copy.start()
            blocks.append((at_block, copies))
    written = []
    for i, (at_block, copies) in enumerate(blocks):
        for copy in copies:
            copy.wait()
        copy = pltpu.make_async_copy(held.at[at_block], out.at[at_block], sems.at[count + i])
        copy.start()
        written.append(copy)
    for copy in written:
        copy.wait()


class Gather:
    def __init__(self, shard):
        self.shard = shard
        self.n_z = lax.axis_size("fsdp") // 2
        self.rows = shard.shape[0] // lax.axis_size("replica")
        half = round_up(self.rows // 2, 16)
        self.cuts = ((0, half), (half, self.rows - half))
        self.orders = [bit_order(i) for i in range(len(self.cuts))]
        self.masks = [[0] for _ in self.cuts]

    def start(self, mine, direct):
        if direct:
            self.pieces = [shift_core_pairs(mine, k) for k in range(1, self.n_z)]
        else:
            self.pieces = [lax.all_gather(mine, "fsdp", axis_index_groups=core_groups())]

    def stack(self, after=()):
        in_specs = [pl.BlockSpec(p.shape, (lambda i, _: (0, 0, 0)) if p.ndim == 3 else (lambda i, _: (0, 0))) for p in self.pieces]
        shapes = [(1, self.n_z - 1, size, BLK) for _, size in self.cuts]
        self.stacks = kernel_call(
            functools.partial(stack_kernel, self.cuts, self.n_z),
            [(lax.axis_index("fsdp") // 2).astype(jnp.int32)[None], *self.pieces],
            prefetch=1,
            grid=(1,),
            in_specs=in_specs,
            out_specs=[pl.BlockSpec(shape, lambda i, _: (0, 0, 0, 0)) for shape in shapes],
            out_shape=[jax.ShapeDtypeStruct(shape, bf16) for shape in shapes],
            name="stack",
            cost_estimate=cost(0, 4 * self.rows * BLK * (self.n_z - 1)),
            after=after,
        )
        self.swap(0)

    def swap(self, step):
        self.received = [swap_replica(x, order[step]) for x, order in zip(self.stacks, self.orders)]
        self.masks = [m + [v ^ order[step] for v in m] for m, order in zip(self.masks, self.orders)]

    def double(self, after=()):
        for step in range(1, len(self.orders[0])):
            arrived = hold(self.received, after)
            self.stacks = [jnp.concatenate(pair) for pair in zip(self.stacks, arrived)]
            self.swap(step)

    def swap_early(self):
        self.own_c = swap_core(self.shard)
        self.low_c = [swap_core(x) for x in self.stacks]

    def settle(self, after):
        self.received, self.own_c, self.low_c = hold((self.received, self.own_c, self.low_c), after)

    def assemble(self, after=()):
        place = lax.axis_index("fsdp")
        idx = jnp.stack([lax.axis_index("replica"), place // 2, place % 2]).astype(jnp.int32)
        ins = [self.shard]
        other = [self.own_c]
        high_c = self.high_c = [swap_core(x) for x in self.received]
        for pair in zip(self.stacks, self.received):
            ins += pair
        for pair in zip(self.low_c, high_c):
            other += pair
        n_f = lax.axis_size("fsdp")
        n_copies = 2 * (1 + len(self.cuts) * len(self.masks[0]) * (self.n_z - 1))
        anyspec = pl.BlockSpec(memory_space=pl.ANY)
        return kernel_call(
            functools.partial(assemble_kernel, self.masks, self.n_z, self.cuts, self.rows),
            [idx, *ins, *other],
            prefetch=1,
            grid=(1,),
            in_specs=[anyspec] * (2 * len(ins)),
            out_specs=anyspec,
            out_shape=jax.ShapeDtypeStruct((n_f,) + self.shard.shape, bf16),
            scratch=[
                pltpu.SemaphoreType.DMA((n_copies + n_f,)),
                pltpu.VMEM((n_f,) + self.shard.shape, bf16),
            ],
            name="assemble",
            cost_estimate=cost(0, 4 * n_f * self.shard.size),
            after=after,
        )


class Reduce:
    def __init__(self, keep, received, first=0):
        n_rep, self.n_z = lax.axis_size("replica"), lax.axis_size("fsdp") // 2
        self.part, self.z = lax.axis_index("replica"), lax.axis_index("fsdp") // 2
        self.rows = keep.shape[1] // n_rep
        n_bits = len(bit_order(0))
        self.bits = [1 << b for b in range(n_bits)]
        self.order = bit_order(first)
        shape = (self.n_z,) + (2,) * n_bits + (self.rows, BLK)
        half = round_up(self.rows // 2, 16)
        self.cuts = ((0, half), (half, self.rows - half))
        self.orders = [bit_order(i) for i in range(len(self.cuts))]
        self.live = [list(reversed(self.bits)) for _ in self.cuts]
        self.terms = [[keep.reshape(shape)] for _ in self.cuts]
        self.newest = [received.reshape(shape)]
        self.have = None
        halves = [functools.partial(self.halve, i) for i in range(n_bits)]
        gathers = [functools.partial(self.gather, i, bit) for i, bit in enumerate(self.order)]
        self.todo = [halves[:1], halves[1:], [self.along], gathers[:1], gathers[1:]]

    def step(self, after=()):
        self.newest = hold(self.newest, after)
        for action in self.todo.pop(0):
            sent = action()
        return sent

    def part_sum(self, terms):
        return functools.reduce(jnp.add, [t.astype(f32) for t in terms])

    def halve(self, i):
        news, marks = [], []
        for p, (at, size) in enumerate(self.cuts):
            self.terms[p] = self.terms[p] + [self.newest[p % len(self.newest)]]
            bit = self.orders[p][i]
            axis = 1 + self.live[p].index(bit)
            self.live[p].remove(bit)
            own = (self.part // bit) % 2

            def take(t, index):
                starts, sizes = [0] * t.ndim, list(t.shape)
                starts[axis], sizes[axis] = index, 1
                if i == 0:
                    starts[-2], sizes[-2] = at, size
                out = lax.dynamic_slice(t, starts, sizes)
                return out.reshape(out.shape[:axis] + out.shape[axis + 1 :])

            away = self.part_sum([take(t, 1 - own) for t in self.terms[p]]).astype(bf16)
            self.terms[p] = [take(t, own) for t in self.terms[p]]
            news.append(swap_replica(away, bit))
            marks.append(away)
        self.newest = news
        return marks

    def at_place(self, z):
        parts = [
            self.part_sum([lax.dynamic_index_in_dim(t, z, 0, keepdims=False) for t in terms]) for terms in self.terms
        ]
        return jnp.concatenate(parts)

    def along(self):
        self.terms = [terms + [new] for terms, new in zip(self.terms, self.newest)]
        aways = [self.at_place((self.z + k) % self.n_z).astype(bf16) for k in range(1, self.n_z)]
        self.newest = [shift_core_pairs(away, k) for k, away in enumerate(aways, 1)]
        return aways

    def sum_here(self, after=()):
        if self.have is None:
            summed = self.at_place(self.z)
            for got in hold(self.newest, after):
                summed = summed + got.astype(f32)
            self.have = summed.astype(bf16)
        return self.have

    def gather(self, i, bit):
        if i == 0:
            self.sum_here()
        else:
            self.have = self.joined()
        self.newest, self.bit = [swap_replica(self.have, bit)], bit
        return [self.have]

    def joined(self):
        pair = jnp.stack([self.have, self.newest[0]])
        return jnp.where((self.part // self.bit) % 2 == 1, pair[::-1], pair)

    def result(self, after=()):
        self.newest = hold(self.newest, after)
        stack = self.joined()
        names = list(reversed(self.order))
        n_bits = len(names)
        stack = jnp.transpose(stack, tuple(names.index(b) for b in reversed(self.bits)) + (n_bits, n_bits + 1))
        return stack.reshape(-1, BLK)


def pair_sum(keep, got):
    return (keep.astype(f32) + got.astype(f32)).astype(bf16)


def sum_small(x, bit=1, after=()):
    size = lax.axis_size("fsdp")
    while bit < size:
        x = x + hold(lax.ppermute(x, "fsdp", [(i, i ^ bit) for i in range(size)]), after)
        bit *= 2
        after = ()
    return x


def pack_kernel(counts, has_extra, has_before, prefix_ref, *refs):
    n = len(counts) + has_extra + has_before
    out = refs[n]
    at = 0
    for ref, count in zip(refs, counts):
        value = ref[0] if len(ref.shape) == 3 else ref[...]
        for j in range(count):
            out[at : at + value.shape[0], :] = value[:, j * BLK : (j + 1) * BLK].astype(bf16)
            at += value.shape[0]
    if has_extra:
        extra = refs[len(counts)][...]
        out[at : at + extra.shape[0], :] = extra
        at += extra.shape[0]
    if at < out.shape[0]:
        out[at:, :] = jnp.zeros((out.shape[0] - at, BLK), bf16)
    mine = refs[n + 1]
    rows = mine.shape[0]
    mine[...] = out[pl.ds(pl.multiple_of(prefix_ref[0] * rows, 16), rows), :]
    if has_before:
        refs[n + 2][...] = refs[n - 1][...]


def pack_call(parts, unit, extra=None, before=None, after=()):
    specs, counts, total = [], [], 0
    for w, e in parts:
        if e is None:
            specs.append(pl.BlockSpec(w.shape, lambda i, _: (0, 0)))
        else:
            specs.append(pl.BlockSpec((1,) + w.shape[1:], lambda i, _, e=e: (e, 0, 0)))
        counts.append(w.shape[-1] // BLK)
        total += counts[-1] * w.shape[-2]
    part = lax.axis_index("replica").astype(jnp.int32)[None]
    args = [part] + [w for w, _ in parts]
    if extra is not None:
        args.append(extra)
        specs.append(pl.BlockSpec(extra.shape, lambda i, _: (0, 0)))
        total += extra.shape[0]
    total = round_up(total, unit)
    n_rep = lax.axis_size("replica")
    shapes = [(total, BLK), (total // n_rep, BLK)]
    if before is not None:
        shapes.append((before.shape[0] // n_rep, BLK))
        args.append(before)
        specs.append(pl.BlockSpec(shapes[-1], lambda i, part: (part[0], 0)))
    return kernel_call(
        functools.partial(pack_kernel, tuple(counts), extra is not None, before is not None),
        args,
        prefetch=1,
        grid=(1,),
        in_specs=specs,
        out_specs=[pl.BlockSpec(shape, lambda i, _: (0, 0)) for shape in shapes],
        out_shape=[jax.ShapeDtypeStruct(shape, bf16) for shape in shapes],
        cost_estimate=cost(0, 6 * total * BLK),
        name="pack",
        after=after,
    )


def pad_rows(x, rows):
    return jnp.pad(x, ((0, rows - x.shape[0]), (0, 0)))


def qkv_kernel(x_ref, gain_ref, w_ref, qkv_ref, n1_ref):
    tokens, width = x_ref.shape

    @pl.when(pl.program_id(0) == 0)
    def _():
        def body(i, _):
            rows = pl.ds(pl.multiple_of(i * 128, 128), 128)
            xf = x_ref[rows, :].astype(f32)
            scale = lax.rsqrt(jnp.mean(xf * xf, axis=-1, keepdims=True) + epsilon)
            n1_ref[rows, :] = (xf * scale * gain_ref[...]).astype(bf16)
            return 0

        lax.fori_loop(0, tokens // 128, body, 0)

    w = w_ref[...].reshape(width, BLK)

    def body(i, _):
        rows = pl.ds(pl.multiple_of(i * 256, 256), 256)
        qkv_ref[rows, :] = dot(n1_ref[rows, :], w).astype(bf16)
        return 0

    lax.fori_loop(0, tokens // 256, body, 0)


def qkv_call(x, gain, w_in, rows, n, after=()):
    tokens, width = x.shape
    n_f = w_in.shape[0]
    return kernel_call(
        qkv_kernel,
        [x, gain, w_in],
        grid=(n,),
        in_specs=[
            whole((tokens, width)),
            whole((1, width)),
            pl.BlockSpec((n_f, rows, BLK), lambda j: (0, j, 0)),
        ],
        out_specs=[
            pl.BlockSpec((tokens, BLK), lambda j: (0, j)),
            pl.BlockSpec((tokens, width), lambda j: (0, 0)),
        ],
        out_shape=[
            jax.ShapeDtypeStruct((tokens, n * BLK), bf16),
            jax.ShapeDtypeStruct((tokens, width), bf16),
        ],
        cost_estimate=cost(2 * tokens * width * n * BLK, 2 * width * n * BLK + 4 * tokens * width),
        name="qkv",
        after=after,
    )


HALF = 256


def attention_kernel(len_ref, q_ref, k_ref, v_ref, p_ref, mix_ref):
    seq = q_ref.shape[0]
    length = len_ref[pl.program_id(0)]
    key = lax.broadcasted_iota(jnp.int32, (seq, seq), 0)
    query = lax.broadcasted_iota(jnp.int32, (seq, seq), 1)
    bias = jnp.where((key <= query) & (key < length), 0.0, -1000000000.0).astype(f32)
    group = QUERY_HEADS // KEY_VALUE_HEADS
    for h in range(2 * group):
        g = h // group
        lanes = slice(h * HEAD_SIZE, (h + 1) * HEAD_SIZE)
        kv = slice(g * HEAD_SIZE, (g + 1) * HEAD_SIZE)
        q = q_ref[:, lanes] * jnp.asarray(HEAD_SIZE ** (-0.5), bf16)
        for start in range(0, seq, HALF):
            stop = start + HALF
            s = dot_last(k_ref[:stop, kv], q[start:stop]) + bias[:stop, start:stop]
            raised = jnp.exp(s - jnp.max(s, axis=0, keepdims=True))
            probs = (raised * (1.0 / jnp.sum(raised, axis=0, keepdims=True))).astype(bf16)
            p_ref[0, h, :stop, start:stop] = probs
            if stop < seq:
                p_ref[0, h, stop:, start:stop] = jnp.zeros((seq - stop, HALF), bf16)
            mixed = dot_first(v_ref[:stop, kv], probs)
            mix_ref[start:stop, lanes] = mixed.T.astype(bf16)


def attention_call(lengths, qkv, n_seq, after=()):
    tokens = qkv.shape[0]
    seq = tokens // n_seq
    pairs = KEY_VALUE_HEADS // 2
    heads = QUERY_HEADS // pairs
    qw = heads * HEAD_SIZE
    kw = 2 * HEAD_SIZE
    k_at = QUERY_HEADS * HEAD_SIZE // kw
    v_at = k_at + pairs
    return kernel_call(
        attention_kernel,
        [lengths, qkv, qkv, qkv],
            prefetch=1,
            grid=(n_seq, pairs),
            in_specs=[
                pl.BlockSpec((seq, qw), lambda s, j, _: (s, j)),
                pl.BlockSpec((seq, kw), lambda s, j, _: (s, k_at + j)),
                pl.BlockSpec((seq, kw), lambda s, j, _: (s, v_at + j)),
            ],
            out_specs=[
                pl.BlockSpec((1, heads, seq, seq), lambda s, j, _: (s, j, 0, 0)),
                pl.BlockSpec((seq, qw), lambda s, j, _: (s, j)),
            ],
        out_shape=[
            jax.ShapeDtypeStruct((n_seq, QUERY_HEADS, seq, seq), bf16),
            jax.ShapeDtypeStruct((tokens, QUERY_HEADS * HEAD_SIZE), bf16),
        ],
        cost_estimate=cost(16 * n_seq * QUERY_HEADS * seq * seq * HEAD_SIZE, 2 * n_seq * QUERY_HEADS * seq * seq),
        name="attention",
        after=after,
    )


def attention_back_kernel(q_ref, k_ref, v_ref, p_ref, mix_ref, dmix_ref, dq_ref, dk_ref, dv_ref):
    seq = q_ref.shape[0]
    group = QUERY_HEADS // KEY_VALUE_HEADS
    scale = HEAD_SIZE ** (-0.5)
    ones = jnp.ones((8, HEAD_SIZE), bf16)
    for g in range(2):
        kv = slice(g * HEAD_SIZE, (g + 1) * HEAD_SIZE)
        k, v = k_ref[:, kv], v_ref[:, kv]
        n_half = seq // HALF
        dk = [jnp.zeros((HALF, HEAD_SIZE), f32) for _ in range(n_half)]
        dv = [jnp.zeros((HALF, HEAD_SIZE), f32) for _ in range(n_half)]
        for i in range(group):
            h = g * group + i
            lanes = slice(h * HEAD_SIZE, (h + 1) * HEAD_SIZE)
            for start in range(0, seq, HALF):
                stop = start + HALF
                dmix = dmix_ref[start:stop, lanes]
                q = q_ref[start:stop, lanes]
                both = dmix.astype(f32) * mix_ref[start:stop, lanes].astype(f32)
                high = both.astype(bf16)
                low = (both - high.astype(f32)).astype(bf16)
                delta = (dot_last(ones, high) + dot_last(ones, low))[:1]
                probs = p_ref[0, h, :stop, start:stop]
                dp = dot_last(v[:stop], dmix)
                ds = (probs.astype(f32) * (dp - delta)).astype(bf16)
                dq = dot_first(k[:stop], ds)
                dq_ref[start:stop, lanes] = (dq.T * scale).astype(bf16)
                dk_part = dot(ds, q)
                dv_part = dot(probs, dmix)
                for m in range(stop // HALF):
                    rows = slice(m * HALF, (m + 1) * HALF)
                    dk[m] += dk_part[rows]
                    dv[m] += dv_part[rows]
        for m in range(n_half):
            rows = slice(m * HALF, (m + 1) * HALF)
            dk_ref[rows, kv] = (dk[m] * scale).astype(bf16)
            dv_ref[rows, kv] = dv[m].astype(bf16)


def attention_back_call(qkv, probs, mixed, dmixed, n_seq, after=()):
    tokens = qkv.shape[0]
    seq = tokens // n_seq
    pairs = KEY_VALUE_HEADS // 2
    heads = QUERY_HEADS // pairs
    qw = heads * HEAD_SIZE
    kw = 2 * HEAD_SIZE
    k_at = QUERY_HEADS * HEAD_SIZE // kw
    v_at = k_at + pairs
    qspec = pl.BlockSpec((seq, qw), lambda s, j: (s, j))
    kspec = pl.BlockSpec((seq, kw), lambda s, j: (s, j))
    return kernel_call(
        attention_back_kernel,
        [qkv, qkv, qkv, probs, mixed, dmixed],
        grid=(n_seq, pairs),
        in_specs=[
            qspec,
            pl.BlockSpec((seq, kw), lambda s, j: (s, k_at + j)),
            pl.BlockSpec((seq, kw), lambda s, j: (s, v_at + j)),
            pl.BlockSpec((1, heads, seq, seq), lambda s, j: (s, j, 0, 0)),
            qspec,
            qspec,
        ],
        out_specs=[qspec, kspec, kspec],
        out_shape=[
            jax.ShapeDtypeStruct((tokens, QUERY_HEADS * HEAD_SIZE), bf16),
            jax.ShapeDtypeStruct((tokens, KEY_VALUE_HEADS * HEAD_SIZE), bf16),
            jax.ShapeDtypeStruct((tokens, KEY_VALUE_HEADS * HEAD_SIZE), bf16),
        ],
        cost_estimate=cost(32 * n_seq * QUERY_HEADS * seq * seq * HEAD_SIZE, 2 * n_seq * QUERY_HEADS * seq * seq),
        name="attention_back",
        after=after,
    )


TILE = 256


def resid_kernel(rows, n, mix_ref, w_ref, x_ref, gain_ref, router_ref, resid_ref, n2_ref, prob_ref):
    width = x_ref.shape[1]
    mixed = mix_ref[...]
    squares = jnp.zeros((TILE, 1), f32)
    for j in range(n):
        cols = slice(j * BLK, (j + 1) * BLK)
        w = w_ref[:, j * rows : (j + 1) * rows, :].reshape(-1, BLK)
        part = x_ref[:, cols].astype(f32) + dot(mixed, w)
        resid_ref[:, cols] = part
        squares += jnp.sum(part * part, axis=-1, keepdims=True)
    scale = lax.rsqrt(squares * (1.0 / width) + epsilon)
    n2 = (resid_ref[...] * scale * gain_ref[...]).astype(bf16)
    n2_ref[...] = n2
    logits = dot_last(router_ref[...], n2)
    logits = jnp.where(lax.broadcasted_iota(jnp.int32, logits.shape, 0) < E, logits, -1e30)
    raised = jnp.exp(logits - jnp.max(logits, axis=0, keepdims=True))
    prob_ref[...] = raised / jnp.sum(raised, axis=0, keepdims=True)


def resid_call(mixed, w_out, at, x, gain, router, rows, n, after=()):
    tokens, width = x.shape
    tile = pl.BlockSpec((TILE, width), lambda i: (i, 0))
    return kernel_call(
        functools.partial(resid_kernel, rows, n),
        [mixed, w_out, x, gain, router],
        grid=(tokens // TILE,),
        in_specs=[
            tile,
            pl.BlockSpec((w_out.shape[0], n * rows, BLK), lambda i: (0, at, 0), pipeline_mode=pl.Buffered(1)),
            tile,
            whole((1, width)),
            whole((8, width)),
        ],
        out_specs=[tile, tile, pl.BlockSpec((8, TILE), lambda i: (0, i))],
        out_shape=[
            jax.ShapeDtypeStruct((tokens, width), f32),
            jax.ShapeDtypeStruct((tokens, width), bf16),
            jax.ShapeDtypeStruct((8, tokens), f32),
        ],
        cost_estimate=cost(2 * tokens * width * width, 2 * width * width + 12 * tokens * width),
        name="resid",
        after=after,
    )


def dispatch_kernel(slot_ref, prob_ref, n2_ref, cot_ref, buf_ref, dys_ref, gate_ref):
    e = pl.program_id(1)
    slots = slot_ref[0, pl.ds(e, 1), :]
    hit = lax.broadcasted_iota(jnp.int32, (CAP, slots.shape[1]), 0) == slots
    gate = jnp.sum(jnp.where(hit, prob_ref[pl.ds(e, 1), :], 0.0), axis=-1, keepdims=True)
    gate_ref[0, 0] = jnp.broadcast_to(gate, (CAP, 128))
    hit = jnp.where(hit, 1.0, 0.0).astype(bf16)
    buf_ref[0, 0] = dot(hit, n2_ref[...]).astype(bf16)
    dys_ref[0, 0] = dot(hit, cot_ref[...]).astype(bf16)


def dispatch_call(slots, prob, n2, cot, n_seq, after=()):
    tokens, width = n2.shape
    seq = tokens // n_seq
    out = pl.BlockSpec((1, 1, CAP, width), lambda s, e: (e, s, 0, 0))
    return kernel_call(
        dispatch_kernel,
        [slots, prob, n2, cot],
        grid=(n_seq, E),
        in_specs=[
            pl.BlockSpec((1, 8, seq), lambda s, e: (s, 0, 0)),
            pl.BlockSpec((8, seq), lambda s, e: (0, s)),
            pl.BlockSpec((seq, width), lambda s, e: (s, 0)),
            pl.BlockSpec((seq, width), lambda s, e: (s, 0)),
        ],
        out_specs=[out, out, pl.BlockSpec((1, 1, CAP, 128), lambda s, e: (e, s, 0, 0))],
        out_shape=[
            jax.ShapeDtypeStruct((E, n_seq, CAP, width), bf16),
            jax.ShapeDtypeStruct((E, n_seq, CAP, width), bf16),
            jax.ShapeDtypeStruct((E, n_seq, CAP, 128), f32),
        ],
        cost_estimate=cost(4 * E * CAP * tokens * width, 20 * tokens * width),
        name="dispatch",
        after=after,
    )


def split_cores(block, c, rows):
    parts = block.reshape(-1, 2, rows, block.shape[-1])
    even, odd = parts[:, 0], parts[:, 1]
    return (
        jnp.where(c == 0, even, odd).astype(bf16),
        jnp.where(c == 0, odd, even).astype(bf16),
    )


def expert_kernel(
    e,
    up_rows,
    down_rows,
    idx_ref,
    buf_ref,
    dys_ref,
    gate_ref,
    slot_ref,
    up_a_ref,
    up_b_ref,
    down_ref,
    yg_ref,
    dbuf_ref,
    dgate_ref,
    keep_ref,
    send_ref,
    y_acc,
    d_acc,
    dyexp_ref,
    hid_ref,
    da_ref,
    db_ref,
    dg_acc,
    up_held,
    down_held,
    sems,
):
    h = pl.program_id(0)
    last = pl.num_programs(0) - 1
    c = idx_ref[0]
    n_seq = buf_ref.shape[1]
    width = buf_ref.shape[3]
    n_d = width // BLK
    up_a = up_a_ref[...].reshape(width, BLK)
    up_b = up_b_ref[...].reshape(width, BLK)
    downs = [down_ref[:, j * down_rows : (j + 1) * down_rows, :].reshape(BLK, BLK) for j in range(n_d)]
    for s in range(n_seq):
        rows = slice(s * CAP, (s + 1) * CAP)
        gate = gate_ref[0, s, :, :1]

        @pl.when(h == 0)
        def _():
            dyexp_ref[rows, :] = (gate * dys_ref[0, s].astype(f32)).astype(bf16)

        x = buf_ref[0, s]
        a = dot(x, up_a)
        b = dot(x, up_b)
        sigma = jax.nn.sigmoid(a)
        silu = a * sigma
        hid = (silu * b).astype(bf16)
        hid_ref[rows, :] = hid
        du = dot_last(dys_ref[0, s, :, :BLK], downs[0])
        for j in range(1, n_d):
            du += dot_last(dys_ref[0, s, :, j * BLK : (j + 1) * BLK], downs[j])
        dg = jnp.sum(du * hid.astype(f32), axis=-1, keepdims=True)
        dh = gate * du
        da = (dh * b * sigma * (1.0 + a * (1.0 - sigma))).astype(bf16)
        db = (dh * silu).astype(bf16)
        da_ref[rows, :] = da
        db_ref[rows, :] = db

        @pl.when(h == 0)
        def _():
            dg_acc[rows, :] = jnp.broadcast_to(dg, (CAP, 128))
            for j in range(n_d):
                y_acc[rows, j * BLK : (j + 1) * BLK] = dot(hid, downs[j])
            d_acc[rows, :] = dot_last(da, up_a) + dot_last(db, up_b)

        @pl.when(h > 0)
        def _():
            dg_acc[rows, :] += jnp.broadcast_to(dg, (CAP, 128))
            for j in range(n_d):
                y_acc[rows, j * BLK : (j + 1) * BLK] += dot(hid, downs[j])
            d_acc[rows, :] += dot_last(da, up_a) + dot_last(db, up_b)

        @pl.when(h == last)
        def _():
            yg_ref[s] = (gate * y_acc[rows, :]).astype(bf16)
            dbuf_ref[s] = d_acc[rows, :].astype(bf16)
            slots = slot_ref[s, e : e + 1, :]
            hit = lax.broadcasted_iota(jnp.int32, (CAP, slots.shape[1]), 0) == slots
            row = jnp.sum(jnp.where(hit, dg_acc[rows, :1], 0.0), axis=0, keepdims=True)
            dgate_ref[s] = jnp.broadcast_to(row, (8, slots.shape[1]))

    step = 384
    per = step // (2 * up_rows)

    for m in range(width // step):
        x = jnp.concatenate([buf_ref[0, s, :, m * step : (m + 1) * step] for s in range(n_seq)], axis=0)
        xt = x.T
        for i, d_ref in enumerate((da_ref, db_ref)):
            keep, send = split_cores(dot(xt, d_ref[...]), c, up_rows)
            up_held[h, 0, i, m * per : (m + 1) * per] = keep
            up_held[h, 1, i, m * per : (m + 1) * per] = send
    hid_t = hid_ref[...].T
    for j in range(n_d):
        keep, send = split_cores(dot(hid_t, dyexp_ref[:, j * BLK : (j + 1) * BLK]), c, down_rows)
        down_held[h, 0, :, j * down_rows : (j + 1) * down_rows, :] = keep
        down_held[h, 1, :, j * down_rows : (j + 1) * down_rows, :] = send
    n_h = FE // BLK
    n_zh = keep_ref.shape[0] // n_h

    def copies(step):
        found = []
        for side, ref in enumerate((keep_ref, send_ref)):
            for i in range(2):
                place = pl.ds((i * n_h + step) * up_rows, up_rows)
                found.append((up_held.at[step, side, i], ref.at[:, place, :]))
            place = pl.ds(2 * n_h * up_rows, n_d * down_rows)
            found.append((down_held.at[step, side], ref.at[step * n_zh : (step + 1) * n_zh, place, :]))
        return [pltpu.make_async_copy(a, b, sems.at[step, i]) for i, (a, b) in enumerate(found)]

    for step in range(n_h):

        @pl.when(h == step)
        def _():
            for copy in copies(step):
                copy.start()

    @pl.when(h == last)
    def _():
        for step in range(n_h):
            for copy in copies(step):
                copy.wait()


def expert_call(e, at, core, buf, dys, gates, slots, w, up_rows, down_rows, unit, after=()):
    _, n_seq, _, width = buf.shape
    n_f = w.shape[0]
    n_z = n_f // 2
    n_h = FE // BLK
    n_d = width // BLK
    seq = slots.shape[2]
    data = pl.BlockSpec((1, n_seq, CAP, width), lambda h, _: (e, 0, 0, 0), pipeline_mode=pl.Buffered(1))
    out = pl.BlockSpec((n_seq, CAP, width), lambda h, _: (0, 0, 0))
    anyspec = pl.BlockSpec(memory_space=pl.ANY)
    total = round_up(2 * n_h * up_rows + n_d * down_rows, unit)
    grad_shape = jax.ShapeDtypeStruct((n_z, total, BLK), bf16)
    rows = n_seq * CAP
    yg, dbuf, dgate, keep, send = kernel_call(
        functools.partial(expert_kernel, e, up_rows, down_rows),
        [core, buf, dys, gates, slots, w, w, w],
            prefetch=1,
            grid=(n_h,),
            in_specs=[
                data,
                data,
                pl.BlockSpec((1, n_seq, CAP, 128), lambda h, _: (e, 0, 0, 0)),
                pl.BlockSpec((n_seq, 8, seq), lambda h, _: (0, 0, 0)),
                pl.BlockSpec((n_f, up_rows, BLK), lambda h, _: (0, at // up_rows + h, 0)),
                pl.BlockSpec((n_f, up_rows, BLK), lambda h, _: (0, at // up_rows + n_h + h, 0)),
                pl.BlockSpec(
                    (n_f // n_h, n_d * down_rows, BLK),
                    lambda h, _: (h, (at + 2 * n_h * up_rows) // (n_d * down_rows), 0),
                ),
            ],
            out_specs=[
                out,
                out,
                pl.BlockSpec((n_seq, 8, seq), lambda h, _: (0, 0, 0)),
                anyspec,
                anyspec,
            ],
            scratch=[
                pltpu.VMEM((rows, width), f32),
                pltpu.VMEM((rows, width), f32),
                pltpu.VMEM((rows, width), bf16),
                pltpu.VMEM((rows, BLK), bf16),
                pltpu.VMEM((rows, BLK), bf16),
                pltpu.VMEM((rows, BLK), bf16),
                pltpu.VMEM((rows, 128), f32),
                pltpu.VMEM((n_h, 2, 2, n_z, up_rows, BLK), bf16),
                pltpu.VMEM((n_h, 2, n_z // n_h, n_d * down_rows, BLK), bf16),
                pltpu.SemaphoreType.DMA((n_h, 6)),
            ],
        out_shape=[
            jax.ShapeDtypeStruct((n_seq, CAP, width), bf16),
            jax.ShapeDtypeStruct((n_seq, CAP, width), bf16),
            jax.ShapeDtypeStruct((n_seq, 8, seq), f32),
            grad_shape,
            grad_shape,
        ],
        mib=60,
        cost_estimate=cost(18 * rows * width * FE, 40 * width * FE),
        name="expert",
        after=after,
    )
    return yg, dbuf, dgate, keep, send


def spread(col_ref, e):
    slots = col_ref[:, e : e + 1]
    hit = lax.broadcasted_iota(jnp.int32, (col_ref.shape[0], CAP), 1) == slots
    return jnp.where(hit, 1.0, 0.0).astype(bf16)


def combine_kernel(col_ref, resid_ref, y0_ref, y1_ref, y2_ref, out_ref):
    total = resid_ref[...]
    for e, y_ref in enumerate((y0_ref, y1_ref, y2_ref)):
        total += dot(spread(col_ref, e), y_ref[0])
    out_ref[...] = jnp.where(col_ref[:, E : E + 1] > 0, total, 0.0).astype(bf16)


def combine_call(cols, resid, ys, n_seq, after=()):
    tokens, width = resid.shape
    per = tokens // n_seq // TILE
    tile = pl.BlockSpec((TILE, width), lambda i: (i, 0))
    return kernel_call(
        combine_kernel,
        [cols, resid, *ys],
        grid=(tokens // TILE,),
        in_specs=[pl.BlockSpec((TILE, 8), lambda i: (i, 0)), tile]
        + [pl.BlockSpec((1, CAP, width), lambda i: (i // per, 0, 0))] * E,
        out_specs=tile,
        out_shape=jax.ShapeDtypeStruct((tokens, width), bf16),
        cost_estimate=cost(2 * E * CAP * tokens * width, 12 * tokens * width),
        name="combine",
        after=after,
    )


def hi_lo(x):
    high = x.astype(bf16)
    return high, (x - high.astype(f32)).astype(bf16)


def middle_kernel(
    rows,
    n,
    col_ref,
    d0_ref,
    d1_ref,
    d2_ref,
    g0_ref,
    g1_ref,
    g2_ref,
    prob_ref,
    router_ref,
    n2_ref,
    resid_ref,
    cot_ref,
    gain_ref,
    w_ref,
    dresid_ref,
    dattn_ref,
    dmix_ref,
    small_ref,
):

    @pl.when(pl.program_id(0) == 0)
    def _():
        small_ref[...] = jnp.zeros_like(small_ref)

    prob = prob_ref[...]
    expert = lax.broadcasted_iota(jnp.int32, prob.shape, 0)
    dprob = jnp.zeros_like(prob)
    for e, g_ref in enumerate((g0_ref, g1_ref, g2_ref)):
        dprob = jnp.where(expert == e, g_ref[0], dprob)
    dlogit = prob * (dprob - jnp.sum(dprob * prob, axis=0, keepdims=True))
    high, low = hi_lo(dlogit)
    dn2 = dot_first(high, router_ref[...]) + dot_first(low, router_ref[...])
    for e, d_ref in enumerate((d0_ref, d1_ref, d2_ref)):
        dn2 += dot(spread(col_ref, e), d_ref[0])
    n2 = n2_ref[...]
    small_ref[...] += dot(high, n2) + dot(low, n2)
    resid = resid_ref[...]
    scale = lax.rsqrt(jnp.mean(resid * resid, axis=-1, keepdims=True) + epsilon)
    weighted = dn2 * gain_ref[...]
    along = jnp.mean(weighted * resid, axis=-1, keepdims=True)
    dy = jnp.where(col_ref[:, E : E + 1] > 0, cot_ref[...].astype(f32), 0.0)
    dresid = dy + scale * weighted - resid * (scale * scale * scale * along)
    dresid_ref[...] = dresid
    dattn = dresid.astype(bf16)
    dattn_ref[...] = dattn
    dmix = dot_last(dattn[:, :BLK], w_ref[:, :rows, :].reshape(-1, BLK))
    for j in range(1, n):
        w = w_ref[:, j * rows : (j + 1) * rows, :].reshape(-1, BLK)
        dmix += dot_last(dattn[:, j * BLK : (j + 1) * BLK], w)
    dmix_ref[...] = dmix.astype(bf16)


def middle_call(cols, ds, dgates, prob, router, n2, resid, cot, gain, w_out, at, rows, n, n_seq, after=()):
    tokens, width = resid.shape
    per = tokens // n_seq // TILE
    tile = pl.BlockSpec((TILE, width), lambda i: (i, 0))
    row8 = pl.BlockSpec((8, TILE), lambda i: (0, i))
    return kernel_call(
        functools.partial(middle_kernel, rows, n),
        [cols, *ds, *dgates, prob, router, n2, resid, cot, gain, w_out],
        grid=(tokens // TILE,),
        in_specs=[pl.BlockSpec((TILE, 8), lambda i: (i, 0))]
        + [pl.BlockSpec((1, CAP, width), lambda i: (i // per, 0, 0))] * E
        + [pl.BlockSpec((1, 8, TILE), lambda i: (i // per, 0, i % per))] * E
        + [
            row8,
            whole((8, width)),
            tile,
            tile,
            tile,
            whole((1, width)),
            pl.BlockSpec((w_out.shape[0], n * rows, BLK), lambda i: (0, at, 0), pipeline_mode=pl.Buffered(1)),
        ],
        out_specs=[tile, tile, tile, pl.BlockSpec((8, width), lambda i: (0, 0))],
        out_shape=[
            jax.ShapeDtypeStruct((tokens, width), f32),
            jax.ShapeDtypeStruct((tokens, width), bf16),
            jax.ShapeDtypeStruct((tokens, width), bf16),
            jax.ShapeDtypeStruct((8, width), f32),
        ],
        cost_estimate=cost(2 * tokens * width * (width + E * CAP), 20 * tokens * width),
        name="middle",
        after=after,
    )


def weight_grad_kernel(rows, n_old, idx_ref, left_ref, right_ref, *refs):
    keep_ref, send_ref, turned_ref = refs[n_old:]
    c = idx_ref[0]
    width = left_ref.shape[1]
    step = 384
    per = step // (2 * rows)

    @pl.when(pl.program_id(0) == 0)
    def _():
        for m in range(width // step):
            turned_ref[m * step : (m + 1) * step, :] = left_ref[:, m * step : (m + 1) * step].T

    right = right_ref[...]
    for m in range(width // step):
        keep, send = split_cores(dot(turned_ref[m * step : (m + 1) * step, :], right), c, rows)
        keep_ref[m * per : (m + 1) * per] = keep
        send_ref[m * per : (m + 1) * per] = send


def weight_grad_call(core, left, right, rows, n_z, total, at, name, old=(), after=()):
    tokens, width = left.shape
    n = right.shape[1] // BLK
    out = pl.BlockSpec((n_z, rows, BLK), lambda j, _: (0, at + j, 0))
    shape = jax.ShapeDtypeStruct((n_z, total, BLK), bf16)
    return kernel_call(
        functools.partial(weight_grad_kernel, rows, len(old)),
        [core, left, right, *old],
        prefetch=1,
        grid=(n,),
        in_specs=[
            pl.BlockSpec((tokens, width), lambda j, _: (0, 0), pipeline_mode=pl.Buffered(1)),
            pl.BlockSpec((tokens, BLK), lambda j, _: (0, j)),
        ]
        + [pl.BlockSpec(memory_space=pl.ANY)] * len(old),
        out_specs=[out, out],
        scratch=[pltpu.VMEM((width, tokens), bf16)],
        out_shape=[shape, shape],
        cost_estimate=cost(2 * tokens * width * n * BLK, 2 * width * n * BLK + 4 * tokens * width),
        aliases={3 + i: i for i in range(len(old))},
        name=name,
        after=after,
    )


def input_grad_kernel(rows, n, d_ref, w_ref, x_ref, dresid_ref, gain_ref, out_ref):
    dn1 = dot_last(d_ref[:, :BLK], w_ref[:, :rows, :].reshape(-1, BLK))
    for j in range(1, n):
        w = w_ref[:, j * rows : (j + 1) * rows, :].reshape(-1, BLK)
        dn1 += dot_last(d_ref[:, j * BLK : (j + 1) * BLK], w)
    x = x_ref[...].astype(f32)
    scale = lax.rsqrt(jnp.mean(x * x, axis=-1, keepdims=True) + epsilon)
    weighted = dn1 * gain_ref[...]
    along = jnp.mean(weighted * x, axis=-1, keepdims=True)
    out = dresid_ref[...] + scale * weighted - x * (scale * scale * scale * along)
    out_ref[...] = out.astype(bf16)


def input_grad_call(dqkv, w_in, x, dresid, gain, rows, n, after=()):
    tokens, width = x.shape
    tile = pl.BlockSpec((TILE, width), lambda i: (i, 0))
    return kernel_call(
        functools.partial(input_grad_kernel, rows, n),
        [dqkv, w_in, x, dresid, gain],
        grid=(tokens // TILE,),
        in_specs=[
            pl.BlockSpec((TILE, n * BLK), lambda i: (i, 0)),
            whole((w_in.shape[0], n * rows, BLK)),
            tile,
            tile,
            whole((1, width)),
        ],
        out_specs=tile,
        out_shape=jax.ShapeDtypeStruct((tokens, width), bf16),
        cost_estimate=cost(2 * tokens * width * n * BLK, 2 * width * n * BLK + 12 * tokens * width),
        name="input_grad",
        after=after,
    )


def adam_step(master, first, second, gradient, clip, decayed):
    clipped = gradient * clip
    first_new = beta_first * first + (1.0 - beta_first) * clipped
    second_new = beta_second * second + (1.0 - beta_second) * clipped * clipped
    first_hat = first_new * (1.0 / (1.0 - beta_first**STEP))
    second_hat = second_new * (1.0 / (1.0 - beta_second**STEP))
    change = first_hat / (jnp.sqrt(second_hat) + adam_floor) + decayed * weight_decay * master
    update = -learn_rate * change
    return (gradient, update, first_new, second_new)


def adam_kernel(scale, which, clip_ref, g_ref, master_ref, first_ref, second_ref, *outs):
    gradient = g_ref[...].astype(f32) * scale
    results = adam_step(master_ref[...], first_ref[...], second_ref[...], gradient, clip_ref[0, which], 1.0)
    for out, result in zip(outs, results):
        out[...] = result


def adam_call(clip, which, packed, at, master, first, second, scale, name, after=()):
    rows, cols = master.shape
    natural = pl.BlockSpec((rows, BLK), lambda j, _: (0, j))
    shape = jax.ShapeDtypeStruct(master.shape, f32)
    return kernel_call(
        functools.partial(adam_kernel, scale, which),
        [clip, packed, master, first, second],
            prefetch=1,
            grid=(cols // BLK,),
            in_specs=[pl.BlockSpec((rows, BLK), lambda j, _: (at // rows + j, 0)), natural, natural, natural],
            out_specs=[natural] * 4,
        out_shape=[shape] * 4,
        cost_estimate=cost(20 * master.size, 30 * master.size),
        name=name,
        after=after,
    )


def adam_experts_kernel(scale, which, clip_ref, g0_ref, g1_ref, g2_ref, master_ref, first_ref, second_ref, *outs):
    for e, g_ref in enumerate((g0_ref, g1_ref, g2_ref)):

        @pl.when(pl.program_id(0) == e)
        def _():
            gradient = g_ref[...].astype(f32) * scale
            results = adam_step(master_ref[0], first_ref[0], second_ref[0], gradient, clip_ref[0, which], 1.0)
            for out, result in zip(outs, results):
                out[0] = result


def adam_experts_call(clip, which, packed, at, master, first, second, scale, name, after=()):
    _, rows, cols = master.shape
    n = cols // BLK
    natural = pl.BlockSpec((1, rows, BLK), lambda e, j, _: (e, 0, j))
    shape = jax.ShapeDtypeStruct(master.shape, f32)

    def g_spec(own):
        return pl.BlockSpec(
            (rows, BLK), lambda e, j, _: (at // rows + jnp.where(e < own, 0, jnp.where(e > own, n - 1, j)), 0)
        )

    return kernel_call(
        functools.partial(adam_experts_kernel, scale, which),
        [clip, *packed, master, first, second],
            prefetch=1,
            grid=(E, n),
            in_specs=[g_spec(e) for e in range(E)] + [natural] * 3,
            out_specs=[natural] * 4,
        out_shape=[shape] * 4,
        cost_estimate=cost(20 * master.size, 30 * master.size),
        name=name,
        after=after,
    )


def per_device(
    tokens,
    cotangent,
    lengths,
    routes,
    slot_index,
    norm_gains,
    norm_first,
    norm_second,
    in_proj,
    in_first,
    in_second,
    out_proj,
    out_first,
    out_second,
    router,
    router_first,
    router_second,
    up_proj,
    up_first,
    up_second,
    down_proj,
    down_first,
    down_second,
):
    n_rep, n_f = lax.axis_size("replica"), lax.axis_size("fsdp")
    n_z = n_f // 2
    n_mb, n_local, seq, width = tokens.shape
    n_seq = n_mb * n_local
    total_tokens = n_seq * seq
    unit = 16 * n_rep
    rows = in_proj.shape[0]
    down_rows = down_proj.shape[1]
    n_in, n_out, n_up, n_down = (w.shape[-1] // BLK for w in (in_proj, out_proj, up_proj, down_proj))
    core = (lax.axis_index("fsdp") % 2).astype(jnp.int32)[None]

    smalls = jnp.concatenate([norm_gains.astype(bf16), router.astype(bf16).T], axis=0)
    n_small = round_up(smalls.size, BLK) // BLK
    smalls = jnp.pad(smalls.reshape(-1), (0, 16 * BLK - smalls.size)).reshape(16, BLK)
    e_rows = n_up * rows + n_down * down_rows
    in_shard, in_mine = pack_call([(in_proj, None)], unit, smalls)
    mid_shard, _ = pack_call([(up_proj, 0), (down_proj, 0), (out_proj, None)], unit, after=[in_shard])
    late_shard, late_mine, mid_mine = pack_call(
        [(w, e) for e in range(1, E) for w in (up_proj, down_proj)], unit, before=mid_shard
    )
    g_in, g_mid, g_late = Gather(in_shard), Gather(mid_shard), Gather(late_shard)
    g_in.start(in_mine, True)
    g_in.own_c = swap_core(in_shard)
    g_in.stack(after=[late_shard, g_in.own_c])
    g_mid.start(hold(mid_mine, g_in.stacks), False)
    g_in.double(after=[late_shard])
    g_in.low_c = [swap_core(x) for x in hold(g_in.stacks, g_in.received)]
    g_mid.stack(after=g_in.received)
    w_in = g_in.assemble(after=g_mid.stacks)
    g_late.start(hold(late_mine, g_mid.pieces), False)

    small_all = w_in[:, n_in * rows : n_in * rows + n_small, :].reshape(n_f, n_small * BLK)[:, : 5 * rows]
    small_all = small_all.reshape(n_f, 5, rows).transpose(1, 0, 2).reshape(5, width)
    gain_one = small_all[0:1].astype(f32)
    gain_two = small_all[1:2].astype(f32)
    router8 = pad_rows(small_all[2:5], 8)

    length = lengths.reshape(n_seq).astype(jnp.int32)
    route = routes.reshape(n_seq, seq, 2)
    slot = slot_index.reshape(n_seq, seq, 2)
    live = jnp.arange(seq)[None, :] < length[:, None]
    kept = live[:, :, None] & (slot < CAP)
    slot_of = [
        jnp.max(jnp.where(kept & (route == e), slot, -1), axis=-1) for e in range(E)
    ]
    slot_rows = jnp.stack(slot_of + [live.astype(jnp.int32)] + [jnp.full_like(slot_of[0], -1)] * 4, axis=1)
    slot_cols = slot_rows.transpose(0, 2, 1).reshape(total_tokens, 8)

    x = tokens.reshape(total_tokens, width)
    cot = cotangent.reshape(total_tokens, width)

    qkv, n1 = qkv_call(x, gain_one, w_in, rows, n_in)
    g_mid.double(after=[qkv])
    g_mid.swap_early()
    probs, mixed = attention_call(length, qkv, n_seq, after=g_mid.stacks)
    g_mid.settle([mixed])
    g_late.stack(after=[mixed, *g_mid.received])
    w_mid = g_mid.assemble(after=g_late.stacks)
    w_at = e_rows // (n_out * rows)
    resid, n2, prob = resid_call(mixed, w_mid, w_at, x, gain_two, router8, rows, n_out)
    g_late.double(after=[resid])
    g_late.swap_early()
    buf, dys, gates = dispatch_call(slot_rows, prob, n2, cot, n_seq, after=g_late.stacks)

    def expert(e, w, at, after):
        return expert_call(e, at, core, buf, dys, gates, slot_rows, w, rows, down_rows, unit, after)

    y0, dbuf0, dgate0, keep0, send0 = expert(0, w_mid, 0, ())
    g_late.settle([y0])
    w_late = g_late.assemble(after=[y0])
    got0 = swap_core(hold(send0, g_late.high_c))
    total0 = pair_sum(keep0, hold(got0, [w_late]))
    part0 = lax.psum_scatter(total0, "fsdp", axis_index_groups=core_groups())
    y1, dbuf1, dgate1, keep1, send1 = expert(1, w_late, 0, [total0])
    got1 = swap_core(send1)
    y2, dbuf2, dgate2, keep2, send2 = expert(2, w_late, e_rows, [y1])
    sum1 = Reduce(keep1, got1, 0)
    sent = sum1.step([y2])
    got2 = swap_core(hold(send2, sent))

    dresid, dattn, dmixed, router_part = middle_call(
        slot_cols,
        (dbuf0, dbuf1, dbuf2),
        (dgate0, dgate1, dgate2),
        prob,
        router8,
        n2,
        resid,
        cot,
        gain_two,
        w_mid,
        w_at,
        rows,
        n_out,
        n_seq,
        after=sent,
    )
    io_rows = round_up((n_in + n_out) * rows + 16, unit)
    keep, send = weight_grad_call(core, mixed, dattn, rows, n_z, io_rows, n_in, "out_grad")
    router_part = router_part[:E].astype(bf16).reshape(E, n_z, 2, rows).transpose(2, 1, 0, 3)
    router_part = jnp.pad(router_part, ((0, 0), (0, 0), (0, 16 - E), (0, BLK - rows)))
    at = (0, (n_in + n_out) * rows, 0)
    keep = lax.dynamic_update_slice(keep, lax.dynamic_index_in_dim(router_part, core[0], keepdims=False), at)
    send = lax.dynamic_update_slice(send, lax.dynamic_index_in_dim(router_part, 1 - core[0], keepdims=False), at)
    sum2 = Reduce(keep2, got2, 1)
    sent = sum1.step([send]) + sum2.step([send])
    dq, dk, dv = attention_back_call(qkv, probs, mixed, dmixed, n_seq, sent + [part0])
    sent = sum1.step([dq]) + sum2.step([dq])
    dqkv = jnp.concatenate([dq, dk, dv], axis=1)
    keep, send = weight_grad_call(core, n1, dqkv, rows, n_z, io_rows, 0, "in_grad", (keep, send), sent)
    sum2.newest = hold(sum2.newest, [send])
    got = swap_core(hold(send, sum2.newest))
    sum0 = lax.psum(part0, "replica")
    block_out = combine_call(slot_cols, resid, (y0, y1, y2), n_seq, [send])
    io_sum = Reduce(keep, hold(got, [block_out]), 0)
    sent = io_sum.step()
    input_grad = input_grad_call(dqkv, w_in, x, dresid, gain_one, rows, n_in, sent)
    io_sum.newest = hold(io_sum.newest, [input_grad])
    sent = io_sum.step()
    sum1.newest = hold(sum1.newest, sent)
    sent = sum2.step(sum1.newest)
    io_sum.newest = hold(io_sum.newest, sent)
    sent = sum1.step(io_sum.newest)
    sum2.newest = hold(sum2.newest, sent)
    sent = io_sum.step(sum2.newest)
    sent = sum2.step(sent)
    sent = sum1.step(sent)
    sent = sum2.step(sent)
    sums = [hold(sum0, sent), sum1.result(sent), sum2.result(sent)]

    grad_scale = 1.0 / (n_seq * n_rep * n_f)
    weights = (norm_gains, in_proj, out_proj, router, up_proj, down_proj)
    counts = (2 * width,) + tuple(w.size * n_f for w in weights[1:])

    def square(packed):
        values = packed.astype(f32) * grad_scale
        return jnp.sum(values * values)

    def along_rows(shard, packed, n):
        both = shard[: n * rows].astype(f32) * packed[: n * rows].astype(f32)
        return jnp.sum(both.reshape(n, rows, BLK), axis=(0, 2)) * grad_scale

    def lanes(values):
        lane = lax.broadcasted_iota(jnp.int32, (8, 128), 1)
        return sum(jnp.where(lane == i, value, 0.0) for i, value in enumerate(values))

    def rms_and_clip(squares, which):
        rms = jnp.sqrt(squares * lanes([1.0 / counts[w] for w in which]) + epsilon)
        return rms, jnp.minimum(1.0, clip_level / rms)

    at_down = n_up * rows
    up_square = sum(square(s[:at_down]) for s in sums) / n_rep
    down_square = sum(square(s[at_down:e_rows]) for s in sums) / n_rep
    gains_low = norm_gains.astype(bf16).astype(f32)
    shards = (mid_shard, late_shard, late_shard[e_rows:])
    gain_two_grad = sum(along_rows(shard, packed, n_up) for shard, packed in zip(shards, sums))

    here = io_sum.sum_here([up_square, down_square, gain_two_grad])
    row = lax.axis_index("replica") * here.shape[0] + lax.broadcasted_iota(jnp.int32, (here.shape[0], 1), 0)
    lane = lax.broadcasted_iota(jnp.int32, (1, BLK), 1)
    ends = (n_in * rows, (n_in + n_out) * rows)
    values = here.astype(f32) * grad_scale
    values = values * values
    spread_squares = [
        jnp.sum(jnp.where(row < ends[0], values, 0.0)),
        jnp.sum(jnp.where((row >= ends[0]) & (row < ends[1]), values, 0.0)),
        jnp.sum(jnp.where((row >= ends[1]) & (row < ends[1] + E) & (lane < rows), values, 0.0)),
    ]
    squares = lanes(spread_squares + [up_square, down_square])
    for bit in bit_order(0):
        squares = squares + swap_replica(squares, bit)
    io_sum.have = hold(io_sum.have, [squares])
    sent = io_sum.step()
    all_rms, all_clip = rms_and_clip(sum_small(hold(squares, sent)), (1, 2, 3, 4, 5))
    sent = io_sum.step([all_clip])
    down_res = adam_experts_call(
        hold(all_clip, sent), 4, sums, at_down, down_proj, down_first, down_second, grad_scale, "down_adam"
    )
    up_res = adam_experts_call(
        hold(all_clip, [down_res[1]]), 3, sums, 0, up_proj, up_first, up_second, grad_scale, "up_adam"
    )
    total = io_sum.result([up_res[1]])
    in_sum = total[: ends[0]]
    router_grad = total[ends[1] : ends[1] + E, :rows].astype(f32) * grad_scale
    gain_one_grad = along_rows(in_shard, in_sum, n_in) / gains_low[0]
    gain_two_grad = gain_two_grad + jnp.sum(router.astype(bf16).astype(f32).T * router_grad, axis=0)
    gain_two_grad = gain_two_grad / gains_low[1]
    gain_grad = jnp.stack([gain_one_grad, gain_two_grad])
    squares = lanes([jnp.sum(gain_grad * gain_grad)])
    out_res = adam_call(
        hold(all_clip, [squares]), 1, total, ends[0], out_proj, out_first, out_second, grad_scale, "out_adam"
    )
    squares = squares + hold(swap_core(squares), [out_res[1]])
    in_res = adam_call(
        hold(all_clip, [squares]), 0, total, 0, in_proj, in_first, in_second, grad_scale, "in_adam"
    )
    gain_rms, gain_clip = rms_and_clip(sum_small(squares, 2, [in_res[1]]), (0,))
    norm_res = adam_step(norm_gains, norm_first, norm_second, gain_grad, gain_clip[0, 0], 0.0)
    router_res = adam_step(router, router_first, router_second, router_grad.T, all_clip[0, 2], 1.0)
    rms = jnp.concatenate([gain_rms[0, :1], all_rms[0, :5]])
    return (
        block_out.reshape(tokens.shape),
        input_grad.reshape(tokens.shape),
        rms[:5],
        rms[5:],
        *norm_res,
        *in_res,
        *out_res,
        *router_res,
        *up_res,
        *down_res,
    )


def solution(mesh):
    data = P(None, ("replica", "fsdp"), None, None)
    gains = P(None, "fsdp")
    flat = P("fsdp", None)
    experts = P(None, "fsdp", None)
    return jax.shard_map(
        per_device,
        mesh=mesh,
        in_specs=(data, data, P(None, ("replica", "fsdp")), data, data)
        + (gains,) * 3
        + (flat,) * 9
        + (experts,) * 6,
        out_specs=(data, data, P(), P()) + (gains,) * 4 + (flat,) * 12 + (experts,) * 8,
        check_vma=False,
    )
```

```python
import functools

import jax
import jax.numpy as jnp
from jax import lax
from jax.experimental import pallas as pl
from jax.experimental.pallas import tpu as pltpu
from jax.sharding import PartitionSpec as P

QUERY_HEADS = 24
KEY_VALUE_HEADS = 8
HEAD_SIZE = 64
FE = 1024
E = 3
STEP = 10
CAP = 320
BLK = 512

epsilon = 1e-06
beta_first = 0.9
beta_second = 0.95
learn_rate = 0.02
weight_decay = 0.1
adam_floor = 1e-08
clip_level = 0.005

bf16 = jnp.bfloat16
f32 = jnp.float32

LAST = (((1,), (1,)), ((), ()))
FIRST = (((0,), (0,)), ((), ()))


def dot(a, b):
    return jnp.dot(a, b, preferred_element_type=f32)


def dot_last(a, b):
    return lax.dot_general(a, b, LAST, preferred_element_type=f32)


def dot_first(a, b):
    return lax.dot_general(a, b, FIRST, preferred_element_type=f32)


def params(mib=56):
    return pltpu.CompilerParams(vmem_limit_bytes=mib * 1024 * 1024)


def cost(flops, nbytes):
    return pl.CostEstimate(flops=int(flops) // 1000000000, bytes_accessed=int(nbytes) // 1000000, transcendentals=0)


def whole(shape, space=None):
    zeros = (0,) * len(shape)
    return pl.BlockSpec(shape, lambda *_: zeros, pipeline_mode=pl.Buffered(1))


def hold(values, after):
    if not after:
        return values
    return lax.optimization_barrier((values, list(after)))[0]


def kernel_call(
    kernel, args, *, grid, in_specs, out_specs, out_shape, name, cost_estimate, prefetch=0, scratch=(), after=(), mib=56, aliases=None
):
    args = list(args)
    args[0] = hold(args[0], after)
    return pl.pallas_call(
        kernel,
        grid_spec=pltpu.PrefetchScalarGridSpec(
            num_scalar_prefetch=prefetch,
            grid=grid,
            in_specs=list(in_specs),
            out_specs=out_specs,
            scratch_shapes=list(scratch),
        ),
        out_shape=out_shape,
        compiler_params=params(mib),
        cost_estimate=cost_estimate,
        input_output_aliases=aliases or {},
        name=name,
    )(*args)


def round_up(n, m):
    return -(-n // m) * m


def shift_core_pairs(x, k):
    size = lax.axis_size("fsdp")
    return lax.ppermute(x, "fsdp", [(i, (i + 2 * k) % size) for i in range(size)])


def core_groups():
    size = lax.axis_size("fsdp")
    return [list(range(c, size, 2)) for c in range(2)]


def swap_core(x):
    size = lax.axis_size("fsdp")
    return lax.ppermute(x, "fsdp", [(i, i ^ 1) for i in range(size)])


def swap_replica(x, bit):
    size = lax.axis_size("replica")
    return lax.ppermute(x, "replica", [(i, i ^ bit) for i in range(size)])


def bit_order(first):
    bits = []
    while (1 << len(bits)) < lax.axis_size("replica"):
        bits.append(1 << len(bits))
    return bits[first % len(bits) :] + bits[: first % len(bits)]


def stack_kernel(cuts, n_z, z_ref, *refs):
    pieces, outs = refs[: -len(cuts)], refs[-len(cuts) :]
    for (at, size), out in zip(cuts, outs):
        for k in range(1, n_z):
            if len(pieces) > 1:
                out[0, k - 1] = pieces[k - 1][at : at + size, :]
            else:
                out[0, k - 1] = pieces[0][lax.rem(z_ref[0] + n_z - k, n_z), at : at + size, :]


def assemble_kernel(masks, n_z, cuts, rows, idx_ref, *refs):
    n_in = 2 * (1 + 2 * len(cuts))
    out, sems, held = refs[n_in:]
    part, z, c = idx_ref[0], idx_ref[1], idx_ref[2]
    half = len(masks[0]) // 2
    blocks, count = [], 0
    for ins, core in ((refs[: n_in // 2], c), (refs[n_in // 2 : n_in], 1 - c)):
        for k in range(n_z):
            at_block = 2 * lax.rem(z + n_z - k, n_z) + core
            found = []
            if k == 0:
                found.append((ins[0], held.at[at_block]))
            else:
                for i, (offset, size) in enumerate(cuts):
                    for j, mask in enumerate(masks[i]):
                        at = pl.multiple_of((part ^ mask) * rows + offset, 16)
                        found.append(
                            (ins[1 + 2 * i + j // half].at[j % half, k - 1], held.at[at_block, pl.ds(at, size)])
                        )
            copies = [pltpu.make_async_copy(a, b, sems.at[count + i]) for i, (a, b) in enumerate(found)]
            count += len(copies)
            for copy in copies:
                copy.start()
            blocks.append((at_block, copies))
    written = []
    for i, (at_block, copies) in enumerate(blocks):
        for copy in copies:
            copy.wait()
        copy = pltpu.make_async_copy(held.at[at_block], out.at[at_block], sems.at[count + i])
        copy.start()
        written.append(copy)
    for copy in written:
        copy.wait()


class Gather:
    def __init__(self, shard):
        self.shard = shard
        self.n_z = lax.axis_size("fsdp") // 2
        self.rows = shard.shape[0] // lax.axis_size("replica")
        half = round_up(self.rows // 2, 16)
        self.cuts = ((0, half), (half, self.rows - half))
        self.orders = [bit_order(i) for i in range(len(self.cuts))]
        self.masks = [[0] for _ in self.cuts]

    def start(self, mine, direct):
        if direct:
            self.pieces = [shift_core_pairs(mine, k) for k in range(1, self.n_z)]
        else:
            self.pieces = [lax.all_gather(mine, "fsdp", axis_index_groups=core_groups())]

    def stack(self, after=()):
        in_specs = [pl.BlockSpec(p.shape, (lambda i, _: (0, 0, 0)) if p.ndim == 3 else (lambda i, _: (0, 0))) for p in self.pieces]
        shapes = [(1, self.n_z - 1, size, BLK) for _, size in self.cuts]
        self.stacks = kernel_call(
            functools.partial(stack_kernel, self.cuts, self.n_z),
            [(lax.axis_index("fsdp") // 2).astype(jnp.int32)[None], *self.pieces],
            prefetch=1,
            grid=(1,),
            in_specs=in_specs,
            out_specs=[pl.BlockSpec(shape, lambda i, _: (0, 0, 0, 0)) for shape in shapes],
            out_shape=[jax.ShapeDtypeStruct(shape, bf16) for shape in shapes],
            name="stack",
            cost_estimate=cost(0, 4 * self.rows * BLK * (self.n_z - 1)),
            after=after,
        )
        self.swap(0)

    def swap(self, step):
        self.received = [swap_replica(x, order[step]) for x, order in zip(self.stacks, self.orders)]
        self.masks = [m + [v ^ order[step] for v in m] for m, order in zip(self.masks, self.orders)]

    def double(self, after=()):
        for step in range(1, len(self.orders[0])):
            arrived = hold(self.received, after)
            self.stacks = [jnp.concatenate(pair) for pair in zip(self.stacks, arrived)]
            self.swap(step)

    def swap_early(self):
        self.own_c = swap_core(self.shard)
        self.low_c = [swap_core(x) for x in self.stacks]

    def settle(self, after):
        self.received, self.own_c, self.low_c = hold((self.received, self.own_c, self.low_c), after)

    def assemble(self, after=()):
        place = lax.axis_index("fsdp")
        idx = jnp.stack([lax.axis_index("replica"), place // 2, place % 2]).astype(jnp.int32)
        ins = [self.shard]
        other = [self.own_c]
        high_c = self.high_c = [swap_core(x) for x in self.received]
        for pair in zip(self.stacks, self.received):
            ins += pair
        for pair in zip(self.low_c, high_c):
            other += pair
        n_f = lax.axis_size("fsdp")
        n_copies = 2 * (1 + len(self.cuts) * len(self.masks[0]) * (self.n_z - 1))
        anyspec = pl.BlockSpec(memory_space=pl.ANY)
        return kernel_call(
            functools.partial(assemble_kernel, self.masks, self.n_z, self.cuts, self.rows),
            [idx, *ins, *other],
            prefetch=1,
            grid=(1,),
            in_specs=[anyspec] * (2 * len(ins)),
            out_specs=anyspec,
            out_shape=jax.ShapeDtypeStruct((n_f,) + self.shard.shape, bf16),
            scratch=[
                pltpu.SemaphoreType.DMA((n_copies + n_f,)),
                pltpu.VMEM((n_f,) + self.shard.shape, bf16),
            ],
            name="assemble",
            cost_estimate=cost(0, 4 * n_f * self.shard.size),
            after=after,
        )


class Reduce:
    def __init__(self, keep, received, first=0):
        n_rep, self.n_z = lax.axis_size("replica"), lax.axis_size("fsdp") // 2
        self.part, self.z = lax.axis_index("replica"), lax.axis_index("fsdp") // 2
        self.rows = keep.shape[1] // n_rep
        n_bits = len(bit_order(0))
        self.bits = [1 << b for b in range(n_bits)]
        self.order = bit_order(first)
        shape = (self.n_z,) + (2,) * n_bits + (self.rows, BLK)
        half = round_up(self.rows // 2, 16)
        self.cuts = ((0, half), (half, self.rows - half))
        self.orders = [bit_order(i) for i in range(len(self.cuts))]
        self.live = [list(reversed(self.bits)) for _ in self.cuts]
        self.terms = [[keep.reshape(shape)] for _ in self.cuts]
        self.newest = [received.reshape(shape)]
        self.have = None
        halves = [functools.partial(self.halve, i) for i in range(n_bits)]
        gathers = [functools.partial(self.gather, i, bit) for i, bit in enumerate(self.order)]
        self.todo = [halves[:1], halves[1:], [self.along], gathers[:1], gathers[1:]]

    def step(self, after=()):
        self.newest = hold(self.newest, after)
        for action in self.todo.pop(0):
            sent = action()
        return sent

    def part_sum(self, terms):
        return functools.reduce(jnp.add, [t.astype(f32) for t in terms])

    def halve(self, i):
        news, marks = [], []
        for p, (at, size) in enumerate(self.cuts):
            self.terms[p] = self.terms[p] + [self.newest[p % len(self.newest)]]
            bit = self.orders[p][i]
            axis = 1 + self.live[p].index(bit)
            self.live[p].remove(bit)
            own = (self.part // bit) % 2

            def take(t, index):
                starts, sizes = [0] * t.ndim, list(t.shape)
                starts[axis], sizes[axis] = index, 1
                if i == 0:
                    starts[-2], sizes[-2] = at, size
                out = lax.dynamic_slice(t, starts, sizes)
                return out.reshape(out.shape[:axis] + out.shape[axis + 1 :])

            away = self.part_sum([take(t, 1 - own) for t in self.terms[p]]).astype(bf16)
            self.terms[p] = [take(t, own) for t in self.terms[p]]
            news.append(swap_replica(away, bit))
            marks.append(away)
        self.newest = news
        return marks

    def at_place(self, z):
        parts = [
            self.part_sum([lax.dynamic_index_in_dim(t, z, 0, keepdims=False) for t in terms]) for terms in self.terms
        ]
        return jnp.concatenate(parts)

    def along(self):
        self.terms = [terms + [new] for terms, new in zip(self.terms, self.newest)]
        aways = [self.at_place((self.z + k) % self.n_z).astype(bf16) for k in range(1, self.n_z)]
        self.newest = [shift_core_pairs(away, k) for k, away in enumerate(aways, 1)]
        return aways

    def sum_here(self, after=()):
        if self.have is None:
            summed = self.at_place(self.z)
            for got in hold(self.newest, after):
                summed = summed + got.astype(f32)
            self.have = summed.astype(bf16)
        return self.have

    def gather(self, i, bit):
        if i == 0:
            self.sum_here()
        else:
            self.have = self.joined()
        self.newest, self.bit = [swap_replica(self.have, bit)], bit
        return [self.have]

    def joined(self):
        pair = jnp.stack([self.have, self.newest[0]])
        return jnp.where((self.part // self.bit) % 2 == 1, pair[::-1], pair)

    def result(self, after=()):
        self.newest = hold(self.newest, after)
        stack = self.joined()
        names = list(reversed(self.order))
        n_bits = len(names)
        stack = jnp.transpose(stack, tuple(names.index(b) for b in reversed(self.bits)) + (n_bits, n_bits + 1))
        return stack.reshape(-1, BLK)


def pair_sum(keep, got):
    return (keep.astype(f32) + got.astype(f32)).astype(bf16)


def sum_small(x, bit=1, after=()):
    size = lax.axis_size("fsdp")
    while bit < size:
        x = x + hold(lax.ppermute(x, "fsdp", [(i, i ^ bit) for i in range(size)]), after)
        bit *= 2
        after = ()
    return x


def pack_kernel(counts, has_extra, has_before, prefix_ref, *refs):
    n = len(counts) + has_extra + has_before
    out = refs[n]
    at = 0
    for ref, count in zip(refs, counts):
        value = ref[0] if len(ref.shape) == 3 else ref[...]
        for j in range(count):
            out[at : at + value.shape[0], :] = value[:, j * BLK : (j + 1) * BLK].astype(bf16)
            at += value.shape[0]
    if has_extra:
        extra = refs[len(counts)][...]
        out[at : at + extra.shape[0], :] = extra
        at += extra.shape[0]
    if at < out.shape[0]:
        out[at:, :] = jnp.zeros((out.shape[0] - at, BLK), bf16)
    mine = refs[n + 1]
    rows = mine.shape[0]
    mine[...] = out[pl.ds(pl.multiple_of(prefix_ref[0] * rows, 16), rows), :]
    if has_before:
        refs[n + 2][...] = refs[n - 1][...]


def pack_call(parts, unit, extra=None, before=None, after=()):
    specs, counts, total = [], [], 0
    for w, e in parts:
        if e is None:
            specs.append(pl.BlockSpec(w.shape, lambda i, _: (0, 0)))
        else:
            specs.append(pl.BlockSpec((1,) + w.shape[1:], lambda i, _, e=e: (e, 0, 0)))
        counts.append(w.shape[-1] // BLK)
        total += counts[-1] * w.shape[-2]
    part = lax.axis_index("replica").astype(jnp.int32)[None]
    args = [part] + [w for w, _ in parts]
    if extra is not None:
        args.append(extra)
        specs.append(pl.BlockSpec(extra.shape, lambda i, _: (0, 0)))
        total += extra.shape[0]
    total = round_up(total, unit)
    n_rep = lax.axis_size("replica")
    shapes = [(total, BLK), (total // n_rep, BLK)]
    if before is not None:
        shapes.append((before.shape[0] // n_rep, BLK))
        args.append(before)
        specs.append(pl.BlockSpec(shapes[-1], lambda i, part: (part[0], 0)))
    return kernel_call(
        functools.partial(pack_kernel, tuple(counts), extra is not None, before is not None),
        args,
        prefetch=1,
        grid=(1,),
        in_specs=specs,
        out_specs=[pl.BlockSpec(shape, lambda i, _: (0, 0)) for shape in shapes],
        out_shape=[jax.ShapeDtypeStruct(shape, bf16) for shape in shapes],
        cost_estimate=cost(0, 6 * total * BLK),
        name="pack",
        after=after,
    )


def pad_rows(x, rows):
    return jnp.pad(x, ((0, rows - x.shape[0]), (0, 0)))


def qkv_kernel(x_ref, gain_ref, w_ref, qkv_ref, n1_ref):
    tokens, width = x_ref.shape

    @pl.when(pl.program_id(0) == 0)
    def _():
        def body(i, _):
            rows = pl.ds(pl.multiple_of(i * 128, 128), 128)
            xf = x_ref[rows, :].astype(f32)
            scale = lax.rsqrt(jnp.mean(xf * xf, axis=-1, keepdims=True) + epsilon)
            n1_ref[rows, :] = (xf * scale * gain_ref[...]).astype(bf16)
            return 0

        lax.fori_loop(0, tokens // 128, body, 0)

    w = w_ref[...].reshape(width, BLK)

    def body(i, _):
        rows = pl.ds(pl.multiple_of(i * 512, 512), 512)
        qkv_ref[rows, :] = dot(n1_ref[rows, :], w).astype(bf16)
        return 0

    lax.fori_loop(0, tokens // 512, body, 0)


def qkv_call(x, gain, w_in, rows, n, after=()):
    tokens, width = x.shape
    n_f = w_in.shape[0]
    return kernel_call(
        qkv_kernel,
        [x, gain, w_in],
        grid=(n,),
        in_specs=[
            whole((tokens, width)),
            whole((1, width)),
            pl.BlockSpec((n_f, rows, BLK), lambda j: (0, j, 0)),
        ],
        out_specs=[
            pl.BlockSpec((tokens, BLK), lambda j: (0, j)),
            pl.BlockSpec((tokens, width), lambda j: (0, 0)),
        ],
        out_shape=[
            jax.ShapeDtypeStruct((tokens, n * BLK), bf16),
            jax.ShapeDtypeStruct((tokens, width), bf16),
        ],
        cost_estimate=cost(2 * tokens * width * n * BLK, 2 * width * n * BLK + 4 * tokens * width),
        name="qkv",
        after=after,
    )


HALF = 256


def attention_kernel(len_ref, q_ref, k_ref, v_ref, p_ref, mix_ref):
    seq = q_ref.shape[0]
    length = len_ref[pl.program_id(0)]
    key = lax.broadcasted_iota(jnp.int32, (seq, seq), 0)
    query = lax.broadcasted_iota(jnp.int32, (seq, seq), 1)
    bias = jnp.where((key <= query) & (key < length), 0.0, -1000000000.0).astype(f32)
    group = QUERY_HEADS // KEY_VALUE_HEADS
    for h in range(2 * group):
        g = h // group
        lanes = slice(h * HEAD_SIZE, (h + 1) * HEAD_SIZE)
        kv = slice(g * HEAD_SIZE, (g + 1) * HEAD_SIZE)
        q = q_ref[:, lanes] * jnp.asarray(HEAD_SIZE ** (-0.5), bf16)
        for start in range(0, seq, HALF):
            stop = start + HALF
            s = dot_last(k_ref[:stop, kv], q[start:stop]) + bias[:stop, start:stop]
            raised = jnp.exp(s - jnp.max(s, axis=0, keepdims=True))
            probs = (raised * (1.0 / jnp.sum(raised, axis=0, keepdims=True))).astype(bf16)
            p_ref[0, h, :stop, start:stop] = probs
            mixed = dot_first(v_ref[:stop, kv], probs)
            mix_ref[start:stop, lanes] = mixed.T.astype(bf16)


def attention_call(lengths, qkv, n_seq, after=()):
    tokens = qkv.shape[0]
    seq = tokens // n_seq
    pairs = KEY_VALUE_HEADS // 2
    heads = QUERY_HEADS // pairs
    qw = heads * HEAD_SIZE
    kw = 2 * HEAD_SIZE
    k_at = QUERY_HEADS * HEAD_SIZE // kw
    v_at = k_at + pairs
    return kernel_call(
        attention_kernel,
        [lengths, qkv, qkv, qkv],
            prefetch=1,
            grid=(n_seq, pairs),
            in_specs=[
                pl.BlockSpec((seq, qw), lambda s, j, _: (s, j)),
                pl.BlockSpec((seq, kw), lambda s, j, _: (s, k_at + j)),
                pl.BlockSpec((seq, kw), lambda s, j, _: (s, v_at + j)),
            ],
            out_specs=[
                pl.BlockSpec((1, heads, seq, seq), lambda s, j, _: (s, j, 0, 0)),
                pl.BlockSpec((seq, qw), lambda s, j, _: (s, j)),
            ],
        out_shape=[
            jax.ShapeDtypeStruct((n_seq, QUERY_HEADS, seq, seq), bf16),
            jax.ShapeDtypeStruct((tokens, QUERY_HEADS * HEAD_SIZE), bf16),
        ],
        cost_estimate=cost(16 * n_seq * QUERY_HEADS * seq * seq * HEAD_SIZE, 2 * n_seq * QUERY_HEADS * seq * seq),
        name="attention",
        after=after,
    )


def attention_back_kernel(q_ref, k_ref, v_ref, p_ref, mix_ref, dmix_ref, dq_ref, dk_ref, dv_ref):
    seq = q_ref.shape[0]
    group = QUERY_HEADS // KEY_VALUE_HEADS
    scale = HEAD_SIZE ** (-0.5)
    ones = jnp.ones((8, HEAD_SIZE), bf16)
    for g in range(2):
        kv = slice(g * HEAD_SIZE, (g + 1) * HEAD_SIZE)
        k, v = k_ref[:, kv], v_ref[:, kv]
        n_half = seq // HALF
        dk = [jnp.zeros((HALF, HEAD_SIZE), f32) for _ in range(n_half)]
        dv = [jnp.zeros((HALF, HEAD_SIZE), f32) for _ in range(n_half)]
        for i in range(group):
            h = g * group + i
            lanes = slice(h * HEAD_SIZE, (h + 1) * HEAD_SIZE)
            for start in range(0, seq, HALF):
                stop = start + HALF
                dmix = dmix_ref[start:stop, lanes]
                q = q_ref[start:stop, lanes]
                both = dmix.astype(f32) * mix_ref[start:stop, lanes].astype(f32)
                high = both.astype(bf16)
                low = (both - high.astype(f32)).astype(bf16)
                delta = (dot_last(ones, high) + dot_last(ones, low))[:1]
                probs = p_ref[0, h, :stop, start:stop]
                dp = dot_last(v[:stop], dmix)
                ds = (probs.astype(f32) * (dp - delta)).astype(bf16)
                dq = dot_first(k[:stop], ds)
                dq_ref[start:stop, lanes] = (dq.T * scale).astype(bf16)
                dk_part = dot(ds, q)
                dv_part = dot(probs, dmix)
                for m in range(stop // HALF):
                    rows = slice(m * HALF, (m + 1) * HALF)
                    dk[m] += dk_part[rows]
                    dv[m] += dv_part[rows]
        for m in range(n_half):
            rows = slice(m * HALF, (m + 1) * HALF)
            dk_ref[rows, kv] = (dk[m] * scale).astype(bf16)
            dv_ref[rows, kv] = dv[m].astype(bf16)


def attention_back_call(qkv, probs, mixed, dmixed, n_seq, after=()):
    tokens = qkv.shape[0]
    seq = tokens // n_seq
    pairs = KEY_VALUE_HEADS // 2
    heads = QUERY_HEADS // pairs
    qw = heads * HEAD_SIZE
    kw = 2 * HEAD_SIZE
    k_at = QUERY_HEADS * HEAD_SIZE // kw
    v_at = k_at + pairs
    qspec = pl.BlockSpec((seq, qw), lambda s, j: (s, j))
    kspec = pl.BlockSpec((seq, kw), lambda s, j: (s, j))
    return kernel_call(
        attention_back_kernel,
        [qkv, qkv, qkv, probs, mixed, dmixed],
        grid=(n_seq, pairs),
        in_specs=[
            qspec,
            pl.BlockSpec((seq, kw), lambda s, j: (s, k_at + j)),
            pl.BlockSpec((seq, kw), lambda s, j: (s, v_at + j)),
            pl.BlockSpec((1, heads, seq, seq), lambda s, j: (s, j, 0, 0)),
            qspec,
            qspec,
        ],
        out_specs=[qspec, kspec, kspec],
        out_shape=[
            jax.ShapeDtypeStruct((tokens, QUERY_HEADS * HEAD_SIZE), bf16),
            jax.ShapeDtypeStruct((tokens, KEY_VALUE_HEADS * HEAD_SIZE), bf16),
            jax.ShapeDtypeStruct((tokens, KEY_VALUE_HEADS * HEAD_SIZE), bf16),
        ],
        cost_estimate=cost(32 * n_seq * QUERY_HEADS * seq * seq * HEAD_SIZE, 2 * n_seq * QUERY_HEADS * seq * seq),
        name="attention_back",
        after=after,
    )


TILE = 256
WIDE_TILE = 512


def resid_kernel(rows, n, mix_ref, w_ref, x_ref, gain_ref, router_ref, resid_ref, n2_ref, prob_ref):
    width = x_ref.shape[1]
    mixed = mix_ref[...]
    squares = jnp.zeros((WIDE_TILE, 1), f32)
    for j in range(n):
        cols = slice(j * BLK, (j + 1) * BLK)
        w = w_ref[:, j * rows : (j + 1) * rows, :].reshape(-1, BLK)
        part = x_ref[:, cols].astype(f32) + dot(mixed, w)
        resid_ref[:, cols] = part
        squares += jnp.sum(part * part, axis=-1, keepdims=True)
    scale = lax.rsqrt(squares * (1.0 / width) + epsilon)
    n2 = (resid_ref[...] * scale * gain_ref[...]).astype(bf16)
    n2_ref[...] = n2
    logits = dot_last(router_ref[...], n2)
    logits = jnp.where(lax.broadcasted_iota(jnp.int32, logits.shape, 0) < E, logits, -1e30)
    raised = jnp.exp(logits - jnp.max(logits, axis=0, keepdims=True))
    prob_ref[...] = raised / jnp.sum(raised, axis=0, keepdims=True)


def resid_call(mixed, w_out, at, x, gain, router, rows, n, after=()):
    tokens, width = x.shape
    tile = pl.BlockSpec((WIDE_TILE, width), lambda i: (i, 0))
    return kernel_call(
        functools.partial(resid_kernel, rows, n),
        [mixed, w_out, x, gain, router],
        grid=(tokens // WIDE_TILE,),
        in_specs=[
            tile,
            pl.BlockSpec((w_out.shape[0], n * rows, BLK), lambda i: (0, at, 0), pipeline_mode=pl.Buffered(1)),
            tile,
            whole((1, width)),
            whole((8, width)),
        ],
        out_specs=[tile, tile, pl.BlockSpec((8, WIDE_TILE), lambda i: (0, i))],
        out_shape=[
            jax.ShapeDtypeStruct((tokens, width), f32),
            jax.ShapeDtypeStruct((tokens, width), bf16),
            jax.ShapeDtypeStruct((8, tokens), f32),
        ],
        cost_estimate=cost(2 * tokens * width * width, 2 * width * width + 12 * tokens * width),
        name="resid",
        after=after,
    )


def dispatch_kernel(slot_ref, prob_ref, n2_ref, cot_ref, buf_ref, dys_ref, gate_ref):
    e = pl.program_id(1)
    slots = slot_ref[0, pl.ds(e, 1), :]
    hit = lax.broadcasted_iota(jnp.int32, (CAP, slots.shape[1]), 0) == slots
    gate = jnp.sum(jnp.where(hit, prob_ref[pl.ds(e, 1), :], 0.0), axis=-1, keepdims=True)
    gate_ref[0, 0] = jnp.broadcast_to(gate, (CAP, 128))
    hit = jnp.where(hit, 1.0, 0.0).astype(bf16)
    buf_ref[0, 0] = dot(hit, n2_ref[...]).astype(bf16)
    dys_ref[0, 0] = dot(hit, cot_ref[...]).astype(bf16)


def dispatch_call(slots, prob, n2, cot, n_seq, after=()):
    tokens, width = n2.shape
    seq = tokens // n_seq
    out = pl.BlockSpec((1, 1, CAP, width), lambda s, e: (e, s, 0, 0))
    return kernel_call(
        dispatch_kernel,
        [slots, prob, n2, cot],
        grid=(n_seq, E),
        in_specs=[
            pl.BlockSpec((1, 8, seq), lambda s, e: (s, 0, 0)),
            pl.BlockSpec((8, seq), lambda s, e: (0, s)),
            pl.BlockSpec((seq, width), lambda s, e: (s, 0)),
            pl.BlockSpec((seq, width), lambda s, e: (s, 0)),
        ],
        out_specs=[out, out, pl.BlockSpec((1, 1, CAP, 128), lambda s, e: (e, s, 0, 0))],
        out_shape=[
            jax.ShapeDtypeStruct((E, n_seq, CAP, width), bf16),
            jax.ShapeDtypeStruct((E, n_seq, CAP, width), bf16),
            jax.ShapeDtypeStruct((E, n_seq, CAP, 128), f32),
        ],
        cost_estimate=cost(4 * E * CAP * tokens * width, 20 * tokens * width),
        name="dispatch",
        after=after,
    )


def split_cores(block, c, rows):
    parts = block.reshape(-1, 2, rows, block.shape[-1])
    even, odd = parts[:, 0], parts[:, 1]
    return (
        jnp.where(c == 0, even, odd).astype(bf16),
        jnp.where(c == 0, odd, even).astype(bf16),
    )


def expert_kernel(
    e,
    up_rows,
    down_rows,
    idx_ref,
    buf_ref,
    dys_ref,
    gate_ref,
    slot_ref,
    up_a_ref,
    up_b_ref,
    down_ref,
    yg_ref,
    dbuf_ref,
    dgate_ref,
    keep_ref,
    send_ref,
    y_acc,
    d_acc,
    dyexp_ref,
    hid_ref,
    da_ref,
    db_ref,
    dg_acc,
    up_held,
    down_held,
    sems,
):
    h = pl.program_id(0)
    last = pl.num_programs(0) - 1
    c = idx_ref[0]
    n_seq = buf_ref.shape[1]
    width = buf_ref.shape[3]
    n_d = width // BLK
    up_a = up_a_ref[...].reshape(width, BLK)
    up_b = up_b_ref[...].reshape(width, BLK)
    downs = [down_ref[:, j * down_rows : (j + 1) * down_rows, :].reshape(BLK, BLK) for j in range(n_d)]
    for s in range(n_seq):
        rows = slice(s * CAP, (s + 1) * CAP)
        gate = gate_ref[0, s, :, :1]

        @pl.when(h == 0)
        def _():
            dyexp_ref[rows, :] = (gate * dys_ref[0, s].astype(f32)).astype(bf16)

        x = buf_ref[0, s]
        a = dot(x, up_a)
        b = dot(x, up_b)
        sigma = jax.nn.sigmoid(a)
        silu = a * sigma
        hid = (silu * b).astype(bf16)
        hid_ref[rows, :] = hid
        du = dot_last(dys_ref[0, s, :, :BLK], downs[0])
        for j in range(1, n_d):
            du += dot_last(dys_ref[0, s, :, j * BLK : (j + 1) * BLK], downs[j])
        dg = jnp.sum(du * hid.astype(f32), axis=-1, keepdims=True)
        dh = gate * du
        da = (dh * b * sigma * (1.0 + a * (1.0 - sigma))).astype(bf16)
        db = (dh * silu).astype(bf16)
        da_ref[rows, :] = da
        db_ref[rows, :] = db

        @pl.when(h == 0)
        def _():
            dg_acc[rows, :] = jnp.broadcast_to(dg, (CAP, 128))
            for j in range(n_d):
                y_acc[rows, j * BLK : (j + 1) * BLK] = dot(hid, downs[j])
            d_acc[rows, :] = dot_last(da, up_a) + dot_last(db, up_b)

        @pl.when(h > 0)
        def _():
            dg_acc[rows, :] += jnp.broadcast_to(dg, (CAP, 128))
            for j in range(n_d):
                y_acc[rows, j * BLK : (j + 1) * BLK] += dot(hid, downs[j])
            d_acc[rows, :] += dot_last(da, up_a) + dot_last(db, up_b)

        @pl.when(h == last)
        def _():
            yg_ref[s] = (gate * y_acc[rows, :]).astype(bf16)
            dbuf_ref[s] = d_acc[rows, :].astype(bf16)
            slots = slot_ref[s, e : e + 1, :]
            hit = lax.broadcasted_iota(jnp.int32, (CAP, slots.shape[1]), 0) == slots
            row = jnp.sum(jnp.where(hit, dg_acc[rows, :1], 0.0), axis=0, keepdims=True)
            dgate_ref[s] = jnp.broadcast_to(row, (8, slots.shape[1]))

    step = 384
    per = step // (2 * up_rows)

    for m in range(width // step):
        x = jnp.concatenate([buf_ref[0, s, :, m * step : (m + 1) * step] for s in range(n_seq)], axis=0)
        xt = x.T
        for i, d_ref in enumerate((da_ref, db_ref)):
            keep, send = split_cores(dot(xt, d_ref[...]), c, up_rows)
            up_held[h, 0, i, m * per : (m + 1) * per] = keep
            up_held[h, 1, i, m * per : (m + 1) * per] = send
    hid_t = hid_ref[...].T
    for j in range(n_d):
        keep, send = split_cores(dot(hid_t, dyexp_ref[:, j * BLK : (j + 1) * BLK]), c, down_rows)
        down_held[h, 0, :, j * down_rows : (j + 1) * down_rows, :] = keep
        down_held[h, 1, :, j * down_rows : (j + 1) * down_rows, :] = send
    n_h = FE // BLK
    n_zh = keep_ref.shape[0] // n_h

    def copies(step):
        found = []
        for side, ref in enumerate((keep_ref, send_ref)):
            for i in range(2):
                place = pl.ds((i * n_h + step) * up_rows, up_rows)
                found.append((up_held.at[step, side, i], ref.at[:, place, :]))
            place = pl.ds(2 * n_h * up_rows, n_d * down_rows)
            found.append((down_held.at[step, side], ref.at[step * n_zh : (step + 1) * n_zh, place, :]))
        return [pltpu.make_async_copy(a, b, sems.at[step, i]) for i, (a, b) in enumerate(found)]

    for step in range(n_h):

        @pl.when(h == step)
        def _():
            for copy in copies(step):
                copy.start()

    @pl.when(h == last)
    def _():
        for step in range(n_h):
            for copy in copies(step):
                copy.wait()


def expert_call(e, at, core, buf, dys, gates, slots, w, up_rows, down_rows, unit, after=()):
    _, n_seq, _, width = buf.shape
    n_f = w.shape[0]
    n_z = n_f // 2
    n_h = FE // BLK
    n_d = width // BLK
    seq = slots.shape[2]
    data = pl.BlockSpec((1, n_seq, CAP, width), lambda h, _: (e, 0, 0, 0), pipeline_mode=pl.Buffered(1))
    out = pl.BlockSpec((n_seq, CAP, width), lambda h, _: (0, 0, 0))
    anyspec = pl.BlockSpec(memory_space=pl.ANY)
    total = round_up(2 * n_h * up_rows + n_d * down_rows, unit)
    grad_shape = jax.ShapeDtypeStruct((n_z, total, BLK), bf16)
    rows = n_seq * CAP
    yg, dbuf, dgate, keep, send = kernel_call(
        functools.partial(expert_kernel, e, up_rows, down_rows),
        [core, buf, dys, gates, slots, w, w, w],
            prefetch=1,
            grid=(n_h,),
            in_specs=[
                data,
                data,
                pl.BlockSpec((1, n_seq, CAP, 128), lambda h, _: (e, 0, 0, 0)),
                pl.BlockSpec((n_seq, 8, seq), lambda h, _: (0, 0, 0)),
                pl.BlockSpec((n_f, up_rows, BLK), lambda h, _: (0, at // up_rows + h, 0)),
                pl.BlockSpec((n_f, up_rows, BLK), lambda h, _: (0, at // up_rows + n_h + h, 0)),
                pl.BlockSpec(
                    (n_f // n_h, n_d * down_rows, BLK),
                    lambda h, _: (h, (at + 2 * n_h * up_rows) // (n_d * down_rows), 0),
                ),
            ],
            out_specs=[
                out,
                out,
                pl.BlockSpec((n_seq, 8, seq), lambda h, _: (0, 0, 0)),
                anyspec,
                anyspec,
            ],
            scratch=[
                pltpu.VMEM((rows, width), f32),
                pltpu.VMEM((rows, width), f32),
                pltpu.VMEM((rows, width), bf16),
                pltpu.VMEM((rows, BLK), bf16),
                pltpu.VMEM((rows, BLK), bf16),
                pltpu.VMEM((rows, BLK), bf16),
                pltpu.VMEM((rows, 128), f32),
                pltpu.VMEM((n_h, 2, 2, n_z, up_rows, BLK), bf16),
                pltpu.VMEM((n_h, 2, n_z // n_h, n_d * down_rows, BLK), bf16),
                pltpu.SemaphoreType.DMA((n_h, 6)),
            ],
        out_shape=[
            jax.ShapeDtypeStruct((n_seq, CAP, width), bf16),
            jax.ShapeDtypeStruct((n_seq, CAP, width), bf16),
            jax.ShapeDtypeStruct((n_seq, 8, seq), f32),
            grad_shape,
            grad_shape,
        ],
        mib=60,
        cost_estimate=cost(18 * rows * width * FE, 40 * width * FE),
        name="expert",
        after=after,
    )
    return yg, dbuf, dgate, keep, send


def spread(col_ref, e):
    slots = col_ref[:, e : e + 1]
    hit = lax.broadcasted_iota(jnp.int32, (col_ref.shape[0], CAP), 1) == slots
    return jnp.where(hit, 1.0, 0.0).astype(bf16)


def combine_kernel(col_ref, resid_ref, y0_ref, y1_ref, y2_ref, out_ref):
    total = resid_ref[...]
    for e, y_ref in enumerate((y0_ref, y1_ref, y2_ref)):
        total += dot(spread(col_ref, e), y_ref[0])
    out_ref[...] = jnp.where(col_ref[:, E : E + 1] > 0, total, 0.0).astype(bf16)


def combine_call(cols, resid, ys, n_seq, after=()):
    tokens, width = resid.shape
    per = tokens // n_seq // TILE
    tile = pl.BlockSpec((TILE, width), lambda i: (i, 0))
    return kernel_call(
        combine_kernel,
        [cols, resid, *ys],
        grid=(tokens // TILE,),
        in_specs=[pl.BlockSpec((TILE, 8), lambda i: (i, 0)), tile]
        + [pl.BlockSpec((1, CAP, width), lambda i: (i // per, 0, 0))] * E,
        out_specs=tile,
        out_shape=jax.ShapeDtypeStruct((tokens, width), bf16),
        cost_estimate=cost(2 * E * CAP * tokens * width, 12 * tokens * width),
        name="combine",
        after=after,
    )


def hi_lo(x):
    high = x.astype(bf16)
    return high, (x - high.astype(f32)).astype(bf16)


def middle_kernel(
    rows,
    n,
    col_ref,
    d0_ref,
    d1_ref,
    d2_ref,
    g0_ref,
    g1_ref,
    g2_ref,
    prob_ref,
    router_ref,
    n2_ref,
    resid_ref,
    cot_ref,
    gain_ref,
    w_ref,
    dresid_ref,
    dattn_ref,
    dmix_ref,
    small_ref,
):

    @pl.when(pl.program_id(0) == 0)
    def _():
        small_ref[...] = jnp.zeros_like(small_ref)

    prob = prob_ref[...]
    expert = lax.broadcasted_iota(jnp.int32, prob.shape, 0)
    dprob = jnp.zeros_like(prob)
    for e, g_ref in enumerate((g0_ref, g1_ref, g2_ref)):
        dprob = jnp.where(expert == e, g_ref[0], dprob)
    dlogit = prob * (dprob - jnp.sum(dprob * prob, axis=0, keepdims=True))
    high, low = hi_lo(dlogit)
    dn2 = dot_first(high, router_ref[...]) + dot_first(low, router_ref[...])
    for e, d_ref in enumerate((d0_ref, d1_ref, d2_ref)):
        dn2 += dot(spread(col_ref, e), d_ref[0])
    n2 = n2_ref[...]
    small_ref[...] += dot(high, n2) + dot(low, n2)
    resid = resid_ref[...]
    scale = lax.rsqrt(jnp.mean(resid * resid, axis=-1, keepdims=True) + epsilon)
    weighted = dn2 * gain_ref[...]
    along = jnp.mean(weighted * resid, axis=-1, keepdims=True)
    dy = jnp.where(col_ref[:, E : E + 1] > 0, cot_ref[...].astype(f32), 0.0)
    dresid = dy + scale * weighted - resid * (scale * scale * scale * along)
    dresid_ref[...] = dresid
    dattn = dresid.astype(bf16)
    dattn_ref[...] = dattn
    dmix = dot_last(dattn[:, :BLK], w_ref[:, :rows, :].reshape(-1, BLK))
    for j in range(1, n):
        w = w_ref[:, j * rows : (j + 1) * rows, :].reshape(-1, BLK)
        dmix += dot_last(dattn[:, j * BLK : (j + 1) * BLK], w)
    dmix_ref[...] = dmix.astype(bf16)


def middle_call(cols, ds, dgates, prob, router, n2, resid, cot, gain, w_out, at, rows, n, n_seq, after=()):
    tokens, width = resid.shape
    per = tokens // n_seq // TILE
    tile = pl.BlockSpec((TILE, width), lambda i: (i, 0))
    row8 = pl.BlockSpec((8, TILE), lambda i: (0, i))
    return kernel_call(
        functools.partial(middle_kernel, rows, n),
        [cols, *ds, *dgates, prob, router, n2, resid, cot, gain, w_out],
        grid=(tokens // TILE,),
        in_specs=[pl.BlockSpec((TILE, 8), lambda i: (i, 0))]
        + [pl.BlockSpec((1, CAP, width), lambda i: (i // per, 0, 0))] * E
        + [pl.BlockSpec((1, 8, TILE), lambda i: (i // per, 0, i % per))] * E
        + [
            row8,
            whole((8, width)),
            tile,
            tile,
            tile,
            whole((1, width)),
            pl.BlockSpec((w_out.shape[0], n * rows, BLK), lambda i: (0, at, 0), pipeline_mode=pl.Buffered(1)),
        ],
        out_specs=[tile, tile, tile, pl.BlockSpec((8, width), lambda i: (0, 0))],
        out_shape=[
            jax.ShapeDtypeStruct((tokens, width), f32),
            jax.ShapeDtypeStruct((tokens, width), bf16),
            jax.ShapeDtypeStruct((tokens, width), bf16),
            jax.ShapeDtypeStruct((8, width), f32),
        ],
        cost_estimate=cost(2 * tokens * width * (width + E * CAP), 20 * tokens * width),
        name="middle",
        after=after,
    )


def weight_grad_kernel(rows, n_old, idx_ref, left_ref, right_ref, *refs):
    keep_ref, send_ref, turned_ref = refs[n_old:]
    c = idx_ref[0]
    width = left_ref.shape[1]
    step = 384
    per = step // (2 * rows)

    @pl.when(pl.program_id(0) == 0)
    def _():
        for m in range(width // step):
            turned_ref[m * step : (m + 1) * step, :] = left_ref[:, m * step : (m + 1) * step].T

    right = right_ref[...]
    for m in range(width // step):
        keep, send = split_cores(dot(turned_ref[m * step : (m + 1) * step, :], right), c, rows)
        keep_ref[m * per : (m + 1) * per] = keep
        send_ref[m * per : (m + 1) * per] = send


def weight_grad_call(core, left, right, rows, n_z, total, at, name, old=(), after=()):
    tokens, width = left.shape
    n = right.shape[1] // BLK
    out = pl.BlockSpec((n_z, rows, BLK), lambda j, _: (0, at + j, 0))
    shape = jax.ShapeDtypeStruct((n_z, total, BLK), bf16)
    return kernel_call(
        functools.partial(weight_grad_kernel, rows, len(old)),
        [core, left, right, *old],
        prefetch=1,
        grid=(n,),
        in_specs=[
            pl.BlockSpec((tokens, width), lambda j, _: (0, 0), pipeline_mode=pl.Buffered(1)),
            pl.BlockSpec((tokens, BLK), lambda j, _: (0, j)),
        ]
        + [pl.BlockSpec(memory_space=pl.ANY)] * len(old),
        out_specs=[out, out],
        scratch=[pltpu.VMEM((width, tokens), bf16)],
        out_shape=[shape, shape],
        cost_estimate=cost(2 * tokens * width * n * BLK, 2 * width * n * BLK + 4 * tokens * width),
        aliases={3 + i: i for i in range(len(old))},
        name=name,
        after=after,
    )


def input_grad_kernel(rows, n, d_ref, w_ref, x_ref, dresid_ref, gain_ref, out_ref):
    dn1 = dot_last(d_ref[:, :BLK], w_ref[:, :rows, :].reshape(-1, BLK))
    for j in range(1, n):
        w = w_ref[:, j * rows : (j + 1) * rows, :].reshape(-1, BLK)
        dn1 += dot_last(d_ref[:, j * BLK : (j + 1) * BLK], w)
    x = x_ref[...].astype(f32)
    scale = lax.rsqrt(jnp.mean(x * x, axis=-1, keepdims=True) + epsilon)
    weighted = dn1 * gain_ref[...]
    along = jnp.mean(weighted * x, axis=-1, keepdims=True)
    out = dresid_ref[...] + scale * weighted - x * (scale * scale * scale * along)
    out_ref[...] = out.astype(bf16)


def input_grad_call(dqkv, w_in, x, dresid, gain, rows, n, after=()):
    tokens, width = x.shape
    tile = pl.BlockSpec((WIDE_TILE, width), lambda i: (i, 0))
    return kernel_call(
        functools.partial(input_grad_kernel, rows, n),
        [dqkv, w_in, x, dresid, gain],
        grid=(tokens // WIDE_TILE,),
        in_specs=[
            pl.BlockSpec((WIDE_TILE, n * BLK), lambda i: (i, 0)),
            whole((w_in.shape[0], n * rows, BLK)),
            tile,
            tile,
            whole((1, width)),
        ],
        out_specs=tile,
        out_shape=jax.ShapeDtypeStruct((tokens, width), bf16),
        cost_estimate=cost(2 * tokens * width * n * BLK, 2 * width * n * BLK + 12 * tokens * width),
        name="input_grad",
        after=after,
    )


def adam_step(master, first, second, gradient, clip, decayed):
    clipped = gradient * clip
    first_new = beta_first * first + (1.0 - beta_first) * clipped
    second_new = beta_second * second + (1.0 - beta_second) * clipped * clipped
    first_hat = first_new * (1.0 / (1.0 - beta_first**STEP))
    second_hat = second_new * (1.0 / (1.0 - beta_second**STEP))
    change = first_hat / (jnp.sqrt(second_hat) + adam_floor) + decayed * weight_decay * master
    update = -learn_rate * change
    return (gradient, update, first_new, second_new)


def adam_kernel(scale, which, clip_ref, g_ref, master_ref, first_ref, second_ref, *outs):
    gradient = g_ref[...].astype(f32) * scale
    results = adam_step(master_ref[...], first_ref[...], second_ref[...], gradient, clip_ref[0, which], 1.0)
    for out, result in zip(outs, results):
        out[...] = result


def adam_call(clip, which, packed, at, master, first, second, scale, name, after=()):
    rows, cols = master.shape
    natural = pl.BlockSpec((rows, BLK), lambda j, _: (0, j))
    shape = jax.ShapeDtypeStruct(master.shape, f32)
    return kernel_call(
        functools.partial(adam_kernel, scale, which),
        [clip, packed, master, first, second],
            prefetch=1,
            grid=(cols // BLK,),
            in_specs=[pl.BlockSpec((rows, BLK), lambda j, _: (at // rows + j, 0)), natural, natural, natural],
            out_specs=[natural] * 4,
        out_shape=[shape] * 4,
        cost_estimate=cost(20 * master.size, 30 * master.size),
        name=name,
        after=after,
    )


def adam_experts_kernel(scale, which, clip_ref, g0_ref, g1_ref, g2_ref, master_ref, first_ref, second_ref, *outs):
    for e, g_ref in enumerate((g0_ref, g1_ref, g2_ref)):

        @pl.when(pl.program_id(0) == e)
        def _():
            gradient = g_ref[...].astype(f32) * scale
            results = adam_step(master_ref[0], first_ref[0], second_ref[0], gradient, clip_ref[0, which], 1.0)
            for out, result in zip(outs, results):
                out[0] = result


def adam_experts_call(clip, which, packed, at, master, first, second, scale, name, after=()):
    _, rows, cols = master.shape
    n = cols // BLK
    natural = pl.BlockSpec((1, rows, BLK), lambda e, j, _: (e, 0, j))
    shape = jax.ShapeDtypeStruct(master.shape, f32)

    def g_spec(own):
        return pl.BlockSpec(
            (rows, BLK), lambda e, j, _: (at // rows + jnp.where(e < own, 0, jnp.where(e > own, n - 1, j)), 0)
        )

    return kernel_call(
        functools.partial(adam_experts_kernel, scale, which),
        [clip, *packed, master, first, second],
            prefetch=1,
            grid=(E, n),
            in_specs=[g_spec(e) for e in range(E)] + [natural] * 3,
            out_specs=[natural] * 4,
        out_shape=[shape] * 4,
        cost_estimate=cost(20 * master.size, 30 * master.size),
        name=name,
        after=after,
    )


def per_device(
    tokens,
    cotangent,
    lengths,
    routes,
    slot_index,
    norm_gains,
    norm_first,
    norm_second,
    in_proj,
    in_first,
    in_second,
    out_proj,
    out_first,
    out_second,
    router,
    router_first,
    router_second,
    up_proj,
    up_first,
    up_second,
    down_proj,
    down_first,
    down_second,
):
    n_rep, n_f = lax.axis_size("replica"), lax.axis_size("fsdp")
    n_z = n_f // 2
    n_mb, n_local, seq, width = tokens.shape
    n_seq = n_mb * n_local
    total_tokens = n_seq * seq
    unit = 16 * n_rep
    rows = in_proj.shape[0]
    down_rows = down_proj.shape[1]
    n_in, n_out, n_up, n_down = (w.shape[-1] // BLK for w in (in_proj, out_proj, up_proj, down_proj))
    core = (lax.axis_index("fsdp") % 2).astype(jnp.int32)[None]

    smalls = jnp.concatenate([norm_gains.astype(bf16), router.astype(bf16).T], axis=0)
    n_small = round_up(smalls.size, BLK) // BLK
    smalls = jnp.pad(smalls.reshape(-1), (0, 16 * BLK - smalls.size)).reshape(16, BLK)
    e_rows = n_up * rows + n_down * down_rows
    in_shard, in_mine = pack_call([(in_proj, None)], unit, smalls)
    mid_shard, _ = pack_call([(up_proj, 0), (down_proj, 0), (out_proj, None)], unit, after=[in_shard])
    late_shard, late_mine, mid_mine = pack_call(
        [(w, e) for e in range(1, E) for w in (up_proj, down_proj)], unit, before=mid_shard
    )
    g_in, g_mid, g_late = Gather(in_shard), Gather(mid_shard), Gather(late_shard)
    g_in.start(in_mine, True)
    g_in.own_c = swap_core(in_shard)
    g_in.stack(after=[late_shard, g_in.own_c])
    g_mid.start(hold(mid_mine, g_in.stacks), False)
    g_in.double(after=[late_shard])
    g_in.low_c = [swap_core(x) for x in hold(g_in.stacks, g_in.received)]
    g_mid.stack(after=g_in.received)
    w_in = g_in.assemble(after=g_mid.stacks)
    g_late.start(hold(late_mine, g_mid.pieces), False)

    small_all = w_in[:, n_in * rows : n_in * rows + n_small, :].reshape(n_f, n_small * BLK)[:, : 5 * rows]
    small_all = small_all.reshape(n_f, 5, rows).transpose(1, 0, 2).reshape(5, width)
    gain_one = small_all[0:1].astype(f32)
    gain_two = small_all[1:2].astype(f32)
    router8 = pad_rows(small_all[2:5], 8)

    length = lengths.reshape(n_seq).astype(jnp.int32)
    route = routes.reshape(n_seq, seq, 2)
    slot = slot_index.reshape(n_seq, seq, 2)
    live = jnp.arange(seq)[None, :] < length[:, None]
    kept = live[:, :, None] & (slot < CAP)
    slot_of = [
        jnp.max(jnp.where(kept & (route == e), slot, -1), axis=-1) for e in range(E)
    ]
    slot_rows = jnp.stack(slot_of + [live.astype(jnp.int32)] + [jnp.full_like(slot_of[0], -1)] * 4, axis=1)
    slot_cols = slot_rows.transpose(0, 2, 1).reshape(total_tokens, 8)

    x = tokens.reshape(total_tokens, width)
    cot = cotangent.reshape(total_tokens, width)

    qkv, n1 = qkv_call(x, gain_one, w_in, rows, n_in)
    g_mid.double(after=[qkv])
    g_mid.swap_early()
    probs, mixed = attention_call(length, qkv, n_seq, after=g_mid.stacks)
    g_mid.settle([mixed])
    g_late.stack(after=[mixed, *g_mid.received])
    w_mid = g_mid.assemble(after=g_late.stacks)
    w_at = e_rows // (n_out * rows)
    resid, n2, prob = resid_call(mixed, w_mid, w_at, x, gain_two, router8, rows, n_out)
    g_late.double(after=[resid])
    g_late.swap_early()
    buf, dys, gates = dispatch_call(slot_rows, prob, n2, cot, n_seq, after=g_late.stacks)

    def expert(e, w, at, after):
        return expert_call(e, at, core, buf, dys, gates, slot_rows, w, rows, down_rows, unit, after)

    y0, dbuf0, dgate0, keep0, send0 = expert(0, w_mid, 0, ())
    g_late.settle([y0])
    w_late = g_late.assemble(after=[y0])
    got0 = swap_core(hold(send0, g_late.high_c))
    total0 = pair_sum(keep0, hold(got0, [w_late]))
    part0 = lax.psum_scatter(total0, "fsdp", axis_index_groups=core_groups())
    y1, dbuf1, dgate1, keep1, send1 = expert(1, w_late, 0, [total0])
    got1 = swap_core(send1)
    y2, dbuf2, dgate2, keep2, send2 = expert(2, w_late, e_rows, [y1])
    sum1 = Reduce(keep1, got1, 0)
    sent = sum1.step([y2])
    got2 = swap_core(hold(send2, sent))

    dresid, dattn, dmixed, router_part = middle_call(
        slot_cols,
        (dbuf0, dbuf1, dbuf2),
        (dgate0, dgate1, dgate2),
        prob,
        router8,
        n2,
        resid,
        cot,
        gain_two,
        w_mid,
        w_at,
        rows,
        n_out,
        n_seq,
        after=sent,
    )
    io_rows = round_up((n_in + n_out) * rows + 16, unit)
    keep, send = weight_grad_call(core, mixed, dattn, rows, n_z, io_rows, n_in, "out_grad")
    router_part = router_part[:E].astype(bf16).reshape(E, n_z, 2, rows).transpose(2, 1, 0, 3)
    router_part = jnp.pad(router_part, ((0, 0), (0, 0), (0, 16 - E), (0, BLK - rows)))
    at = (0, (n_in + n_out) * rows, 0)
    keep = lax.dynamic_update_slice(keep, lax.dynamic_index_in_dim(router_part, core[0], keepdims=False), at)
    send = lax.dynamic_update_slice(send, lax.dynamic_index_in_dim(router_part, 1 - core[0], keepdims=False), at)
    sum2 = Reduce(keep2, got2, 1)
    sent = sum1.step([send]) + sum2.step([send])
    dq, dk, dv = attention_back_call(qkv, probs, mixed, dmixed, n_seq, sent + [part0])
    sent = sum1.step([dq]) + sum2.step([dq])
    dqkv = jnp.concatenate([dq, dk, dv], axis=1)
    keep, send = weight_grad_call(core, n1, dqkv, rows, n_z, io_rows, 0, "in_grad", (keep, send), sent)
    sum2.newest = hold(sum2.newest, [send])
    got = swap_core(hold(send, sum2.newest))
    sum0 = lax.psum(part0, "replica")
    block_out = combine_call(slot_cols, resid, (y0, y1, y2), n_seq, [send])
    io_sum = Reduce(keep, hold(got, [block_out]), 0)
    sent = io_sum.step()
    input_grad = input_grad_call(dqkv, w_in, x, dresid, gain_one, rows, n_in, sent)
    io_sum.newest = hold(io_sum.newest, [input_grad])
    sent = io_sum.step()
    sum1.newest = hold(sum1.newest, sent)
    sent = sum2.step(sum1.newest)
    io_sum.newest = hold(io_sum.newest, sent)
    sent = sum1.step(io_sum.newest)
    sum2.newest = hold(sum2.newest, sent)
    sent = io_sum.step(sum2.newest)
    sent = sum2.step(sent)
    sent = sum1.step(sent)
    sent = sum2.step(sent)
    sums = [hold(sum0, sent), sum1.result(sent), sum2.result(sent)]

    grad_scale = 1.0 / (n_seq * n_rep * n_f)
    weights = (norm_gains, in_proj, out_proj, router, up_proj, down_proj)
    counts = (2 * width,) + tuple(w.size * n_f for w in weights[1:])

    def square(packed):
        values = packed.astype(f32) * grad_scale
        return jnp.sum(values * values)

    def along_rows(shard, packed, n):
        both = shard[: n * rows].astype(f32) * packed[: n * rows].astype(f32)
        return jnp.sum(both.reshape(n, rows, BLK), axis=(0, 2)) * grad_scale

    def lanes(values):
        lane = lax.broadcasted_iota(jnp.int32, (8, 128), 1)
        return sum(jnp.where(lane == i, value, 0.0) for i, value in enumerate(values))

    def rms_and_clip(squares, which):
        rms = jnp.sqrt(squares * lanes([1.0 / counts[w] for w in which]) + epsilon)
        return rms, jnp.minimum(1.0, clip_level / rms)

    at_down = n_up * rows
    up_square = sum(square(s[:at_down]) for s in sums) / n_rep
    down_square = sum(square(s[at_down:e_rows]) for s in sums) / n_rep
    gains_low = norm_gains.astype(bf16).astype(f32)
    shards = (mid_shard, late_shard, late_shard[e_rows:])
    gain_two_grad = sum(along_rows(shard, packed, n_up) for shard, packed in zip(shards, sums))

    here = io_sum.sum_here([up_square, down_square, gain_two_grad])
    row = lax.axis_index("replica") * here.shape[0] + lax.broadcasted_iota(jnp.int32, (here.shape[0], 1), 0)
    lane = lax.broadcasted_iota(jnp.int32, (1, BLK), 1)
    ends = (n_in * rows, (n_in + n_out) * rows)
    values = here.astype(f32) * grad_scale
    values = values * values
    spread_squares = [
        jnp.sum(jnp.where(row < ends[0], values, 0.0)),
        jnp.sum(jnp.where((row >= ends[0]) & (row < ends[1]), values, 0.0)),
        jnp.sum(jnp.where((row >= ends[1]) & (row < ends[1] + E) & (lane < rows), values, 0.0)),
    ]
    squares = lanes(spread_squares + [up_square, down_square])
    for bit in bit_order(0):
        squares = squares + swap_replica(squares, bit)
    io_sum.have = hold(io_sum.have, [squares])
    sent = io_sum.step()
    all_rms, all_clip = rms_and_clip(sum_small(hold(squares, sent)), (1, 2, 3, 4, 5))
    sent = io_sum.step([all_clip])
    down_res = adam_experts_call(
        hold(all_clip, sent), 4, sums, at_down, down_proj, down_first, down_second, grad_scale, "down_adam"
    )
    up_res = adam_experts_call(
        hold(all_clip, [down_res[1]]), 3, sums, 0, up_proj, up_first, up_second, grad_scale, "up_adam"
    )
    total = io_sum.result([up_res[1]])
    in_sum = total[: ends[0]]
    router_grad = total[ends[1] : ends[1] + E, :rows].astype(f32) * grad_scale
    gain_one_grad = along_rows(in_shard, in_sum, n_in) / gains_low[0]
    gain_two_grad = gain_two_grad + jnp.sum(router.astype(bf16).astype(f32).T * router_grad, axis=0)
    gain_two_grad = gain_two_grad / gains_low[1]
    gain_grad = jnp.stack([gain_one_grad, gain_two_grad])
    squares = lanes([jnp.sum(gain_grad * gain_grad)])
    out_res = adam_call(
        hold(all_clip, [squares]), 1, total, ends[0], out_proj, out_first, out_second, grad_scale, "out_adam"
    )
    squares = squares + hold(swap_core(squares), [out_res[1]])
    in_res = adam_call(
        hold(all_clip, [squares]), 0, total, 0, in_proj, in_first, in_second, grad_scale, "in_adam"
    )
    gain_rms, gain_clip = rms_and_clip(sum_small(squares, 2, [in_res[1]]), (0,))
    norm_res = adam_step(norm_gains, norm_first, norm_second, gain_grad, gain_clip[0, 0], 0.0)
    router_res = adam_step(router, router_first, router_second, router_grad.T, all_clip[0, 2], 1.0)
    rms = jnp.concatenate([gain_rms[0, :1], all_rms[0, :5]])
    return (
        block_out.reshape(tokens.shape),
        input_grad.reshape(tokens.shape),
        rms[:5],
        rms[5:],
        *norm_res,
        *in_res,
        *out_res,
        *router_res,
        *up_res,
        *down_res,
    )


def solution(mesh):
    data = P(None, ("replica", "fsdp"), None, None)
    gains = P(None, "fsdp")
    flat = P("fsdp", None)
    experts = P(None, "fsdp", None)
    return jax.shard_map(
        per_device,
        mesh=mesh,
        in_specs=(data, data, P(None, ("replica", "fsdp")), data, data)
        + (gains,) * 3
        + (flat,) * 9
        + (experts,) * 6,
        out_specs=(data, data, P(), P()) + (gains,) * 4 + (flat,) * 12 + (experts,) * 8,
        check_vma=False,
    )
```

```python
import functools

import jax
import jax.numpy as jnp
from jax import lax
from jax.experimental import pallas as pl
from jax.experimental.pallas import tpu as pltpu
from jax.sharding import PartitionSpec as P

QUERY_HEADS = 24
KEY_VALUE_HEADS = 8
HEAD_SIZE = 64
FE = 1024
E = 3
STEP = 10
CAP = 320
BLK = 512

epsilon = 1e-06
beta_first = 0.9
beta_second = 0.95
learn_rate = 0.02
weight_decay = 0.1
adam_floor = 1e-08
clip_level = 0.005

bf16 = jnp.bfloat16
f32 = jnp.float32

LAST = (((1,), (1,)), ((), ()))
FIRST = (((0,), (0,)), ((), ()))


def dot(a, b):
    return jnp.dot(a, b, preferred_element_type=f32)


def dot_last(a, b):
    return lax.dot_general(a, b, LAST, preferred_element_type=f32)


def dot_first(a, b):
    return lax.dot_general(a, b, FIRST, preferred_element_type=f32)


def params(mib=56):
    return pltpu.CompilerParams(vmem_limit_bytes=mib * 1024 * 1024)


def cost(flops, nbytes):
    return pl.CostEstimate(flops=int(flops) // 1000000000, bytes_accessed=int(nbytes) // 1000000, transcendentals=0)


def whole(shape, space=None):
    zeros = (0,) * len(shape)
    return pl.BlockSpec(shape, lambda *_: zeros, pipeline_mode=pl.Buffered(1))


def hold(values, after):
    if not after:
        return values
    return lax.optimization_barrier((values, list(after)))[0]


def kernel_call(
    kernel, args, *, grid, in_specs, out_specs, out_shape, name, cost_estimate, prefetch=0, scratch=(), after=(), mib=56, aliases=None
):
    args = list(args)
    args[0] = hold(args[0], after)
    return pl.pallas_call(
        kernel,
        grid_spec=pltpu.PrefetchScalarGridSpec(
            num_scalar_prefetch=prefetch,
            grid=grid,
            in_specs=list(in_specs),
            out_specs=out_specs,
            scratch_shapes=list(scratch),
        ),
        out_shape=out_shape,
        compiler_params=params(mib),
        cost_estimate=cost_estimate,
        input_output_aliases=aliases or {},
        name=name,
    )(*args)


def round_up(n, m):
    return -(-n // m) * m


def shift_core_pairs(x, k):
    size = lax.axis_size("fsdp")
    return lax.ppermute(x, "fsdp", [(i, (i + 2 * k) % size) for i in range(size)])


def core_groups():
    size = lax.axis_size("fsdp")
    return [list(range(c, size, 2)) for c in range(2)]


def swap_core(x):
    size = lax.axis_size("fsdp")
    return lax.ppermute(x, "fsdp", [(i, i ^ 1) for i in range(size)])


def swap_replica(x, bit):
    size = lax.axis_size("replica")
    return lax.ppermute(x, "replica", [(i, i ^ bit) for i in range(size)])


def bit_order(first):
    bits = []
    while (1 << len(bits)) < lax.axis_size("replica"):
        bits.append(1 << len(bits))
    return bits[first % len(bits) :] + bits[: first % len(bits)]


def stack_kernel(cuts, n_z, z_ref, *refs):
    pieces, outs = refs[: -len(cuts)], refs[-len(cuts) :]
    for (at, size), out in zip(cuts, outs):
        for k in range(1, n_z):
            if len(pieces) > 1:
                out[0, k - 1] = pieces[k - 1][at : at + size, :]
            else:
                out[0, k - 1] = pieces[0][lax.rem(z_ref[0] + n_z - k, n_z), at : at + size, :]


def assemble_kernel(masks, n_z, cuts, rows, idx_ref, *refs):
    n_in = 2 * (1 + 2 * len(cuts))
    out, sems, held = refs[n_in:]
    part, z, c = idx_ref[0], idx_ref[1], idx_ref[2]
    half = len(masks[0]) // 2
    blocks, count = [], 0
    for ins, core in ((refs[: n_in // 2], c), (refs[n_in // 2 : n_in], 1 - c)):
        for k in range(n_z):
            at_block = 2 * lax.rem(z + n_z - k, n_z) + core
            found = []
            if k == 0:
                found.append((ins[0], held.at[at_block]))
            else:
                for i, (offset, size) in enumerate(cuts):
                    for j, mask in enumerate(masks[i]):
                        at = pl.multiple_of((part ^ mask) * rows + offset, 16)
                        found.append(
                            (ins[1 + 2 * i + j // half].at[j % half, k - 1], held.at[at_block, pl.ds(at, size)])
                        )
            copies = [pltpu.make_async_copy(a, b, sems.at[count + i]) for i, (a, b) in enumerate(found)]
            count += len(copies)
            for copy in copies:
                copy.start()
            blocks.append((at_block, copies))
    written = []
    for i, (at_block, copies) in enumerate(blocks):
        for copy in copies:
            copy.wait()
        copy = pltpu.make_async_copy(held.at[at_block], out.at[at_block], sems.at[count + i])
        copy.start()
        written.append(copy)
    for copy in written:
        copy.wait()


class Gather:
    def __init__(self, shard):
        self.shard = shard
        self.n_z = lax.axis_size("fsdp") // 2
        self.rows = shard.shape[0] // lax.axis_size("replica")
        half = round_up(self.rows // 2, 16)
        self.cuts = ((0, half), (half, self.rows - half))
        self.orders = [bit_order(i) for i in range(len(self.cuts))]
        self.masks = [[0] for _ in self.cuts]

    def start(self, mine, direct):
        if direct:
            self.pieces = [shift_core_pairs(mine, k) for k in range(1, self.n_z)]
        else:
            self.pieces = [lax.all_gather(mine, "fsdp", axis_index_groups=core_groups())]

    def stack(self, after=()):
        in_specs = [pl.BlockSpec(p.shape, (lambda i, _: (0, 0, 0)) if p.ndim == 3 else (lambda i, _: (0, 0))) for p in self.pieces]
        shapes = [(1, self.n_z - 1, size, BLK) for _, size in self.cuts]
        self.stacks = kernel_call(
            functools.partial(stack_kernel, self.cuts, self.n_z),
            [(lax.axis_index("fsdp") // 2).astype(jnp.int32)[None], *self.pieces],
            prefetch=1,
            grid=(1,),
            in_specs=in_specs,
            out_specs=[pl.BlockSpec(shape, lambda i, _: (0, 0, 0, 0)) for shape in shapes],
            out_shape=[jax.ShapeDtypeStruct(shape, bf16) for shape in shapes],
            name="stack",
            cost_estimate=cost(0, 4 * self.rows * BLK * (self.n_z - 1)),
            after=after,
        )
        self.swap(0)

    def swap(self, step):
        self.received = [swap_replica(x, order[step]) for x, order in zip(self.stacks, self.orders)]
        self.masks = [m + [v ^ order[step] for v in m] for m, order in zip(self.masks, self.orders)]

    def double(self, after=()):
        for step in range(1, len(self.orders[0])):
            arrived = hold(self.received, after)
            self.stacks = [jnp.concatenate(pair) for pair in zip(self.stacks, arrived)]
            self.swap(step)

    def swap_early(self):
        self.own_c = swap_core(self.shard)
        self.low_c = [swap_core(x) for x in self.stacks]

    def settle(self, after):
        self.received, self.own_c, self.low_c = hold((self.received, self.own_c, self.low_c), after)

    def assemble(self, after=()):
        place = lax.axis_index("fsdp")
        idx = jnp.stack([lax.axis_index("replica"), place // 2, place % 2]).astype(jnp.int32)
        ins = [self.shard]
        other = [self.own_c]
        high_c = self.high_c = [swap_core(x) for x in self.received]
        for pair in zip(self.stacks, self.received):
            ins += pair
        for pair in zip(self.low_c, high_c):
            other += pair
        n_f = lax.axis_size("fsdp")
        n_copies = 2 * (1 + len(self.cuts) * len(self.masks[0]) * (self.n_z - 1))
        anyspec = pl.BlockSpec(memory_space=pl.ANY)
        return kernel_call(
            functools.partial(assemble_kernel, self.masks, self.n_z, self.cuts, self.rows),
            [idx, *ins, *other],
            prefetch=1,
            grid=(1,),
            in_specs=[anyspec] * (2 * len(ins)),
            out_specs=anyspec,
            out_shape=jax.ShapeDtypeStruct((n_f,) + self.shard.shape, bf16),
            scratch=[
                pltpu.SemaphoreType.DMA((n_copies + n_f,)),
                pltpu.VMEM((n_f,) + self.shard.shape, bf16),
            ],
            name="assemble",
            cost_estimate=cost(0, 4 * n_f * self.shard.size),
            after=after,
        )


class Reduce:
    def __init__(self, keep, received, first=0):
        n_rep, self.n_z = lax.axis_size("replica"), lax.axis_size("fsdp") // 2
        self.part, self.z = lax.axis_index("replica"), lax.axis_index("fsdp") // 2
        self.rows = keep.shape[1] // n_rep
        n_bits = len(bit_order(0))
        self.bits = [1 << b for b in range(n_bits)]
        self.order = bit_order(first)
        shape = (self.n_z,) + (2,) * n_bits + (self.rows, BLK)
        half = round_up(self.rows // 2, 16)
        self.cuts = ((0, half), (half, self.rows - half))
        self.orders = [bit_order(i) for i in range(len(self.cuts))]
        self.live = [list(reversed(self.bits)) for _ in self.cuts]
        self.terms = [[keep.reshape(shape)] for _ in self.cuts]
        self.newest = [received.reshape(shape)]
        self.have = None
        halves = [functools.partial(self.halve, i) for i in range(n_bits)]
        gathers = [functools.partial(self.gather, i, bit) for i, bit in enumerate(self.order)]
        self.todo = [halves[:1], halves[1:], [self.along], gathers[:1], gathers[1:]]

    def step(self, after=()):
        self.newest = hold(self.newest, after)
        for action in self.todo.pop(0):
            sent = action()
        return sent

    def part_sum(self, terms):
        return functools.reduce(jnp.add, [t.astype(f32) for t in terms])

    def halve(self, i):
        news, marks = [], []
        for p, (at, size) in enumerate(self.cuts):
            self.terms[p] = self.terms[p] + [self.newest[p % len(self.newest)]]
            bit = self.orders[p][i]
            axis = 1 + self.live[p].index(bit)
            self.live[p].remove(bit)
            own = (self.part // bit) % 2

            def take(t, index):
                starts, sizes = [0] * t.ndim, list(t.shape)
                starts[axis], sizes[axis] = index, 1
                if i == 0:
                    starts[-2], sizes[-2] = at, size
                out = lax.dynamic_slice(t, starts, sizes)
                return out.reshape(out.shape[:axis] + out.shape[axis + 1 :])

            away = self.part_sum([take(t, 1 - own) for t in self.terms[p]]).astype(bf16)
            self.terms[p] = [take(t, own) for t in self.terms[p]]
            news.append(swap_replica(away, bit))
            marks.append(away)
        self.newest = news
        return marks

    def at_place(self, z):
        parts = [
            self.part_sum([lax.dynamic_index_in_dim(t, z, 0, keepdims=False) for t in terms]) for terms in self.terms
        ]
        return jnp.concatenate(parts)

    def along(self):
        self.terms = [terms + [new] for terms, new in zip(self.terms, self.newest)]
        aways = [self.at_place((self.z + k) % self.n_z).astype(bf16) for k in range(1, self.n_z)]
        self.newest = [shift_core_pairs(away, k) for k, away in enumerate(aways, 1)]
        return aways

    def sum_here(self, after=()):
        if self.have is None:
            summed = self.at_place(self.z)
            for got in hold(self.newest, after):
                summed = summed + got.astype(f32)
            self.have = summed.astype(bf16)
        return self.have

    def gather(self, i, bit):
        if i == 0:
            self.sum_here()
        else:
            self.have = self.joined()
        self.newest, self.bit = [swap_replica(self.have, bit)], bit
        return [self.have]

    def joined(self):
        pair = jnp.stack([self.have, self.newest[0]])
        return jnp.where((self.part // self.bit) % 2 == 1, pair[::-1], pair)

    def result(self, after=()):
        self.newest = hold(self.newest, after)
        stack = self.joined()
        names = list(reversed(self.order))
        n_bits = len(names)
        stack = jnp.transpose(stack, tuple(names.index(b) for b in reversed(self.bits)) + (n_bits, n_bits + 1))
        return stack.reshape(-1, BLK)


def pair_sum(keep, got):
    return (keep.astype(f32) + got.astype(f32)).astype(bf16)


def sum_small(x, bit=1, after=()):
    size = lax.axis_size("fsdp")
    while bit < size:
        x = x + hold(lax.ppermute(x, "fsdp", [(i, i ^ bit) for i in range(size)]), after)
        bit *= 2
        after = ()
    return x


def pack_kernel(counts, has_extra, has_before, prefix_ref, *refs):
    n = len(counts) + has_extra + has_before
    out = refs[n]
    at = 0
    for ref, count in zip(refs, counts):
        value = ref[0] if len(ref.shape) == 3 else ref[...]
        for j in range(count):
            out[at : at + value.shape[0], :] = value[:, j * BLK : (j + 1) * BLK].astype(bf16)
            at += value.shape[0]
    if has_extra:
        extra = refs[len(counts)][...]
        out[at : at + extra.shape[0], :] = extra
        at += extra.shape[0]
    if at < out.shape[0]:
        out[at:, :] = jnp.zeros((out.shape[0] - at, BLK), bf16)
    mine = refs[n + 1]
    rows = mine.shape[0]
    mine[...] = out[pl.ds(pl.multiple_of(prefix_ref[0] * rows, 16), rows), :]
    if has_before:
        refs[n + 2][...] = refs[n - 1][...]


def pack_call(parts, unit, extra=None, before=None, after=()):
    specs, counts, total = [], [], 0
    for w, e in parts:
        if e is None:
            specs.append(pl.BlockSpec(w.shape, lambda i, _: (0, 0)))
        else:
            specs.append(pl.BlockSpec((1,) + w.shape[1:], lambda i, _, e=e: (e, 0, 0)))
        counts.append(w.shape[-1] // BLK)
        total += counts[-1] * w.shape[-2]
    part = lax.axis_index("replica").astype(jnp.int32)[None]
    args = [part] + [w for w, _ in parts]
    if extra is not None:
        args.append(extra)
        specs.append(pl.BlockSpec(extra.shape, lambda i, _: (0, 0)))
        total += extra.shape[0]
    total = round_up(total, unit)
    n_rep = lax.axis_size("replica")
    shapes = [(total, BLK), (total // n_rep, BLK)]
    if before is not None:
        shapes.append((before.shape[0] // n_rep, BLK))
        args.append(before)
        specs.append(pl.BlockSpec(shapes[-1], lambda i, part: (part[0], 0)))
    return kernel_call(
        functools.partial(pack_kernel, tuple(counts), extra is not None, before is not None),
        args,
        prefetch=1,
        grid=(1,),
        in_specs=specs,
        out_specs=[pl.BlockSpec(shape, lambda i, _: (0, 0)) for shape in shapes],
        out_shape=[jax.ShapeDtypeStruct(shape, bf16) for shape in shapes],
        cost_estimate=cost(0, 6 * total * BLK),
        name="pack",
        after=after,
    )


def pad_rows(x, rows):
    return jnp.pad(x, ((0, rows - x.shape[0]), (0, 0)))


def qkv_kernel(x_ref, gain_ref, w_ref, qkv_ref, n1_ref):
    tokens, width = x_ref.shape

    @pl.when(pl.program_id(0) == 0)
    def _():
        def body(i, _):
            rows = pl.ds(pl.multiple_of(i * 128, 128), 128)
            xf = x_ref[rows, :].astype(f32)
            scale = lax.rsqrt(jnp.mean(xf * xf, axis=-1, keepdims=True) + epsilon)
            n1_ref[rows, :] = (xf * scale * gain_ref[...]).astype(bf16)
            return 0

        lax.fori_loop(0, tokens // 128, body, 0)

    w = w_ref[...].reshape(width, BLK)

    def body(i, _):
        rows = pl.ds(pl.multiple_of(i * 512, 512), 512)
        qkv_ref[rows, :] = dot(n1_ref[rows, :], w).astype(bf16)
        return 0

    lax.fori_loop(0, tokens // 512, body, 0)


def qkv_call(x, gain, w_in, rows, n, after=()):
    tokens, width = x.shape
    n_f = w_in.shape[0]
    return kernel_call(
        qkv_kernel,
        [x, gain, w_in],
        grid=(n,),
        in_specs=[
            whole((tokens, width)),
            whole((1, width)),
            pl.BlockSpec((n_f, rows, BLK), lambda j: (0, j, 0)),
        ],
        out_specs=[
            pl.BlockSpec((tokens, BLK), lambda j: (0, j)),
            pl.BlockSpec((tokens, width), lambda j: (0, 0)),
        ],
        out_shape=[
            jax.ShapeDtypeStruct((tokens, n * BLK), bf16),
            jax.ShapeDtypeStruct((tokens, width), bf16),
        ],
        cost_estimate=cost(2 * tokens * width * n * BLK, 2 * width * n * BLK + 4 * tokens * width),
        name="qkv",
        after=after,
    )


HALF = 256


def attention_kernel(len_ref, q_ref, k_ref, v_ref, p_ref, mix_ref):
    seq = q_ref.shape[0]
    length = len_ref[pl.program_id(0)]
    key = lax.broadcasted_iota(jnp.int32, (seq, seq), 0)
    query = lax.broadcasted_iota(jnp.int32, (seq, seq), 1)
    bias = jnp.where((key <= query) & (key < length), 0.0, -1000000000.0).astype(f32)
    group = QUERY_HEADS // KEY_VALUE_HEADS
    for h in range(2 * group):
        g = h // group
        lanes = slice(h * HEAD_SIZE, (h + 1) * HEAD_SIZE)
        kv = slice(g * HEAD_SIZE, (g + 1) * HEAD_SIZE)
        q = q_ref[:, lanes] * jnp.asarray(HEAD_SIZE ** (-0.5), bf16)
        for start in range(0, seq, HALF):
            stop = start + HALF
            s = dot_last(k_ref[:stop, kv], q[start:stop]) + bias[:stop, start:stop]
            raised = jnp.exp(s - jnp.max(s, axis=0, keepdims=True))
            probs = (raised * (1.0 / jnp.sum(raised, axis=0, keepdims=True))).astype(bf16)
            p_ref[0, h, :stop, start:stop] = probs
            mixed = dot_first(v_ref[:stop, kv], probs)
            mix_ref[start:stop, lanes] = mixed.T.astype(bf16)


def attention_call(lengths, qkv, n_seq, after=()):
    tokens = qkv.shape[0]
    seq = tokens // n_seq
    pairs = KEY_VALUE_HEADS // 2
    heads = QUERY_HEADS // pairs
    qw = heads * HEAD_SIZE
    kw = 2 * HEAD_SIZE
    k_at = QUERY_HEADS * HEAD_SIZE // kw
    v_at = k_at + pairs
    return kernel_call(
        attention_kernel,
        [lengths, qkv, qkv, qkv],
            prefetch=1,
            grid=(n_seq, pairs),
            in_specs=[
                pl.BlockSpec((seq, qw), lambda s, j, _: (s, j)),
                pl.BlockSpec((seq, kw), lambda s, j, _: (s, k_at + j)),
                pl.BlockSpec((seq, kw), lambda s, j, _: (s, v_at + j)),
            ],
            out_specs=[
                pl.BlockSpec((1, heads, seq, seq), lambda s, j, _: (s, j, 0, 0)),
                pl.BlockSpec((seq, qw), lambda s, j, _: (s, j)),
            ],
        out_shape=[
            jax.ShapeDtypeStruct((n_seq, QUERY_HEADS, seq, seq), bf16),
            jax.ShapeDtypeStruct((tokens, QUERY_HEADS * HEAD_SIZE), bf16),
        ],
        cost_estimate=cost(16 * n_seq * QUERY_HEADS * seq * seq * HEAD_SIZE, 2 * n_seq * QUERY_HEADS * seq * seq),
        name="attention",
        after=after,
    )


def attention_back_kernel(q_ref, k_ref, v_ref, p_ref, mix_ref, dmix_ref, dq_ref, dk_ref, dv_ref):
    seq = q_ref.shape[0]
    group = QUERY_HEADS // KEY_VALUE_HEADS
    scale = HEAD_SIZE ** (-0.5)
    ones = jnp.ones((8, HEAD_SIZE), bf16)
    for g in range(2):
        kv = slice(g * HEAD_SIZE, (g + 1) * HEAD_SIZE)
        k, v = k_ref[:, kv], v_ref[:, kv]
        n_half = seq // HALF
        dk = [jnp.zeros((HALF, HEAD_SIZE), f32) for _ in range(n_half)]
        dv = [jnp.zeros((HALF, HEAD_SIZE), f32) for _ in range(n_half)]
        for i in range(group):
            h = g * group + i
            lanes = slice(h * HEAD_SIZE, (h + 1) * HEAD_SIZE)
            for start in range(0, seq, HALF):
                stop = start + HALF
                dmix = dmix_ref[start:stop, lanes]
                q = q_ref[start:stop, lanes]
                both = dmix.astype(f32) * mix_ref[start:stop, lanes].astype(f32)
                high = both.astype(bf16)
                low = (both - high.astype(f32)).astype(bf16)
                delta = (dot_last(ones, high) + dot_last(ones, low))[:1]
                probs = p_ref[0, h, :stop, start:stop]
                dp = dot_last(v[:stop], dmix)
                ds = (probs.astype(f32) * (dp - delta)).astype(bf16)
                dq = dot_first(k[:stop], ds)
                dq_ref[start:stop, lanes] = (dq.T * scale).astype(bf16)
                dk_part = dot(ds, q)
                dv_part = dot(probs, dmix)
                for m in range(stop // HALF):
                    rows = slice(m * HALF, (m + 1) * HALF)
                    dk[m] += dk_part[rows]
                    dv[m] += dv_part[rows]
        for m in range(n_half):
            rows = slice(m * HALF, (m + 1) * HALF)
            dk_ref[rows, kv] = (dk[m] * scale).astype(bf16)
            dv_ref[rows, kv] = dv[m].astype(bf16)


def attention_back_call(qkv, probs, mixed, dmixed, n_seq, after=()):
    tokens = qkv.shape[0]
    seq = tokens // n_seq
    pairs = KEY_VALUE_HEADS // 2
    heads = QUERY_HEADS // pairs
    qw = heads * HEAD_SIZE
    kw = 2 * HEAD_SIZE
    k_at = QUERY_HEADS * HEAD_SIZE // kw
    v_at = k_at + pairs
    qspec = pl.BlockSpec((seq, qw), lambda s, j: (s, j))
    kspec = pl.BlockSpec((seq, kw), lambda s, j: (s, j))
    return kernel_call(
        attention_back_kernel,
        [qkv, qkv, qkv, probs, mixed, dmixed],
        grid=(n_seq, pairs),
        in_specs=[
            qspec,
            pl.BlockSpec((seq, kw), lambda s, j: (s, k_at + j)),
            pl.BlockSpec((seq, kw), lambda s, j: (s, v_at + j)),
            pl.BlockSpec((1, heads, seq, seq), lambda s, j: (s, j, 0, 0)),
            qspec,
            qspec,
        ],
        out_specs=[qspec, kspec, kspec],
        out_shape=[
            jax.ShapeDtypeStruct((tokens, QUERY_HEADS * HEAD_SIZE), bf16),
            jax.ShapeDtypeStruct((tokens, KEY_VALUE_HEADS * HEAD_SIZE), bf16),
            jax.ShapeDtypeStruct((tokens, KEY_VALUE_HEADS * HEAD_SIZE), bf16),
        ],
        cost_estimate=cost(32 * n_seq * QUERY_HEADS * seq * seq * HEAD_SIZE, 2 * n_seq * QUERY_HEADS * seq * seq),
        name="attention_back",
        after=after,
    )


TILE = 256
WIDE_TILE = 512


def resid_kernel(rows, n, mix_ref, w_ref, x_ref, gain_ref, router_ref, resid_ref, n2_ref, prob_ref):
    width = x_ref.shape[1]
    mixed = mix_ref[...]
    squares = jnp.zeros((WIDE_TILE, 1), f32)
    for j in range(n):
        cols = slice(j * BLK, (j + 1) * BLK)
        w = w_ref[:, j * rows : (j + 1) * rows, :].reshape(-1, BLK)
        part = x_ref[:, cols].astype(f32) + dot(mixed, w)
        resid_ref[:, cols] = part
        squares += jnp.sum(part * part, axis=-1, keepdims=True)
    scale = lax.rsqrt(squares * (1.0 / width) + epsilon)
    n2 = (resid_ref[...] * scale * gain_ref[...]).astype(bf16)
    n2_ref[...] = n2
    logits = dot_last(router_ref[...], n2)
    logits = jnp.where(lax.broadcasted_iota(jnp.int32, logits.shape, 0) < E, logits, -1e30)
    raised = jnp.exp(logits - jnp.max(logits, axis=0, keepdims=True))
    prob_ref[...] = raised / jnp.sum(raised, axis=0, keepdims=True)


def resid_call(mixed, w_out, at, x, gain, router, rows, n, after=()):
    tokens, width = x.shape
    tile = pl.BlockSpec((WIDE_TILE, width), lambda i: (i, 0))
    return kernel_call(
        functools.partial(resid_kernel, rows, n),
        [mixed, w_out, x, gain, router],
        grid=(tokens // WIDE_TILE,),
        in_specs=[
            tile,
            pl.BlockSpec((w_out.shape[0], n * rows, BLK), lambda i: (0, at, 0), pipeline_mode=pl.Buffered(1)),
            tile,
            whole((1, width)),
            whole((8, width)),
        ],
        out_specs=[tile, tile, pl.BlockSpec((8, WIDE_TILE), lambda i: (0, i))],
        out_shape=[
            jax.ShapeDtypeStruct((tokens, width), f32),
            jax.ShapeDtypeStruct((tokens, width), bf16),
            jax.ShapeDtypeStruct((8, tokens), f32),
        ],
        cost_estimate=cost(2 * tokens * width * width, 2 * width * width + 12 * tokens * width),
        name="resid",
        after=after,
    )


def dispatch_kernel(slot_ref, prob_ref, n2_ref, cot_ref, buf_ref, dys_ref, gate_ref):
    e = pl.program_id(1)
    slots = slot_ref[0, pl.ds(e, 1), :]
    hit = lax.broadcasted_iota(jnp.int32, (CAP, slots.shape[1]), 0) == slots
    gate = jnp.sum(jnp.where(hit, prob_ref[pl.ds(e, 1), :], 0.0), axis=-1, keepdims=True)
    gate_ref[0, 0] = jnp.broadcast_to(gate, (CAP, 128))
    hit = jnp.where(hit, 1.0, 0.0).astype(bf16)
    buf_ref[0, 0] = dot(hit, n2_ref[...]).astype(bf16)
    dys_ref[0, 0] = dot(hit, cot_ref[...]).astype(bf16)


def dispatch_call(slots, prob, n2, cot, n_seq, after=()):
    tokens, width = n2.shape
    seq = tokens // n_seq
    out = pl.BlockSpec((1, 1, CAP, width), lambda s, e: (e, s, 0, 0))
    return kernel_call(
        dispatch_kernel,
        [slots, prob, n2, cot],
        grid=(n_seq, E),
        in_specs=[
            pl.BlockSpec((1, 8, seq), lambda s, e: (s, 0, 0)),
            pl.BlockSpec((8, seq), lambda s, e: (0, s)),
            pl.BlockSpec((seq, width), lambda s, e: (s, 0)),
            pl.BlockSpec((seq, width), lambda s, e: (s, 0)),
        ],
        out_specs=[out, out, pl.BlockSpec((1, 1, CAP, 128), lambda s, e: (e, s, 0, 0))],
        out_shape=[
            jax.ShapeDtypeStruct((E, n_seq, CAP, width), bf16),
            jax.ShapeDtypeStruct((E, n_seq, CAP, width), bf16),
            jax.ShapeDtypeStruct((E, n_seq, CAP, 128), f32),
        ],
        cost_estimate=cost(4 * E * CAP * tokens * width, 20 * tokens * width),
        name="dispatch",
        after=after,
    )


def split_cores(block, c, rows):
    parts = block.reshape(-1, 2, rows, block.shape[-1])
    even, odd = parts[:, 0], parts[:, 1]
    return (
        jnp.where(c == 0, even, odd).astype(bf16),
        jnp.where(c == 0, odd, even).astype(bf16),
    )


def expert_kernel(
    e,
    up_rows,
    down_rows,
    idx_ref,
    buf_ref,
    dys_ref,
    gate_ref,
    slot_ref,
    up_a_ref,
    up_b_ref,
    down_ref,
    yg_ref,
    dbuf_ref,
    dgate_ref,
    keep_ref,
    send_ref,
    y_acc,
    d_acc,
    dyexp_ref,
    hid_ref,
    da_ref,
    db_ref,
    dg_acc,
    up_held,
    down_held,
    sems,
):
    h = pl.program_id(0)
    last = pl.num_programs(0) - 1
    c = idx_ref[0]
    n_seq = buf_ref.shape[1]
    width = buf_ref.shape[3]
    n_d = width // BLK
    up_a = up_a_ref[...].reshape(width, BLK)
    up_b = up_b_ref[...].reshape(width, BLK)
    downs = [down_ref[:, j * down_rows : (j + 1) * down_rows, :].reshape(BLK, BLK) for j in range(n_d)]
    for s in range(n_seq):
        rows = slice(s * CAP, (s + 1) * CAP)
        gate = gate_ref[0, s, :, :1]

        @pl.when(h == 0)
        def _():
            dyexp_ref[rows, :] = (gate * dys_ref[0, s].astype(f32)).astype(bf16)

        x = buf_ref[0, s]
        a = dot(x, up_a)
        b = dot(x, up_b)
        sigma = jax.nn.sigmoid(a)
        silu = a * sigma
        hid = (silu * b).astype(bf16)
        hid_ref[rows, :] = hid
        du = dot_last(dys_ref[0, s, :, :BLK], downs[0])
        for j in range(1, n_d):
            du += dot_last(dys_ref[0, s, :, j * BLK : (j + 1) * BLK], downs[j])
        dg = jnp.sum(du * hid.astype(f32), axis=-1, keepdims=True)
        dh = gate * du
        da = (dh * b * sigma * (1.0 + a * (1.0 - sigma))).astype(bf16)
        db = (dh * silu).astype(bf16)
        da_ref[rows, :] = da
        db_ref[rows, :] = db

        @pl.when(h == 0)
        def _():
            dg_acc[rows, :] = jnp.broadcast_to(dg, (CAP, 128))
            for j in range(n_d):
                y_acc[rows, j * BLK : (j + 1) * BLK] = dot(hid, downs[j])
            d_acc[rows, :] = dot_last(da, up_a) + dot_last(db, up_b)

        @pl.when(h > 0)
        def _():
            dg_acc[rows, :] += jnp.broadcast_to(dg, (CAP, 128))
            for j in range(n_d):
                y_acc[rows, j * BLK : (j + 1) * BLK] += dot(hid, downs[j])
            d_acc[rows, :] += dot_last(da, up_a) + dot_last(db, up_b)

        @pl.when(h == last)
        def _():
            yg_ref[s] = (gate * y_acc[rows, :]).astype(bf16)
            dbuf_ref[s] = d_acc[rows, :].astype(bf16)
            slots = slot_ref[s, e : e + 1, :]
            hit = lax.broadcasted_iota(jnp.int32, (CAP, slots.shape[1]), 0) == slots
            row = jnp.sum(jnp.where(hit, dg_acc[rows, :1], 0.0), axis=0, keepdims=True)
            dgate_ref[s] = jnp.broadcast_to(row, (8, slots.shape[1]))

    step = 384
    per = step // (2 * up_rows)

    for m in range(width // step):
        x = jnp.concatenate([buf_ref[0, s, :, m * step : (m + 1) * step] for s in range(n_seq)], axis=0)
        xt = x.T
        for i, d_ref in enumerate((da_ref, db_ref)):
            keep, send = split_cores(dot(xt, d_ref[...]), c, up_rows)
            up_held[h, 0, i, m * per : (m + 1) * per] = keep
            up_held[h, 1, i, m * per : (m + 1) * per] = send
    hid_t = hid_ref[...].T
    for j in range(n_d):
        keep, send = split_cores(dot(hid_t, dyexp_ref[:, j * BLK : (j + 1) * BLK]), c, down_rows)
        down_held[h, 0, :, j * down_rows : (j + 1) * down_rows, :] = keep
        down_held[h, 1, :, j * down_rows : (j + 1) * down_rows, :] = send
    n_h = FE // BLK
    n_zh = keep_ref.shape[0] // n_h

    def copies(step):
        found = []
        for side, ref in enumerate((keep_ref, send_ref)):
            for i in range(2):
                place = pl.ds((i * n_h + step) * up_rows, up_rows)
                found.append((up_held.at[step, side, i], ref.at[:, place, :]))
            place = pl.ds(2 * n_h * up_rows, n_d * down_rows)
            found.append((down_held.at[step, side], ref.at[step * n_zh : (step + 1) * n_zh, place, :]))
        return [pltpu.make_async_copy(a, b, sems.at[step, i]) for i, (a, b) in enumerate(found)]

    for step in range(n_h):

        @pl.when(h == step)
        def _():
            for copy in copies(step):
                copy.start()

    @pl.when(h == last)
    def _():
        for step in range(n_h):
            for copy in copies(step):
                copy.wait()


def expert_call(e, at, core, buf, dys, gates, slots, w, up_rows, down_rows, unit, after=()):
    _, n_seq, _, width = buf.shape
    n_f = w.shape[0]
    n_z = n_f // 2
    n_h = FE // BLK
    n_d = width // BLK
    seq = slots.shape[2]
    data = pl.BlockSpec((1, n_seq, CAP, width), lambda h, _: (e, 0, 0, 0), pipeline_mode=pl.Buffered(1))
    out = pl.BlockSpec((n_seq, CAP, width), lambda h, _: (0, 0, 0))
    anyspec = pl.BlockSpec(memory_space=pl.ANY)
    total = round_up(2 * n_h * up_rows + n_d * down_rows, unit)
    grad_shape = jax.ShapeDtypeStruct((n_z, total, BLK), bf16)
    rows = n_seq * CAP
    yg, dbuf, dgate, keep, send = kernel_call(
        functools.partial(expert_kernel, e, up_rows, down_rows),
        [core, buf, dys, gates, slots, w, w, w],
            prefetch=1,
            grid=(n_h,),
            in_specs=[
                data,
                data,
                pl.BlockSpec((1, n_seq, CAP, 128), lambda h, _: (e, 0, 0, 0)),
                pl.BlockSpec((n_seq, 8, seq), lambda h, _: (0, 0, 0)),
                pl.BlockSpec((n_f, up_rows, BLK), lambda h, _: (0, at // up_rows + h, 0)),
                pl.BlockSpec((n_f, up_rows, BLK), lambda h, _: (0, at // up_rows + n_h + h, 0)),
                pl.BlockSpec(
                    (n_f // n_h, n_d * down_rows, BLK),
                    lambda h, _: (h, (at + 2 * n_h * up_rows) // (n_d * down_rows), 0),
                ),
            ],
            out_specs=[
                out,
                out,
                pl.BlockSpec((n_seq, 8, seq), lambda h, _: (0, 0, 0)),
                anyspec,
                anyspec,
            ],
            scratch=[
                pltpu.VMEM((rows, width), f32),
                pltpu.VMEM((rows, width), f32),
                pltpu.VMEM((rows, width), bf16),
                pltpu.VMEM((rows, BLK), bf16),
                pltpu.VMEM((rows, BLK), bf16),
                pltpu.VMEM((rows, BLK), bf16),
                pltpu.VMEM((rows, 128), f32),
                pltpu.VMEM((n_h, 2, 2, n_z, up_rows, BLK), bf16),
                pltpu.VMEM((n_h, 2, n_z // n_h, n_d * down_rows, BLK), bf16),
                pltpu.SemaphoreType.DMA((n_h, 6)),
            ],
        out_shape=[
            jax.ShapeDtypeStruct((n_seq, CAP, width), bf16),
            jax.ShapeDtypeStruct((n_seq, CAP, width), bf16),
            jax.ShapeDtypeStruct((n_seq, 8, seq), f32),
            grad_shape,
            grad_shape,
        ],
        mib=60,
        cost_estimate=cost(18 * rows * width * FE, 40 * width * FE),
        name="expert",
        after=after,
    )
    return yg, dbuf, dgate, keep, send


def spread(col_ref, e):
    slots = col_ref[:, e : e + 1]
    hit = lax.broadcasted_iota(jnp.int32, (col_ref.shape[0], CAP), 1) == slots
    return jnp.where(hit, 1.0, 0.0).astype(bf16)


def combine_kernel(col_ref, resid_ref, y0_ref, y1_ref, y2_ref, out_ref):
    total = resid_ref[...]
    for e, y_ref in enumerate((y0_ref, y1_ref, y2_ref)):
        total += dot(spread(col_ref, e), y_ref[0])
    out_ref[...] = jnp.where(col_ref[:, E : E + 1] > 0, total, 0.0).astype(bf16)


def combine_call(cols, resid, ys, n_seq, after=()):
    tokens, width = resid.shape
    per = tokens // n_seq // TILE
    tile = pl.BlockSpec((TILE, width), lambda i: (i, 0))
    return kernel_call(
        combine_kernel,
        [cols, resid, *ys],
        grid=(tokens // TILE,),
        in_specs=[pl.BlockSpec((TILE, 8), lambda i: (i, 0)), tile]
        + [pl.BlockSpec((1, CAP, width), lambda i: (i // per, 0, 0))] * E,
        out_specs=tile,
        out_shape=jax.ShapeDtypeStruct((tokens, width), bf16),
        cost_estimate=cost(2 * E * CAP * tokens * width, 12 * tokens * width),
        name="combine",
        after=after,
    )


def hi_lo(x):
    high = x.astype(bf16)
    return high, (x - high.astype(f32)).astype(bf16)


def middle_kernel(
    rows,
    n,
    col_ref,
    d0_ref,
    d1_ref,
    d2_ref,
    g0_ref,
    g1_ref,
    g2_ref,
    prob_ref,
    router_ref,
    n2_ref,
    resid_ref,
    cot_ref,
    gain_ref,
    w_ref,
    dresid_ref,
    dattn_ref,
    dmix_ref,
    small_ref,
):

    @pl.when(pl.program_id(0) == 0)
    def _():
        small_ref[...] = jnp.zeros_like(small_ref)

    prob = prob_ref[...]
    expert = lax.broadcasted_iota(jnp.int32, prob.shape, 0)
    dprob = jnp.zeros_like(prob)
    for e, g_ref in enumerate((g0_ref, g1_ref, g2_ref)):
        dprob = jnp.where(expert == e, g_ref[0], dprob)
    dlogit = prob * (dprob - jnp.sum(dprob * prob, axis=0, keepdims=True))
    high, low = hi_lo(dlogit)
    dn2 = dot_first(high, router_ref[...]) + dot_first(low, router_ref[...])
    for e, d_ref in enumerate((d0_ref, d1_ref, d2_ref)):
        dn2 += dot(spread(col_ref, e), d_ref[0])
    n2 = n2_ref[...]
    small_ref[...] += dot(high, n2) + dot(low, n2)
    resid = resid_ref[...]
    scale = lax.rsqrt(jnp.mean(resid * resid, axis=-1, keepdims=True) + epsilon)
    weighted = dn2 * gain_ref[...]
    along = jnp.mean(weighted * resid, axis=-1, keepdims=True)
    dy = jnp.where(col_ref[:, E : E + 1] > 0, cot_ref[...].astype(f32), 0.0)
    dresid = dy + scale * weighted - resid * (scale * scale * scale * along)
    dresid_ref[...] = dresid
    dattn = dresid.astype(bf16)
    dattn_ref[...] = dattn
    dmix = dot_last(dattn[:, :BLK], w_ref[:, :rows, :].reshape(-1, BLK))
    for j in range(1, n):
        w = w_ref[:, j * rows : (j + 1) * rows, :].reshape(-1, BLK)
        dmix += dot_last(dattn[:, j * BLK : (j + 1) * BLK], w)
    dmix_ref[...] = dmix.astype(bf16)


def middle_call(cols, ds, dgates, prob, router, n2, resid, cot, gain, w_out, at, rows, n, n_seq, after=()):
    tokens, width = resid.shape
    per = tokens // n_seq // TILE
    tile = pl.BlockSpec((TILE, width), lambda i: (i, 0))
    row8 = pl.BlockSpec((8, TILE), lambda i: (0, i))
    return kernel_call(
        functools.partial(middle_kernel, rows, n),
        [cols, *ds, *dgates, prob, router, n2, resid, cot, gain, w_out],
        grid=(tokens // TILE,),
        in_specs=[pl.BlockSpec((TILE, 8), lambda i: (i, 0))]
        + [pl.BlockSpec((1, CAP, width), lambda i: (i // per, 0, 0))] * E
        + [pl.BlockSpec((1, 8, TILE), lambda i: (i // per, 0, i % per))] * E
        + [
            row8,
            whole((8, width)),
            tile,
            tile,
            tile,
            whole((1, width)),
            pl.BlockSpec((w_out.shape[0], n * rows, BLK), lambda i: (0, at, 0), pipeline_mode=pl.Buffered(1)),
        ],
        out_specs=[tile, tile, tile, pl.BlockSpec((8, width), lambda i: (0, 0))],
        out_shape=[
            jax.ShapeDtypeStruct((tokens, width), f32),
            jax.ShapeDtypeStruct((tokens, width), bf16),
            jax.ShapeDtypeStruct((tokens, width), bf16),
            jax.ShapeDtypeStruct((8, width), f32),
        ],
        cost_estimate=cost(2 * tokens * width * (width + E * CAP), 20 * tokens * width),
        name="middle",
        after=after,
    )


def weight_grad_kernel(rows, n_old, idx_ref, left_ref, right_ref, *refs):
    keep_ref, send_ref, turned_ref = refs[n_old:]
    c = idx_ref[0]
    width = left_ref.shape[1]
    step = 384
    per = step // (2 * rows)

    @pl.when(pl.program_id(0) == 0)
    def _():
        for m in range(width // step):
            turned_ref[m * step : (m + 1) * step, :] = left_ref[:, m * step : (m + 1) * step].T

    right = right_ref[...]
    for m in range(width // step):
        keep, send = split_cores(dot(turned_ref[m * step : (m + 1) * step, :], right), c, rows)
        keep_ref[m * per : (m + 1) * per] = keep
        send_ref[m * per : (m + 1) * per] = send


def weight_grad_call(core, left, right, rows, n_z, total, at, name, old=(), after=()):
    tokens, width = left.shape
    n = right.shape[1] // BLK
    out = pl.BlockSpec((n_z, rows, BLK), lambda j, _: (0, at + j, 0))
    shape = jax.ShapeDtypeStruct((n_z, total, BLK), bf16)
    return kernel_call(
        functools.partial(weight_grad_kernel, rows, len(old)),
        [core, left, right, *old],
        prefetch=1,
        grid=(n,),
        in_specs=[
            pl.BlockSpec((tokens, width), lambda j, _: (0, 0), pipeline_mode=pl.Buffered(1)),
            pl.BlockSpec((tokens, BLK), lambda j, _: (0, j)),
        ]
        + [pl.BlockSpec(memory_space=pl.ANY)] * len(old),
        out_specs=[out, out],
        scratch=[pltpu.VMEM((width, tokens), bf16)],
        out_shape=[shape, shape],
        cost_estimate=cost(2 * tokens * width * n * BLK, 2 * width * n * BLK + 4 * tokens * width),
        aliases={3 + i: i for i in range(len(old))},
        name=name,
        after=after,
    )


def input_grad_kernel(rows, n, d_ref, w_ref, x_ref, dresid_ref, gain_ref, out_ref):
    dn1 = dot_last(d_ref[:, :BLK], w_ref[:, :rows, :].reshape(-1, BLK))
    for j in range(1, n):
        w = w_ref[:, j * rows : (j + 1) * rows, :].reshape(-1, BLK)
        dn1 += dot_last(d_ref[:, j * BLK : (j + 1) * BLK], w)
    x = x_ref[...].astype(f32)
    scale = lax.rsqrt(jnp.mean(x * x, axis=-1, keepdims=True) + epsilon)
    weighted = dn1 * gain_ref[...]
    along = jnp.mean(weighted * x, axis=-1, keepdims=True)
    out = dresid_ref[...] + scale * weighted - x * (scale * scale * scale * along)
    out_ref[...] = out.astype(bf16)


def input_grad_call(dqkv, w_in, x, dresid, gain, rows, n, after=()):
    tokens, width = x.shape
    tile = pl.BlockSpec((TILE, width), lambda i: (i, 0))
    return kernel_call(
        functools.partial(input_grad_kernel, rows, n),
        [dqkv, w_in, x, dresid, gain],
        grid=(tokens // TILE,),
        in_specs=[
            pl.BlockSpec((TILE, n * BLK), lambda i: (i, 0)),
            whole((w_in.shape[0], n * rows, BLK)),
            tile,
            tile,
            whole((1, width)),
        ],
        out_specs=tile,
        out_shape=jax.ShapeDtypeStruct((tokens, width), bf16),
        cost_estimate=cost(2 * tokens * width * n * BLK, 2 * width * n * BLK + 12 * tokens * width),
        name="input_grad",
        after=after,
    )


def adam_step(master, first, second, gradient, clip, decayed):
    clipped = gradient * clip
    first_new = beta_first * first + (1.0 - beta_first) * clipped
    second_new = beta_second * second + (1.0 - beta_second) * clipped * clipped
    first_hat = first_new * (1.0 / (1.0 - beta_first**STEP))
    second_hat = second_new * (1.0 / (1.0 - beta_second**STEP))
    change = first_hat / (jnp.sqrt(second_hat) + adam_floor) + decayed * weight_decay * master
    update = -learn_rate * change
    return (gradient, update, first_new, second_new)


def adam_kernel(scale, which, clip_ref, g_ref, master_ref, first_ref, second_ref, *outs):
    gradient = g_ref[...].astype(f32) * scale
    results = adam_step(master_ref[...], first_ref[...], second_ref[...], gradient, clip_ref[0, which], 1.0)
    for out, result in zip(outs, results):
        out[...] = result


def adam_call(clip, which, packed, at, master, first, second, scale, name, after=()):
    rows, cols = master.shape
    natural = pl.BlockSpec((rows, BLK), lambda j, _: (0, j))
    shape = jax.ShapeDtypeStruct(master.shape, f32)
    return kernel_call(
        functools.partial(adam_kernel, scale, which),
        [clip, packed, master, first, second],
            prefetch=1,
            grid=(cols // BLK,),
            in_specs=[pl.BlockSpec((rows, BLK), lambda j, _: (at // rows + j, 0)), natural, natural, natural],
            out_specs=[natural] * 4,
        out_shape=[shape] * 4,
        cost_estimate=cost(20 * master.size, 30 * master.size),
        name=name,
        after=after,
    )


def adam_experts_kernel(scale, which, clip_ref, g0_ref, g1_ref, g2_ref, master_ref, first_ref, second_ref, *outs):
    for e, g_ref in enumerate((g0_ref, g1_ref, g2_ref)):

        @pl.when(pl.program_id(0) == e)
        def _():
            gradient = g_ref[...].astype(f32) * scale
            results = adam_step(master_ref[0], first_ref[0], second_ref[0], gradient, clip_ref[0, which], 1.0)
            for out, result in zip(outs, results):
                out[0] = result


def adam_experts_call(clip, which, packed, at, master, first, second, scale, name, after=()):
    _, rows, cols = master.shape
    n = cols // BLK
    natural = pl.BlockSpec((1, rows, BLK), lambda e, j, _: (e, 0, j))
    shape = jax.ShapeDtypeStruct(master.shape, f32)

    def g_spec(own):
        return pl.BlockSpec(
            (rows, BLK), lambda e, j, _: (at // rows + jnp.where(e < own, 0, jnp.where(e > own, n - 1, j)), 0)
        )

    return kernel_call(
        functools.partial(adam_experts_kernel, scale, which),
        [clip, *packed, master, first, second],
            prefetch=1,
            grid=(E, n),
            in_specs=[g_spec(e) for e in range(E)] + [natural] * 3,
            out_specs=[natural] * 4,
        out_shape=[shape] * 4,
        cost_estimate=cost(20 * master.size, 30 * master.size),
        name=name,
        after=after,
    )


def per_device(
    tokens,
    cotangent,
    lengths,
    routes,
    slot_index,
    norm_gains,
    norm_first,
    norm_second,
    in_proj,
    in_first,
    in_second,
    out_proj,
    out_first,
    out_second,
    router,
    router_first,
    router_second,
    up_proj,
    up_first,
    up_second,
    down_proj,
    down_first,
    down_second,
):
    n_rep, n_f = lax.axis_size("replica"), lax.axis_size("fsdp")
    n_z = n_f // 2
    n_mb, n_local, seq, width = tokens.shape
    n_seq = n_mb * n_local
    total_tokens = n_seq * seq
    unit = 16 * n_rep
    rows = in_proj.shape[0]
    down_rows = down_proj.shape[1]
    n_in, n_out, n_up, n_down = (w.shape[-1] // BLK for w in (in_proj, out_proj, up_proj, down_proj))
    core = (lax.axis_index("fsdp") % 2).astype(jnp.int32)[None]

    smalls = jnp.concatenate([norm_gains.astype(bf16), router.astype(bf16).T], axis=0)
    n_small = round_up(smalls.size, BLK) // BLK
    smalls = jnp.pad(smalls.reshape(-1), (0, 16 * BLK - smalls.size)).reshape(16, BLK)
    e_rows = n_up * rows + n_down * down_rows
    in_shard, in_mine = pack_call([(in_proj, None)], unit, smalls)
    mid_shard, _ = pack_call([(up_proj, 0), (down_proj, 0), (out_proj, None)], unit, after=[in_shard])
    late_shard, late_mine, mid_mine = pack_call(
        [(w, e) for e in range(1, E) for w in (up_proj, down_proj)], unit, before=mid_shard
    )
    g_in, g_mid, g_late = Gather(in_shard), Gather(mid_shard), Gather(late_shard)
    g_in.start(in_mine, True)
    g_in.own_c = swap_core(in_shard)
    g_in.stack(after=[late_shard, g_in.own_c])
    g_mid.start(hold(mid_mine, g_in.stacks), False)
    g_in.double(after=[late_shard])
    g_in.low_c = [swap_core(x) for x in hold(g_in.stacks, g_in.received)]
    g_mid.stack(after=g_in.received)
    w_in = g_in.assemble(after=g_mid.stacks)
    g_late.start(hold(late_mine, g_mid.pieces), False)

    small_all = w_in[:, n_in * rows : n_in * rows + n_small, :].reshape(n_f, n_small * BLK)[:, : 5 * rows]
    small_all = small_all.reshape(n_f, 5, rows).transpose(1, 0, 2).reshape(5, width)
    gain_one = small_all[0:1].astype(f32)
    gain_two = small_all[1:2].astype(f32)
    router8 = pad_rows(small_all[2:5], 8)

    length = lengths.reshape(n_seq).astype(jnp.int32)
    route = routes.reshape(n_seq, seq, 2)
    slot = slot_index.reshape(n_seq, seq, 2)
    live = jnp.arange(seq)[None, :] < length[:, None]
    kept = live[:, :, None] & (slot < CAP)
    slot_of = [
        jnp.max(jnp.where(kept & (route == e), slot, -1), axis=-1) for e in range(E)
    ]
    slot_rows = jnp.stack(slot_of + [live.astype(jnp.int32)] + [jnp.full_like(slot_of[0], -1)] * 4, axis=1)
    slot_cols = slot_rows.transpose(0, 2, 1).reshape(total_tokens, 8)

    x = tokens.reshape(total_tokens, width)
    cot = cotangent.reshape(total_tokens, width)

    qkv, n1 = qkv_call(x, gain_one, w_in, rows, n_in)
    g_mid.double(after=[qkv])
    g_mid.swap_early()
    probs, mixed = attention_call(length, qkv, n_seq, after=g_mid.stacks)
    g_mid.settle([mixed])
    g_late.stack(after=[mixed, *g_mid.received])
    w_mid = g_mid.assemble(after=g_late.stacks)
    w_at = e_rows // (n_out * rows)
    resid, n2, prob = resid_call(mixed, w_mid, w_at, x, gain_two, router8, rows, n_out)
    g_late.double(after=[resid])
    g_late.swap_early()
    buf, dys, gates = dispatch_call(slot_rows, prob, n2, cot, n_seq, after=g_late.stacks)

    def expert(e, w, at, after):
        return expert_call(e, at, core, buf, dys, gates, slot_rows, w, rows, down_rows, unit, after)

    y0, dbuf0, dgate0, keep0, send0 = expert(0, w_mid, 0, ())
    g_late.settle([y0])
    w_late = g_late.assemble(after=[y0])
    got0 = swap_core(hold(send0, g_late.high_c))
    total0 = pair_sum(keep0, hold(got0, [w_late]))
    part0 = lax.psum_scatter(total0, "fsdp", axis_index_groups=core_groups())
    y1, dbuf1, dgate1, keep1, send1 = expert(1, w_late, 0, [total0])
    got1 = swap_core(send1)
    y2, dbuf2, dgate2, keep2, send2 = expert(2, w_late, e_rows, [y1])
    sum1 = Reduce(keep1, got1, 0)
    sent = sum1.step([y2])
    got2 = swap_core(hold(send2, sent))

    dresid, dattn, dmixed, router_part = middle_call(
        slot_cols,
        (dbuf0, dbuf1, dbuf2),
        (dgate0, dgate1, dgate2),
        prob,
        router8,
        n2,
        resid,
        cot,
        gain_two,
        w_mid,
        w_at,
        rows,
        n_out,
        n_seq,
        after=sent,
    )
    io_rows = round_up((n_in + n_out) * rows + 16, unit)
    keep, send = weight_grad_call(core, mixed, dattn, rows, n_z, io_rows, n_in, "out_grad")
    router_part = router_part[:E].astype(bf16).reshape(E, n_z, 2, rows).transpose(2, 1, 0, 3)
    router_part = jnp.pad(router_part, ((0, 0), (0, 0), (0, 16 - E), (0, BLK - rows)))
    at = (0, (n_in + n_out) * rows, 0)
    keep = lax.dynamic_update_slice(keep, lax.dynamic_index_in_dim(router_part, core[0], keepdims=False), at)
    send = lax.dynamic_update_slice(send, lax.dynamic_index_in_dim(router_part, 1 - core[0], keepdims=False), at)
    sum2 = Reduce(keep2, got2, 1)
    sent = sum1.step([send]) + sum2.step([send])
    dq, dk, dv = attention_back_call(qkv, probs, mixed, dmixed, n_seq, sent + [part0])
    sent = sum1.step([dq]) + sum2.step([dq])
    dqkv = jnp.concatenate([dq, dk, dv], axis=1)
    keep, send = weight_grad_call(core, n1, dqkv, rows, n_z, io_rows, 0, "in_grad", (keep, send), sent)
    sum2.newest = hold(sum2.newest, [send])
    got = swap_core(hold(send, sum2.newest))
    sum0 = lax.psum(part0, "replica")
    block_out = combine_call(slot_cols, resid, (y0, y1, y2), n_seq, [send])
    io_sum = Reduce(keep, hold(got, [block_out]), 0)
    sent = io_sum.step()
    input_grad = input_grad_call(dqkv, w_in, x, dresid, gain_one, rows, n_in, sent)
    io_sum.newest = hold(io_sum.newest, [input_grad])
    sent = io_sum.step()
    sum1.newest = hold(sum1.newest, sent)
    sent = sum2.step(sum1.newest)
    io_sum.newest = hold(io_sum.newest, sent)
    sent = sum1.step(io_sum.newest)
    sum2.newest = hold(sum2.newest, sent)
    sent = io_sum.step(sum2.newest)
    sent = sum2.step(sent)
    sent = sum1.step(sent)
    sent = sum2.step(sent)
    sums = [hold(sum0, sent), sum1.result(sent), sum2.result(sent)]

    grad_scale = 1.0 / (n_seq * n_rep * n_f)
    weights = (norm_gains, in_proj, out_proj, router, up_proj, down_proj)
    counts = (2 * width,) + tuple(w.size * n_f for w in weights[1:])

    def square(packed):
        values = packed.astype(f32) * grad_scale
        return jnp.sum(values * values)

    def along_rows(shard, packed, n):
        both = shard[: n * rows].astype(f32) * packed[: n * rows].astype(f32)
        return jnp.sum(both.reshape(n, rows, BLK), axis=(0, 2)) * grad_scale

    def lanes(values):
        lane = lax.broadcasted_iota(jnp.int32, (8, 128), 1)
        return sum(jnp.where(lane == i, value, 0.0) for i, value in enumerate(values))

    def rms_and_clip(squares, which):
        rms = jnp.sqrt(squares * lanes([1.0 / counts[w] for w in which]) + epsilon)
        return rms, jnp.minimum(1.0, clip_level / rms)

    at_down = n_up * rows
    up_square = sum(square(s[:at_down]) for s in sums) / n_rep
    down_square = sum(square(s[at_down:e_rows]) for s in sums) / n_rep
    gains_low = norm_gains.astype(bf16).astype(f32)
    shards = (mid_shard, late_shard, late_shard[e_rows:])
    gain_two_grad = sum(along_rows(shard, packed, n_up) for shard, packed in zip(shards, sums))

    here = io_sum.sum_here([up_square, down_square, gain_two_grad])
    row = lax.axis_index("replica") * here.shape[0] + lax.broadcasted_iota(jnp.int32, (here.shape[0], 1), 0)
    lane = lax.broadcasted_iota(jnp.int32, (1, BLK), 1)
    ends = (n_in * rows, (n_in + n_out) * rows)
    values = here.astype(f32) * grad_scale
    values = values * values
    spread_squares = [
        jnp.sum(jnp.where(row < ends[0], values, 0.0)),
        jnp.sum(jnp.where((row >= ends[0]) & (row < ends[1]), values, 0.0)),
        jnp.sum(jnp.where((row >= ends[1]) & (row < ends[1] + E) & (lane < rows), values, 0.0)),
    ]
    squares = lanes(spread_squares + [up_square, down_square])
    for bit in bit_order(0):
        squares = squares + swap_replica(squares, bit)
    io_sum.have = hold(io_sum.have, [squares])
    sent = io_sum.step()
    all_rms, all_clip = rms_and_clip(sum_small(hold(squares, sent)), (1, 2, 3, 4, 5))
    sent = io_sum.step([all_clip])
    down_res = adam_experts_call(
        hold(all_clip, sent), 4, sums, at_down, down_proj, down_first, down_second, grad_scale, "down_adam"
    )
    up_res = adam_experts_call(
        hold(all_clip, [down_res[1]]), 3, sums, 0, up_proj, up_first, up_second, grad_scale, "up_adam"
    )
    total = io_sum.result([up_res[1]])
    in_sum = total[: ends[0]]
    router_grad = total[ends[1] : ends[1] + E, :rows].astype(f32) * grad_scale
    gain_one_grad = along_rows(in_shard, in_sum, n_in) / gains_low[0]
    gain_two_grad = gain_two_grad + jnp.sum(router.astype(bf16).astype(f32).T * router_grad, axis=0)
    gain_two_grad = gain_two_grad / gains_low[1]
    gain_grad = jnp.stack([gain_one_grad, gain_two_grad])
    squares = lanes([jnp.sum(gain_grad * gain_grad)])
    out_res = adam_call(
        hold(all_clip, [squares]), 1, total, ends[0], out_proj, out_first, out_second, grad_scale, "out_adam"
    )
    squares = squares + hold(swap_core(squares), [out_res[1]])
    in_res = adam_call(
        hold(all_clip, [squares]), 0, total, 0, in_proj, in_first, in_second, grad_scale, "in_adam"
    )
    gain_rms, gain_clip = rms_and_clip(sum_small(squares, 2, [in_res[1]]), (0,))
    norm_res = adam_step(norm_gains, norm_first, norm_second, gain_grad, gain_clip[0, 0], 0.0)
    router_res = adam_step(router, router_first, router_second, router_grad.T, all_clip[0, 2], 1.0)
    rms = jnp.concatenate([gain_rms[0, :1], all_rms[0, :5]])
    return (
        block_out.reshape(tokens.shape),
        input_grad.reshape(tokens.shape),
        rms[:5],
        rms[5:],
        *norm_res,
        *in_res,
        *out_res,
        *router_res,
        *up_res,
        *down_res,
    )


def solution(mesh):
    data = P(None, ("replica", "fsdp"), None, None)
    gains = P(None, "fsdp")
    flat = P("fsdp", None)
    experts = P(None, "fsdp", None)
    return jax.shard_map(
        per_device,
        mesh=mesh,
        in_specs=(data, data, P(None, ("replica", "fsdp")), data, data)
        + (gains,) * 3
        + (flat,) * 9
        + (experts,) * 6,
        out_specs=(data, data, P(), P()) + (gains,) * 4 + (flat,) * 12 + (experts,) * 8,
        check_vma=False,
    )
```
